32 devices in a mesh: cells: 4 (over y, x), genes: 8 (over z, core).
Axes of the slice: x: 2, y: 2, z: 4, core: 2. Of those that a mesh axis runs over, the one named last changes fastest.
Arguments:
- inputs: float32 [16, 2048, 200], P('cells', 'genes'), may hold values from -6 to 6
- lengths: int32 [16], P('cells'), may hold values from 1 to 2048, as said below
- tissue_ids: int32 [16], P('cells'), may hold values from 0 to 15
- tissue_table: float32 [16, 200], replicated, may hold values from -3 to 3
- first_gain: float32 [200], replicated, may hold values from 0.1 to 1.9
- first_bias: float32 [200], replicated, may hold values from -1.75 to 1.75
- joint_weight: float32 [200, 1920], replicated, may hold values from -0.21875 to 0.21875
- feature_draws: float32 [10, 266, 64], replicated, may hold values from -6 to 6
- output_weight: float32 [640, 200], replicated, may hold values from -6 to 6
- output_bias: float32 [200], replicated, may hold values from -1.75 to 1.75
- second_gain: float32 [200], replicated, may hold values from 0.1 to 1.9
- second_bias: float32 [200], replicated, may hold values from -1.75 to 1.75
- hidden_weight: float32 [200, 800], replicated, may hold values from -0.4375 to 0.4375
- hidden_bias: float32 [800], replicated, may hold values from -1.75 to 1.75
- return_weight: float32 [800, 200], replicated, may hold values from -0.21875 to 0.21875
- return_bias: float32 [200], replicated, may hold values from -3 to 3
- cotangent: bfloat16 [16, 2048, 200], P('cells', 'genes'), may hold values from -6 to 6
Outputs:
- outputs: float32 [16, 2048, 200], P('cells', 'genes')
- input_grad: float32 [16, 2048, 200], P('cells', 'genes')
- tissue_grad: float32 [16, 200], replicated
- first_gain_grad: float32 [200], replicated
- first_bias_grad: float32 [200], replicated
- joint_grad: float32 [200, 1920], replicated
- output_weight_grad: float32 [640, 200], replicated
- output_bias_grad: float32 [200], replicated
- second_gain_grad: float32 [200], replicated
- second_bias_grad: float32 [200], replicated
- hidden_weight_grad: float32 [200, 800], replicated
- hidden_bias_grad: float32 [800], replicated
- return_weight_grad: float32 [800, 200], replicated
- return_bias_grad: float32 [200], replicated
The draws below stay inside these ranges and needn't reach their ends.
Inputs may be any that keep to these rules, and one draw needn't show every extreme that they name: `lengths`: among the 4 cells held by each index of cells, one has all 2048 genes present.
All inputs are finite; a program needn't handle non-finite values.
Results may differ from the reference program's by a relative error of at most 0.012.
The reference program's roundings to bfloat16 on the way count: a program that leaves them out, or rounds other values in their place, can miss the bound.
Values sent between devices are 32-bit elements; how exact they have to be, the bound alone decides.
No kernel may reach another device: no remote copies, remote signals or barrier semaphores. Data moves between devices by JAX's collectives and lax.ppermute only.
A program may use at most 128 MiB of HBM per device.

```python
import math
import jax
import jax.numpy as jnp
import numpy as np
from jax import lax

D = 200
HEADS = 10
HEAD = 64
FEAT = 266
FF = 800
TISSUES = 16
CELLS_DEV = 4
GENE_DEV = 256
CELLS = 16
LENGTH = 2048
N_GENES = 8


def draw_lengths(key, part):
    key = jax.random.fold_in(key, 7)
    first_key, second_key = jax.random.split(key)
    sampled = jax.random.randint(first_key, (CELLS,), 1, LENGTH + 1, dtype=jnp.int32)
    chosen = jax.random.randint(second_key, (CELLS // CELLS_DEV,), 0, CELLS_DEV, dtype=jnp.int32)
    positions = jnp.arange(CELLS, dtype=jnp.int32)
    full_cell = positions % CELLS_DEV == jnp.repeat(chosen, CELLS_DEV)
    return jnp.where(full_cell, LENGTH, sampled).astype(jnp.int32)


def plant(array, stream_key, low, high):
    place = [jax.random.randint(jax.random.fold_in(stream_key, axis), (), 0, length) for axis, length in enumerate(array.shape)]
    longest = array.shape.index(max(array.shape))
    neighbour = place[:longest] + [(place[longest] + 1) % array.shape[longest]] + place[longest + 1:]
    return array.at[tuple(place)].set(low).at[tuple(neighbour)].set(high)


def levels(key, extent, cuts, smallest, largest):
    level = 1.0
    for position, shards_of in cuts:
        steps = jax.random.uniform(jax.random.fold_in(jax.random.fold_in(key, 6), position), (shards_of,), jnp.float32, smallest / len(cuts), largest / len(cuts))
        level = level * jnp.repeat(jnp.exp(steps), extent[position] // shards_of).reshape((-1,) + (1,) * (len(extent) - 1 - position))
    return level


def rank_bounds(number_of, skew):
    loads = [(1 << 20) // math.isqrt(grade ** skew) + 1 for grade in range(1, number_of + 1)]
    spread = 1 + sum(loads) // (1 << 30)
    return np.cumsum(np.array([max(1, weight // spread) for weight in loads]))


def ranked_ids(own_key, shape, amount, slope):
    listing = rank_bounds(amount, slope)
    ticket = jax.random.randint(jax.random.fold_in(own_key, 1), shape, 0, int(listing[amount - 1]))
    standing = jnp.searchsorted(jnp.asarray(listing, jnp.int32), ticket, side="right")
    return jax.random.permutation(jax.random.fold_in(own_key, 2), amount)[standing].astype(jnp.int32)


def normal_values(key, dims, scale, reach, cuts=(), kind=jnp.bfloat16):
    entries = scale * jax.random.normal(key, dims, jnp.float32)
    if cuts:
        entries = entries * levels(key, dims, cuts, -0.22, 0.18)
    return jnp.clip(entries, -reach, reach).astype(kind)


def setup_inputs(seed: int = 0) -> dict:
    arg_keys = jax.random.split(jax.random.key(seed), 18)
    return {
        "inputs": normal_values(arg_keys[0], (CELLS, LENGTH, D), 1.0, 6.0, ((0, 4), (1, 8)), jnp.float32),
        "lengths": draw_lengths(jax.random.fold_in(arg_keys[17], 71), 0),
        "tissue_ids": plant(ranked_ids(arg_keys[2], (CELLS,), TISSUES, 2), jax.random.fold_in(arg_keys[2], 3), 0, TISSUES - 1).astype(jnp.int32),
        "tissue_table": normal_values(arg_keys[3], (TISSUES, D), 0.5, 3.0, (), jnp.float32),
        "first_gain": jnp.clip(1.0 + 0.18 * jax.random.normal(arg_keys[4], (D,), jnp.float32), 0.1, 1.9),
        "first_bias": normal_values(arg_keys[5], (D,), 0.3, 1.75, (), jnp.float32),
        "joint_weight": normal_values(arg_keys[6], (D, 3 * HEADS * HEAD), (4 * D) ** -0.5, 0.21875, (), jnp.float32),
        "feature_draws": normal_values(arg_keys[7], (HEADS, FEAT, HEAD), 1.0, 6.0, (), jnp.float32),
        "output_weight": normal_values(arg_keys[8], (HEADS * HEAD, D), (0.6 * (GENE_DEV * N_GENES) ** 0.5 * (HEADS * HEAD) ** -0.5), 6.0, (), jnp.float32),
        "output_bias": normal_values(arg_keys[9], (D,), 0.3, 1.75, (), jnp.float32),
        "second_gain": jnp.clip(1.0 + 0.18 * jax.random.normal(arg_keys[10], (D,), jnp.float32), 0.1, 1.9),
        "second_bias": normal_values(arg_keys[11], (D,), 0.3, 1.75, (), jnp.float32),
        "hidden_weight": normal_values(arg_keys[12], (D, FF), D ** -0.5, 0.4375, (), jnp.float32),
        "hidden_bias": normal_values(arg_keys[13], (FF,), 0.3, 1.75, (), jnp.float32),
        "return_weight": normal_values(arg_keys[14], (FF, D), FF ** -0.5, 0.21875, (), jnp.float32),
        "return_bias": normal_values(arg_keys[15], (D,), 0.5, 3.0, (), jnp.float32),
        "cotangent": normal_values(arg_keys[16], (CELLS, LENGTH, D), 1.0, 6.0, ((0, 4), (1, 8))),
    }


@jax.custom_vjp
def low(v):
    return lax.optimization_barrier(v.astype(jnp.bfloat16)).astype(jnp.float32)

@jax.custom_vjp
def low_back(v):
    return v

def low_keep(v):
    return (low(v), None)

def low_pass(kept, grad):
    return (grad,)

def back_keep(v):
    return (v, None)

def back_low(kept, grad):
    return (low(grad),)
low.defvjp(low_keep, low_pass)
low_back.defvjp(back_keep, back_low)

def layer_norm(values, gain, shift):
    centered = values - lax.optimization_barrier(jnp.mean(values, -1, keepdims=True))
    inverse = lax.rsqrt(lax.optimization_barrier(jnp.mean(centered * centered, -1, keepdims=True)) + 1e-05)
    return centered * inverse * gain + shift

def reference(inputs, lengths, tissue_ids, tissue_table, first_gain, first_bias, joint_weight, feature_draws, output_weight, output_bias, second_gain, second_bias, hidden_weight, hidden_bias, return_weight, return_bias, cotangent):
    highest = lax.Precision.HIGHEST
    head_count, feature_count, head_size = feature_draws.shape
    inner_width = head_count * head_size
    length_all = inputs.shape[1]
    scaling = head_size ** (-0.25)
    draws_low = low(feature_draws)

    def one_cell(params, cell_input, length, tissue):
        tissue_rows, gain_first, shift_first, joint_matrix, output_matrix, output_shift, gain_second, shift_second, hidden_matrix, hidden_shift, return_matrix, return_shift = params
        shifted = cell_input + tissue_rows[tissue]
        normed = low(layer_norm(shifted, gain_first, shift_first))
        joint_out = jnp.dot(normed, low(joint_matrix), precision=highest)

        def head_split(columns):
            return low_back(low(columns)).reshape(length_all, head_count, head_size)
        query_vec = head_split(joint_out[:, :inner_width])
        key_vec = head_split(joint_out[:, inner_width:2 * inner_width])
        value_vec = head_split(joint_out[:, 2 * inner_width:])
        query_dash = low_back(scaling * jnp.einsum('the,hme->thm', query_vec, draws_low, precision=highest))
        query_feats = jnp.exp(query_dash - scaling * scaling * lax.optimization_barrier(jnp.sum(query_vec * query_vec, -1, keepdims=True)) * 0.5)
        valid_rows = (jnp.arange(length_all, dtype=jnp.int32) < length)[:, None, None]
        key_dash = low_back(scaling * jnp.einsum('the,hme->thm', key_vec, draws_low, precision=highest))
        key_peak = lax.optimization_barrier(jnp.max(jnp.where(valid_rows, key_dash, -1e+30), axis=(0, 2)))
        key_exps = key_dash - scaling * scaling * lax.optimization_barrier(jnp.sum(key_vec * key_vec, -1, keepdims=True)) * 0.5 - key_peak[None, :, None]
        key_feats = low(jnp.exp(jnp.where(valid_rows, key_exps, -10000.0)))
        key_values = jnp.einsum('thm,the->hme', key_feats, value_vec, precision=highest)
        key_sums = lax.optimization_barrier(jnp.sum(key_feats, 0))
        numerator = jnp.einsum('thm,hme->the', query_feats, key_values, precision=highest)
        denominator = jnp.einsum('thm,hm->th', query_feats, key_sums, precision=highest)
        attended = low((numerator / denominator[:, :, None]).reshape(length_all, inner_width))
        middle = shifted + low_back(jnp.dot(attended, low(output_matrix), precision=highest) + output_shift)
        second = low(layer_norm(middle, gain_second, shift_second))
        hidden_pre = low_back(jnp.dot(second, low(hidden_matrix), precision=highest) + hidden_shift)
        hidden_act = low(jax.nn.gelu(hidden_pre, approximate=False))
        return middle + jnp.dot(hidden_act, low(return_matrix), precision=highest) + return_shift

    def forward(params, cell_inputs):
        checked = jax.checkpoint(one_cell)

        def scan_step(carried, cell_items):
            return (carried, checked(params, cell_items[0], cell_items[1], cell_items[2]))
        carried, result = lax.scan(scan_step, jnp.float32(0), (cell_inputs, lengths, tissue_ids))
        return result
    params = (tissue_table, first_gain, first_bias, joint_weight, output_weight, output_bias, second_gain, second_bias, hidden_weight, hidden_bias, return_weight, return_bias)
    outputs, pullback = jax.vjp(forward, params, inputs)
    param_grads, input_grad = pullback(cotangent.astype(jnp.float32))
    return (outputs, input_grad, param_grads[0], param_grads[1], param_grads[2], param_grads[3], param_grads[4], param_grads[5], param_grads[6], param_grads[7], param_grads[8], param_grads[9], param_grads[10], param_grads[11])
```

```python
import jax
import jax.numpy as jnp
from jax import lax
from jax.sharding import Mesh
from jax.sharding import PartitionSpec as P

EPSILON = 1e-05


def layer_norm(values, gain, shift):
    centered = values - jnp.mean(values, -1, keepdims=True)
    inverse = lax.rsqrt(jnp.mean(centered * centered, -1, keepdims=True) + EPSILON)
    normed = centered * inverse
    return (normed * gain + shift, normed, inverse)


def norm_back(upstream, normed, inverse, gain):
    scaled = upstream * gain
    result = inverse * (
        scaled
        - jnp.mean(scaled, -1, keepdims=True)
        - normed * jnp.mean(scaled * normed, -1, keepdims=True)
    )
    return (result, jnp.sum(upstream * normed, axis=0), jnp.sum(upstream, axis=0))


def matmul(left, right):
    return jnp.dot(left, right, preferred_element_type=jnp.float32)


def contract_rows(left, right):
    return lax.dot_general(
        left, right, (((0,), (0,)), ((), ())), preferred_element_type=jnp.float32
    )


def contract_cols(left, right):
    return lax.dot_general(
        left, right, (((1,), (1,)), ((), ())), preferred_element_type=jnp.float32
    )


def gelu_slope(values):
    cumulative = 0.5 * (1.0 + lax.erf(values * 0.7071067811865476))
    density = jnp.exp(-0.5 * values * values) * 0.3989422804014327
    return cumulative + values * density


def partners(size, step):
    return [(i, i ^ step) for i in range(size)]


def swap_blocks(blocks, size):
    out = [blocks[0]]
    for k in range(1, size):
        out.append(lax.ppermute(blocks[k], "home", partners(size, k)))
    return out


def pair_sum(value, size):
    if size == 1:
        return value
    if size == 2:
        return value + lax.ppermute(value, "rest", partners(2, 1))
    return lax.optimization_barrier(lax.psum(value, "rest"))


def scatter_sum(value, axis, size):
    rows = value.shape[0] // size
    me = lax.axis_index(axis)

    def part(k):
        return lax.dynamic_slice_in_dim(value, (me ^ k) * rows, rows, 0)

    total = part(0)
    received = [lax.ppermute(part(k), axis, partners(size, k)) for k in range(1, size)]
    for r in received:
        total = total + r
    return total


def gather_parts(value, axis, size):
    rows = value.shape[0]
    me = lax.axis_index(axis)
    out = jnp.zeros((rows * size, value.shape[1]), value.dtype)
    received = [value] + [lax.ppermute(value, axis, partners(size, k)) for k in range(1, size)]
    for k, r in enumerate(received):
        out = lax.dynamic_update_slice_in_dim(out, r, (me ^ k) * rows, 0)
    return out


def sum_everywhere(value, sizes):
    axes = ("rest", "cells", "home")
    if any(sizes[a] & (sizes[a] - 1) or sizes[a] > 4 for a in axes):
        return lax.psum(value, axes)
    for a in axes:
        if sizes[a] > 1:
            value = scatter_sum(value, a, sizes[a])
    for a in reversed(axes):
        if sizes[a] > 1:
            value = gather_parts(value, a, sizes[a])
    return value


def solution(mesh):
    def whole(inputs, lengths, *others):
        cells_axis, genes_axis = mesh.shape["cells"], mesh.shape["genes"]
        homes = inputs.shape[0] // cells_axis
        rest = genes_axis // homes
        sizes = {"cells": cells_axis, "home": homes, "rest": rest}
        fine = Mesh(
            mesh.devices.reshape(cells_axis, homes, rest), ("cells", "home", "rest")
        )
        tokens = P("cells", ("home", "rest"), None)
        run = jax.shard_map(
            lambda *args: local(sizes, *args),
            mesh=fine,
            in_specs=(tokens, P("cells"), P("cells")) + (P(),) * 13 + (tokens,),
            out_specs=(tokens, tokens) + (P(),) * 12,
            check_vma=False,
        )
        return run(inputs, lengths, *others)

    return whole


def local(
    sizes,
    inputs,
    lengths,
    tissue_ids,
    tissue_table,
    first_gain,
    first_bias,
    joint_weight,
    feature_draws,
    output_weight,
    output_bias,
    second_gain,
    second_bias,
    hidden_weight,
    hidden_bias,
    return_weight,
    return_bias,
    cotangent,
):
    homes, rest = sizes["home"], sizes["rest"]
    _, gene_count, model_width = inputs.shape
    head_count, feature_count, head_size = feature_draws.shape
    inner_width = head_count * head_size
    scaling = head_size ** (-0.25)
    bf16 = jnp.bfloat16
    f32 = jnp.float32
    home = lax.axis_index("home")
    side = lax.axis_index("rest")

    def pick(array, k):
        return lax.dynamic_index_in_dim(array, home ^ k, 0, False)

    arrived = swap_blocks([pick(inputs, k) for k in range(homes)], homes)
    arrived_cot = swap_blocks([pick(cotangent, k).astype(f32) for k in range(homes)], homes)
    token_count = homes * gene_count
    steps = jnp.arange(gene_count, dtype=jnp.int32)
    positions = jnp.concatenate(
        [((home ^ k) * rest + side) * gene_count + steps for k in range(homes)]
    )
    key_mask = positions < pick(lengths, 0)
    tissue = pick(tissue_ids, 0)
    shifted = jnp.concatenate(arrived) + lax.dynamic_index_in_dim(tissue_table, tissue, 0, True)
    upstream = jnp.concatenate(arrived_cot)

    first_out, first_normed, first_inverse = layer_norm(shifted, first_gain, first_bias)
    first_low = first_out.astype(bf16)
    joint_low = joint_weight.astype(bf16)
    projected = matmul(first_low, joint_low).astype(bf16)

    def heads(columns):
        return columns.reshape(token_count, head_count, head_size).transpose(1, 0, 2)

    query_vec = heads(projected[:, :inner_width])
    key_vec = heads(projected[:, inner_width : 2 * inner_width])
    value_vec = heads(projected[:, 2 * inner_width :])
    draws_low = feature_draws.astype(bf16)

    def ein(rule, a, b):
        return jnp.einsum(rule, a.astype(bf16), b.astype(bf16), preferred_element_type=f32)

    query_float = query_vec.astype(f32)
    query_feats = jnp.exp(
        scaling * ein("hge,hme->hgm", query_vec, draws_low)
        - scaling * scaling * jnp.sum(query_float * query_float, -1, keepdims=True) * 0.5
    )
    key_dash = scaling * ein("hge,hme->hgm", key_vec, draws_low)
    key_float = key_vec.astype(f32)
    key_exps = (
        key_dash - scaling * scaling * jnp.sum(key_float * key_float, -1, keepdims=True) * 0.5
    )
    local_peak = jnp.max(jnp.where(key_mask[None, :, None], key_dash, -1e30), axis=(1, 2))
    if rest == 2:
        key_peak = jnp.maximum(local_peak, lax.ppermute(local_peak, "rest", partners(2, 1)))
    elif rest > 1:
        key_peak = lax.pmax(local_peak, "rest")
    else:
        key_peak = local_peak
    key_feats = jnp.exp(
        jnp.where(key_mask[None, :, None], key_exps - key_peak[:, None, None], -10000.0)
    )
    key_feats_low = key_feats.astype(bf16)
    value_wide = jnp.concatenate([value_vec, jnp.ones((head_count, token_count, 1), bf16)], -1)
    kv = pair_sum(ein("hgm,hge->hme", key_feats_low, value_wide), rest)
    numer = ein("hgm,hme->hge", query_feats, kv)
    denominator = numer[..., head_size:]
    attended = numer[..., :head_size] / denominator

    def joined(per_head):
        return per_head.transpose(1, 0, 2).reshape(token_count, inner_width)

    attended_low = joined(attended).astype(bf16)
    output_low = output_weight.astype(bf16)
    middle = shifted + matmul(attended_low, output_low) + output_bias
    second_out, second_normed, second_inverse = layer_norm(middle, second_gain, second_bias)
    second_low = second_out.astype(bf16)
    hidden_low = hidden_weight.astype(bf16)
    hidden_pre = matmul(second_low, hidden_low) + hidden_bias
    hidden_act_low = jax.nn.gelu(hidden_pre, approximate=False).astype(bf16)
    return_low = return_weight.astype(bf16)
    outputs = middle + matmul(hidden_act_low, return_low) + return_bias

    upstream_low = upstream.astype(bf16)
    act_grad = contract_cols(upstream_low, return_low)
    return_weight_grad = contract_rows(hidden_act_low, upstream_low)
    return_bias_grad = jnp.sum(upstream, 0)
    pre_grad_low = (act_grad * gelu_slope(hidden_pre)).astype(bf16)
    hidden_weight_grad = contract_rows(second_low, pre_grad_low)
    hidden_bias_grad = jnp.sum(pre_grad_low.astype(f32), 0)
    second_grad = contract_cols(pre_grad_low, hidden_low)
    back_second, second_gain_grad, second_bias_grad = norm_back(
        second_grad, second_normed, second_inverse, second_gain
    )
    middle_grad = upstream + back_second
    branch_low = middle_grad.astype(bf16)
    output_weight_grad = contract_rows(attended_low, branch_low)
    output_bias_grad = jnp.sum(branch_low.astype(f32), 0)
    attended_grad = heads(contract_cols(branch_low, output_low))
    numer_grad = attended_grad / denominator
    denom_grad = -jnp.sum(attended_grad * attended, -1, keepdims=True) / denominator
    numer_wide = jnp.concatenate([numer_grad, denom_grad], -1)
    query_feat_grad = ein("hge,hme->hgm", numer_wide, kv)
    values_grad = pair_sum(ein("hgm,hge->hme", query_feats, numer_wide), rest)
    key_feat_grad = ein("hge,hme->hgm", value_wide, values_grad)
    value_grad = ein("hgm,hme->hge", key_feats_low, values_grad[..., :head_size]).astype(bf16)
    query_exp = query_feat_grad * query_feats
    query_grad = (
        scaling * ein("hgm,hme->hge", query_exp, draws_low)
        - jnp.sum(query_exp, -1, keepdims=True) * scaling * scaling * query_float
    )
    key_exp = key_feat_grad * key_feats
    key_grad = (
        scaling * ein("hgm,hme->hge", key_exp, draws_low)
        - jnp.sum(key_exp, -1, keepdims=True) * scaling * scaling * key_float
    )
    joint_grad_low = jnp.concatenate(
        [joined(query_grad.astype(bf16)), joined(key_grad.astype(bf16)), joined(value_grad)], 1
    )
    joint_grad = contract_rows(first_low, joint_grad_low)
    first_grad = contract_cols(joint_grad_low, joint_low)
    back_first, first_gain_grad, first_bias_grad = norm_back(
        first_grad, first_normed, first_inverse, first_gain
    )
    input_grad = middle_grad + back_first
    tissue_grad = jnp.where(
        jnp.arange(tissue_table.shape[0])[:, None] == tissue, jnp.sum(input_grad, 0), 0.0
    )

    def return_home(values):
        got = jnp.stack(swap_blocks(list(values.reshape(homes, gene_count, model_width)), homes))
        return jnp.stack([lax.dynamic_index_in_dim(got, home ^ c, 0, False) for c in range(homes)])

    pieces = [
        tissue_grad,
        first_gain_grad,
        first_bias_grad,
        joint_grad,
        output_weight_grad,
        output_bias_grad,
        second_gain_grad,
        second_bias_grad,
        hidden_weight_grad,
        hidden_bias_grad,
        return_weight_grad,
        return_bias_grad,
    ]
    flat = jnp.concatenate([p.reshape(-1) for p in pieces])
    unit = 128 * 8 * sizes["cells"] * homes * rest
    count = -(-flat.shape[0] // unit) * unit
    flat = jnp.pad(flat, (0, count - flat.shape[0])).reshape(-1, 128)
    flat = sum_everywhere(flat, sizes).reshape(-1)
    results, at = [], 0
    for p in pieces:
        results.append(flat[at : at + p.size].reshape(p.shape))
        at += p.size
    return (return_home(outputs), return_home(input_grad)) + tuple(results)
```

```python
import functools

import jax
import jax.numpy as jnp
from jax import lax
from jax.experimental import pallas as pl
from jax.experimental.pallas import tpu as pltpu
from jax.sharding import Mesh
from jax.sharding import PartitionSpec as P

EPSILON = 1e-05
LOWEST = -1e30
bf16 = jnp.bfloat16
f32 = jnp.float32
LANES = 128


def dot(left, right):
    return jnp.dot(left, right, preferred_element_type=f32)


def dot_lanes(left, right):
    return lax.dot_general(left, right, (((1,), (1,)), ((), ())), preferred_element_type=f32)


def norm_rows(values):
    centered = values - jnp.mean(values, 0, keepdims=True)
    inverse = lax.rsqrt(jnp.mean(centered * centered, 0, keepdims=True) + EPSILON)
    return centered * inverse, inverse


def norm_back_rows(upstream, normed, inverse, gain):
    scaled = upstream * gain
    return inverse * (
        scaled
        - jnp.mean(scaled, 0, keepdims=True)
        - normed * jnp.mean(scaled * normed, 0, keepdims=True)
    )


def fold(values):
    total = values[:, :LANES]
    for at in range(LANES, values.shape[1], LANES):
        total = total + values[:, at : at + LANES]
    return total


def split_low(values):
    high = values.astype(bf16)
    return high, (values - high.astype(f32)).astype(bf16)


def lane_index(shape):
    return lax.broadcasted_iota(jnp.int32, shape, len(shape) - 1)


def row_index(shape):
    return lax.broadcasted_iota(jnp.int32, shape, len(shape) - 2)


def merged(own, other, kept_rows, kept_lanes):
    own_peak, other_peak = own[0:1, 127:128], other[0:1, 127:128]
    peak = jnp.maximum(own_peak, other_peak)
    total = own * jnp.exp(own_peak - peak) + other * jnp.exp(other_peak - peak)
    inside = (row_index(own.shape) < kept_rows) & (lane_index(own.shape) < kept_lanes)
    return jnp.where(inside, total, 0.0), peak


class Sizes:
    def __init__(self, mesh_sizes, inputs, feature_draws, hidden_weight):
        self.homes, self.rest = mesh_sizes["home"], mesh_sizes["rest"]
        _, self.genes, self.width = inputs.shape
        self.heads, self.feats, self.head = feature_draws.shape
        self.inner = self.heads * self.head
        self.hidden = hidden_weight.shape[1]
        self.rows = -(-self.feats // 16) * 16
        self.ext = self.head + 16
        self.scale = self.head ** (-0.25)


def whole(*shape):
    return pl.BlockSpec(shape, lambda i, n=len(shape): (0,) * n)


def per_block(*shape, base=0):
    return pl.BlockSpec((1,) + shape, lambda i, n=len(shape): (i + base,) + (0,) * n)


PARAMS = dict(vmem_limit_bytes=56 * 1024 * 1024)


def keys_body(s, base, count, fresh, *refs):
    refs = list(refs)
    place = refs.pop(0)
    xs = [refs.pop(0) for _ in range(count)]
    cols, joint_t, draws = refs.pop(0), refs.pop(0), refs.pop(0)
    if not fresh:
        kv_prev = refs.pop(0)
        refs.pop(0), refs.pop(0)
    kv, shifted, qkv, x_scr, ext = refs
    j = pl.program_id(0)
    for n in range(count):

        @pl.when(j == n)
        def _(n=n):
            x_scr[...] = xs[n][...]

    @pl.when(j == 0)
    def _():
        if fresh:
            kv[...] = jnp.where(lane_index(kv.shape) == 127, LOWEST, 0.0)
        else:
            kv[...] = kv_prev[...]
        tail = (LANES - s.head, s.genes)
        ext[s.head :, :] = jnp.where(row_index(tail) == 0, 1.0, 0.0).astype(bf16)

    x = x_scr[...].T + cols[:, 6:7]
    shifted[0] = x
    normed, _ = norm_rows(x)
    first = (normed * cols[:, 0:1] + cols[:, 1:2]).astype(bf16)
    for part in range(3):
        rows = slice(part * s.inner, (part + 1) * s.inner)
        qkv[0, rows, :] = dot(joint_t[rows, :], first).astype(bf16)
    spots = place[base + j] + lane_index((1, s.genes))
    valid = spots < place[s.homes]
    scale = s.scale

    def head(h, carry):
        at = pl.multiple_of(h * s.head, s.head)
        key = qkv[0, pl.ds(s.inner + at, s.head), :]
        ext[: s.head, :] = qkv[0, pl.ds(2 * s.inner + at, s.head), :]
        dash = dot(draws[h], key)
        key_f = key.astype(f32)
        cut = jnp.sum(key_f * key_f, 0, keepdims=True) * (scale * scale * 0.5)
        top = jnp.max(dash, 0, keepdims=True) * scale
        top = jnp.max(jnp.where(valid, top, LOWEST), 1, keepdims=True)
        before = kv[h]
        old = before[0:1, 127:128]
        new = jnp.maximum(old, top)
        feats = jnp.exp(scale * dash - jnp.where(valid, cut + new, 1e30)).astype(bf16)
        part = dot_lanes(feats, ext[...])
        total = before * jnp.exp(old - new) + part
        kv[h] = jnp.where(lane_index(total.shape) == 127, new, total)
        return carry

    lax.fori_loop(0, s.heads, head, 0, unroll=True)


def run_keys(s, base, count, place, xs, cols, joint_t, draws, before=None):
    kv_shape = (s.heads, s.rows, LANES)
    shifted_shape = (s.homes, s.width, s.genes)
    qkv_shape = (s.homes, 3 * s.inner, s.genes)
    smem = pl.BlockSpec(memory_space=pltpu.SMEM)
    in_specs = [smem] + [whole(s.genes, s.width)] * count
    in_specs += [whole(*a.shape) for a in (cols, joint_t, draws)]
    args = [place, *xs, cols, joint_t, draws]
    aliases = {}
    if before is not None:
        at = len(args)
        in_specs += [whole(*kv_shape), pl.BlockSpec(memory_space=pl.ANY), pl.BlockSpec(memory_space=pl.ANY)]
        args += list(before)
        aliases = {at + 1: 1, at + 2: 2}
    return pl.pallas_call(
        functools.partial(keys_body, s, base, count, before is None),
        grid=(count,),
        in_specs=in_specs,
        out_specs=[
            whole(*kv_shape),
            per_block(s.width, s.genes, base=base),
            per_block(3 * s.inner, s.genes, base=base),
        ],
        out_shape=[
            jax.ShapeDtypeStruct(kv_shape, f32),
            jax.ShapeDtypeStruct(shifted_shape, f32),
            jax.ShapeDtypeStruct(qkv_shape, bf16),
        ],
        scratch_shapes=[
            pltpu.VMEM((s.genes, s.width), f32),
            pltpu.VMEM((LANES, s.genes), bf16),
        ],
        input_output_aliases=aliases,
        compiler_params=pltpu.CompilerParams(**PARAMS),
        name="keys",
    )(*args)


def middle_body(s, *refs):
    refs = list(refs)
    kv_own, kv_other, shifted, qkv = (refs.pop(0) for _ in range(4))
    cots = [refs.pop(0) for _ in range(s.homes)]
    cols, hidden_bias, draws, draws_t, out_w, out_wt = (refs.pop(0) for _ in range(6))
    hid_w, hid_wt, ret_w, ret_wt, joint = (refs.pop(0) for _ in range(5))
    outputs, middle_grad, query_part, values_grad, peaks, early = (refs.pop(0) for _ in range(6))
    kv3, kv_t, feats, att, att_low, over, att_grad, query_grad, cot_scr = (refs.pop(0) for _ in range(9))
    acc_q, acc_o, acc_r, acc_h, acc_cols, acc_hb = refs
    j = pl.program_id(0)
    scale = s.scale
    ext = s.ext

    @pl.when(j == 0)
    def _():
        eye_shape = (2 * ext, 2 * ext)
        eye = (row_index(eye_shape) == lane_index(eye_shape)).astype(f32).astype(bf16)
        for h in range(s.heads):
            total, peak = merged(kv_own[h], kv_other[h], s.feats, s.head + 1)
            peaks[h : h + 1, :] = jnp.broadcast_to(peak, (1, LANES))
            high, low = split_low(total[:, :ext])
            both = jnp.concatenate([high, low], 1)
            kv3[h] = jnp.concatenate([both, high], 1)
            kv_t[h] = dot_lanes(eye, both).astype(bf16)
        for acc in (acc_q, acc_o, acc_r, acc_h, acc_cols, acc_hb, values_grad):
            acc[...] = jnp.zeros_like(acc)

    for n in range(s.homes):

        @pl.when(j == n)
        def _(n=n):
            cot_scr[...] = cots[n][...]

    def attend(h, carry):
        at = pl.multiple_of(h * s.head, s.head)
        query = qkv[0, pl.ds(at, s.head), :]
        query_f = query.astype(f32)
        cut = jnp.sum(query_f * query_f, 0, keepdims=True) * (scale * scale * 0.5)
        value = jnp.exp(scale * dot(draws[h], query) - cut)
        feats[h] = value
        both = dot(kv_t[h], value.astype(bf16))
        total = both[:ext] + both[ext:]
        inverse = 1.0 / total[s.head : s.head + 1]
        over[h] = jnp.broadcast_to(inverse, over.shape[1:])
        result = total[: s.head] * inverse
        att[pl.ds(at, s.head), :] = result
        att_low[pl.ds(at, s.head), :] = result.astype(bf16)
        return carry

    lax.fori_loop(0, s.heads, attend, 0, unroll=True)

    x = shifted[0]
    middle = x + dot(out_wt[...], att_low[...]) + cols[:, 2:3]
    normed, inverse = norm_rows(middle)
    gain = cols[:, 3:4]
    second = (normed * gain + cols[:, 4:5]).astype(bf16)
    pre = dot(hid_wt[...], second) + hidden_bias[:, 0:1]
    cumulative = 0.5 * (1.0 + lax.erf(pre * 0.7071067811865476))
    act = (pre * cumulative).astype(bf16)
    slope = cumulative + pre * (jnp.exp(-0.5 * pre * pre) * 0.3989422804014327)
    outputs[0] = (middle + dot(ret_wt[...], act) + cols[:, 5:6]).T
    cot = cot_scr[...].T
    cot_low = cot.astype(bf16)
    pre_grad = dot(ret_w[...], cot_low) * slope
    pre_low = pre_grad.astype(bf16)
    acc_r[...] += dot_lanes(cot_low, act)
    acc_h[...] += dot_lanes(second, pre_low)
    acc_hb[...] += fold(pre_low.astype(f32))
    second_grad = dot(hid_w[...], pre_low)
    grad = cot + norm_back_rows(second_grad, normed, inverse, gain)
    middle_grad[0] = grad
    branch = grad.astype(bf16)
    acc_cols[0] += fold(branch.astype(f32))
    acc_cols[1] += fold(second_grad * normed)
    acc_cols[2] += fold(second_grad)
    acc_cols[3] += fold(cot)
    acc_o[...] += dot_lanes(branch, att_low[...])
    att_grad[...] = dot(out_w[...], branch)

    def back(h, carry):
        at = pl.multiple_of(h * s.head, s.head)
        upstream = att_grad[pl.ds(at, s.head), :]
        inverse = over[h][0:1]
        numer = upstream * inverse
        denom = -jnp.sum(upstream * att[pl.ds(at, s.head), :], 0, keepdims=True) * inverse
        tail_shape = (ext - s.head, s.genes)
        tail = jnp.where(row_index(tail_shape) == 0, denom, 0.0)
        high, low = split_low(jnp.concatenate([numer, tail], 0))
        value = feats[h]
        gap = jnp.zeros((LANES - ext, s.genes), bf16)
        sums = dot_lanes(value.astype(bf16), jnp.concatenate([high, gap, low, gap], 0))
        values_grad[h] += sums[:, :LANES] + sums[:, LANES:]
        back_feats = dot(kv3[h], jnp.concatenate([high, high, low], 0)) * value
        query = qkv[0, pl.ds(at, s.head), :].astype(f32)
        total = jnp.sum(back_feats, 0, keepdims=True)
        result = scale * dot(draws_t[h], back_feats.astype(bf16)) - query * (total * (scale * scale))
        query_grad[pl.ds(at, s.head), :] = result.astype(bf16)
        return carry

    lax.fori_loop(0, s.heads, back, 0, unroll=True)
    first = (norm_rows(x)[0] * cols[:, 0:1] + cols[:, 1:2]).astype(bf16)
    acc_q[...] += dot_lanes(first, query_grad[...])
    query_part[0] = dot(joint[:, : s.inner], query_grad[...])

    @pl.when(j == s.homes - 1)
    def _():
        at = 0
        for acc in (acc_q, acc_o, acc_r, acc_h):
            for tile in range(acc.shape[1] // LANES):
                early[at : at + s.width, :] = acc[:, tile * LANES : (tile + 1) * LANES]
                at += s.width
        spare = s.hidden % LANES
        lane = lane_index((s.width, LANES))
        last = jnp.zeros((s.width, LANES), f32)
        spot = 2 * spare
        for n in range(4):
            last = jnp.where(lane == spot, jnp.sum(acc_cols[n], 1, keepdims=True), last)
            spot += 1
        for n in range(s.hidden // s.width):
            piece = acc_hb[n * s.width : (n + 1) * s.width, :]
            last = jnp.where(lane == spot, jnp.sum(piece, 1, keepdims=True), last)
            spot += 1
        if spare:
            tops = [acc[:, s.hidden - spare :] for acc in (acc_r, acc_h)]
            last = jnp.concatenate(tops + [last[:, 2 * spare :]], 1)
        early[at : at + s.width, :] = last
        at += s.width
        if at < early.shape[0]:
            early[at:, :] = jnp.zeros((early.shape[0] - at, LANES), f32)


def early_rows(s, parts):
    tiles = 2 * (s.inner // LANES) + 2 * (s.hidden // LANES) + 1
    return -(-tiles * s.width // (8 * parts)) * 8 * parts


def run_middle(s, parts, kv_own, kv_other, shifted, qkv, cots, weights):
    small = (s.heads, s.rows, LANES)
    args = [kv_own, kv_other, shifted, qkv, *cots, *weights]
    in_specs = [whole(*small), whole(*small), per_block(s.width, s.genes), per_block(s.inner, s.genes)]
    in_specs += [whole(s.genes, s.width)] * s.homes + [whole(*a.shape) for a in weights]
    rows = early_rows(s, parts)
    tokens = (s.homes, s.width, s.genes)
    return pl.pallas_call(
        functools.partial(middle_body, s),
        grid=(s.homes,),
        in_specs=in_specs,
        out_specs=[
            per_block(s.genes, s.width),
            per_block(s.width, s.genes),
            per_block(s.width, s.genes),
            whole(*small),
            whole(16, LANES),
            whole(rows, LANES),
        ],
        out_shape=[
            jax.ShapeDtypeStruct((s.homes, s.genes, s.width), f32),
            jax.ShapeDtypeStruct(tokens, f32),
            jax.ShapeDtypeStruct(tokens, f32),
            jax.ShapeDtypeStruct(small, f32),
            jax.ShapeDtypeStruct((16, LANES), f32),
            jax.ShapeDtypeStruct((rows, LANES), f32),
        ],
        scratch_shapes=[
            pltpu.VMEM((s.heads, s.rows, 3 * s.ext), bf16),
            pltpu.VMEM((s.heads, 2 * s.ext, s.rows), bf16),
            pltpu.VMEM((s.heads, s.rows, s.genes), f32),
            pltpu.VMEM((s.inner, s.genes), f32),
            pltpu.VMEM((s.inner, s.genes), bf16),
            pltpu.VMEM((s.heads, 8, s.genes), f32),
            pltpu.VMEM((s.inner, s.genes), f32),
            pltpu.VMEM((s.inner, s.genes), bf16),
            pltpu.VMEM((s.genes, s.width), f32),
            pltpu.VMEM((s.width, s.inner), f32),
            pltpu.VMEM((s.width, s.inner), f32),
            pltpu.VMEM((s.width, s.hidden), f32),
            pltpu.VMEM((s.width, s.hidden), f32),
            pltpu.VMEM((4, s.width, LANES), f32),
            pltpu.VMEM((s.hidden, LANES), f32),
        ],
        compiler_params=pltpu.CompilerParams(**PARAMS),
        name="middle",
    )(*args)


def last_body(s, groups, *refs):
    refs = list(refs)
    place, vg_own, vg_other, peaks, shifted, keys, values = (refs.pop(0) for _ in range(7))
    middle_grad, query_part, cols, draws, draws_t, joint = (refs.pop(0) for _ in range(6))
    input_grad, late = (refs.pop(0) for _ in range(2))
    vg2, vg_t, ext2, grads, acc, acc_cols = refs
    j = pl.program_id(0)
    scale = s.scale
    ext = s.ext

    @pl.when(j == 0)
    def _():
        eye_shape = (2 * ext, 2 * ext)
        eye = (row_index(eye_shape) == lane_index(eye_shape)).astype(f32).astype(bf16)
        for h in range(s.heads):
            total = vg_own[h] + vg_other[h]
            inside = row_index(total.shape) < s.feats
            high, low = split_low(jnp.where(inside, total, 0.0)[:, :ext])
            both = jnp.concatenate([high, low], 1)
            vg2[h] = both
            vg_t[h] = dot_lanes(eye, both).astype(bf16)
        tail = (ext - s.head, s.genes)
        ones = jnp.where(row_index(tail) == 0, 1.0, 0.0).astype(bf16)
        ext2[s.head : ext, :] = ones
        ext2[ext + s.head :, :] = ones
        acc[...] = jnp.zeros_like(acc)
        acc_cols[...] = jnp.zeros_like(acc_cols)

    spots = place[j] + lane_index((1, s.genes))
    valid = spots < place[s.homes]

    def head(h, carry):
        at = pl.multiple_of(h * s.head, s.head)
        key = keys[0, pl.ds(at, s.head), :]
        value = values[0, pl.ds(at, s.head), :]
        ext2[: s.head, :] = value
        ext2[ext : ext + s.head, :] = value
        key_f = key.astype(f32)
        cut = jnp.sum(key_f * key_f, 0, keepdims=True) * (scale * scale * 0.5)
        cut = jnp.where(valid, cut + peaks[pl.ds(h, 1), 0:1], 1e30)
        feats = jnp.exp(scale * dot(draws[h], key) - cut)
        back_feats = dot(vg2[h], ext2[...]) * feats
        total = jnp.sum(back_feats, 0, keepdims=True)
        result = scale * dot(draws_t[h], back_feats.astype(bf16)) - key_f * (total * (scale * scale))
        grads[pl.ds(at, s.head), :] = result.astype(bf16)
        both = dot(vg_t[h], feats.astype(bf16))
        result = both[: s.head] + both[ext : ext + s.head]
        grads[pl.ds(s.inner + at, s.head), :] = result.astype(bf16)
        return carry

    lax.fori_loop(0, s.heads, head, 0, unroll=True)
    x = shifted[0]
    normed, inverse = norm_rows(x)
    gain = cols[:, 0:1]
    first = (normed * gain + cols[:, 1:2]).astype(bf16)
    acc[...] += dot_lanes(first, grads[...])
    first_grad = query_part[0] + dot(joint[:, s.inner :], grads[...])
    result = middle_grad[0] + norm_back_rows(first_grad, normed, inverse, gain)
    input_grad[0] = result.T
    acc_cols[0] += fold(first_grad * normed)
    acc_cols[1] += fold(first_grad)
    acc_cols[2] += fold(result)

    @pl.when(j == s.homes - 1)
    def _():
        at = 0
        for tile in range(acc.shape[1] // LANES):
            late[at : at + s.width, :] = acc[:, tile * LANES : (tile + 1) * LANES]
            at += s.width
        lane = lane_index((s.width, LANES))
        sums = [jnp.sum(acc_cols[n], 1, keepdims=True) for n in range(3)]
        tile = jnp.where(lane == 0, sums[0], jnp.where(lane == 1, sums[1], 0.0))
        late[at : at + s.width, :] = jnp.where(lane == 2 + place[s.homes + 1], sums[2], tile)
        at += s.width
        if at < late.shape[0]:
            late[at:, :] = jnp.zeros((late.shape[0] - at, LANES), f32)


def late_rows(s, parts):
    tiles = 2 * (s.inner // LANES) + 1
    return -(-tiles * s.width // (8 * parts)) * 8 * parts


def run_last(s, parts, groups, place, vg_own, vg_other, peaks, shifted, qkv, middle_grad, query_part, weights):
    small = (s.heads, s.rows, LANES)
    rows = late_rows(s, parts)
    smem = pl.BlockSpec(memory_space=pltpu.SMEM)
    third = (1, s.inner, s.genes)
    in_specs = [smem, whole(*small), whole(*small), whole(16, LANES), per_block(s.width, s.genes)]
    in_specs += [pl.BlockSpec(third, lambda i: (i, 1, 0)), pl.BlockSpec(third, lambda i: (i, 2, 0))]
    in_specs += [per_block(s.width, s.genes)] * 2 + [whole(*a.shape) for a in weights]
    return pl.pallas_call(
        functools.partial(last_body, s, groups),
        grid=(s.homes,),
        in_specs=in_specs,
        out_specs=[per_block(s.genes, s.width), whole(rows, LANES)],
        out_shape=[
            jax.ShapeDtypeStruct((s.homes, s.genes, s.width), f32),
            jax.ShapeDtypeStruct((rows, LANES), f32),
        ],
        scratch_shapes=[
            pltpu.VMEM((s.heads, s.rows, 2 * s.ext), bf16),
            pltpu.VMEM((s.heads, 2 * s.ext, s.rows), bf16),
            pltpu.VMEM((2 * s.ext, s.genes), bf16),
            pltpu.VMEM((2 * s.inner, s.genes), bf16),
            pltpu.VMEM((s.width, 2 * s.inner), f32),
            pltpu.VMEM((3, s.width, LANES), f32),
        ],
        compiler_params=pltpu.CompilerParams(**PARAMS),
        name="last",
    )(place, vg_own, vg_other, peaks, shifted, qkv, qkv, middle_grad, query_part, *weights)


def partners(size, step):
    return [(i, i ^ step) for i in range(size)]


def swap_blocks(blocks, size):
    out = [blocks[0]]
    for k in range(1, size):
        out.append(lax.ppermute(blocks[k], "home", partners(size, k)))
    return out


def scatter_sum(value, axis, size):
    rows = value.shape[0] // size
    me = lax.axis_index(axis)

    def part(k):
        return lax.dynamic_slice_in_dim(value, (me ^ k) * rows, rows, 0)

    received = [lax.ppermute(part(k), axis, partners(size, k)) for k in range(1, size)]
    total = part(0)
    for r in received:
        total = total + r
    return total


def gather_parts(value, axis, size):
    rows = value.shape[0]
    me = lax.axis_index(axis)
    out = jnp.zeros((rows * size, value.shape[1]), value.dtype)
    received = [value] + [lax.ppermute(value, axis, partners(size, k)) for k in range(1, size)]
    for k, r in enumerate(received):
        out = lax.dynamic_update_slice_in_dim(out, r, (me ^ k) * rows, 0)
    return out


def sum_everywhere(value, sizes):
    axes = ("rest", "cells", "home")
    if any(sizes[a] & (sizes[a] - 1) or sizes[a] > 4 for a in axes):
        return lax.psum(value, axes)
    for a in axes:
        if sizes[a] > 1:
            value = scatter_sum(value, a, sizes[a])
    for a in reversed(axes):
        if sizes[a] > 1:
            value = gather_parts(value, a, sizes[a])
    return value


def solution(mesh):
    def run(inputs, lengths, *others):
        cells_axis, genes_axis = mesh.shape["cells"], mesh.shape["genes"]
        homes = inputs.shape[0] // cells_axis
        rest = genes_axis // homes
        sizes = {"cells": cells_axis, "home": homes, "rest": rest}
        fine = Mesh(mesh.devices.reshape(cells_axis, homes, rest), ("cells", "home", "rest"))
        tokens = P("cells", ("home", "rest"), None)
        return jax.shard_map(
            lambda *args: local(sizes, *args),
            mesh=fine,
            in_specs=(tokens, P("cells"), P("cells")) + (P(),) * 13 + (tokens,),
            out_specs=(tokens, tokens) + (P(),) * 12,
            check_vma=False,
        )(inputs, lengths, *others)

    return run


def local(
    sizes,
    inputs,
    lengths,
    tissue_ids,
    tissue_table,
    first_gain,
    first_bias,
    joint_weight,
    feature_draws,
    output_weight,
    output_bias,
    second_gain,
    second_bias,
    hidden_weight,
    hidden_bias,
    return_weight,
    return_bias,
    cotangent,
):
    s = Sizes(sizes, inputs, feature_draws, hidden_weight)
    homes, rest = s.homes, s.rest
    parts = sizes["cells"] * homes * rest
    home = lax.axis_index("home")
    side = lax.axis_index("rest")

    def pick(array, k):
        return lax.dynamic_index_in_dim(array, home ^ k, 0, False)

    arrived = swap_blocks([pick(inputs, k) for k in range(homes)], homes)
    arrived_cot = swap_blocks([pick(cotangent, k).astype(f32) for k in range(homes)], homes)
    starts = jnp.stack([((home ^ k) * rest + side) * s.genes for k in range(homes)])
    tissue = pick(tissue_ids, 0)
    place = jnp.concatenate([starts, pick(lengths, 0)[None], tissue[None]]).astype(jnp.int32)

    joint_low = joint_weight.astype(bf16)
    joint_t = joint_low.T
    filler = jnp.broadcast_to(feature_draws[:, :1], (s.heads, s.rows - s.feats, s.head))
    draws = jnp.concatenate([feature_draws, filler], 1).astype(bf16)
    draws_t = jnp.pad(feature_draws, ((0, 0), (0, s.rows - s.feats), (0, 0))).transpose(0, 2, 1).astype(bf16)
    out_low, hid_low, ret_low = (w.astype(bf16) for w in (output_weight, hidden_weight, return_weight))
    cols = jnp.stack(
        [
            first_gain,
            first_bias,
            output_bias,
            second_gain,
            second_bias,
            return_bias,
            lax.dynamic_index_in_dim(tissue_table, tissue, 0, False),
            first_gain,
        ],
        1,
    )

    state = run_keys(s, 0, 1, place, arrived[:1], cols, joint_t, draws)
    if homes > 1:
        state = run_keys(s, 1, homes - 1, place, arrived[1:], cols, joint_t, draws, state)
    kv, shifted, qkv = state

    def other(value):
        return lax.ppermute(value, "rest", partners(2, 1)) if rest == 2 else jnp.zeros_like(value)

    if rest > 2:
        peak = kv[:, :1, 127:]
        top = lax.pmax(peak, "rest")
        kv = lax.psum(kv * jnp.exp(peak - top), "rest")
        kv = jnp.where(jnp.arange(LANES) == 127, top, kv)
    kv_other = other(kv) if rest == 2 else jnp.where(jnp.arange(LANES) == 127, LOWEST, jnp.zeros_like(kv))
    weights = (
        cols,
        hidden_bias[:, None],
        draws,
        draws_t,
        out_low,
        out_low.T,
        hid_low,
        hid_low.T,
        ret_low,
        ret_low.T,
        joint_low,
    )
    outputs, middle_grad, query_part, vg, peaks, early = run_middle(
        s, parts, kv, kv_other, shifted, qkv, arrived_cot, weights
    )
    if rest > 2:
        vg = lax.psum(vg, "rest")
    vg_other = other(vg)
    input_grad, late = run_last(
        s, parts, 0, place, vg, vg_other, peaks, shifted, qkv, middle_grad, query_part, (cols, draws, draws_t, joint_low)
    )

    def return_home(values):
        got = jnp.stack(swap_blocks([values[k] for k in range(homes)], homes))
        return jnp.stack([lax.dynamic_index_in_dim(got, home ^ c, 0, False) for c in range(homes)])

    early = sum_everywhere(early, sizes)
    late = sum_everywhere(late, sizes)

    def tiles(buffer, first_tile, count):
        return [buffer[(first_tile + n) * s.width : (first_tile + n + 1) * s.width] for n in range(count)]

    ni, nh, spare = s.inner // LANES, s.hidden // LANES, s.hidden % LANES
    mixed = tiles(early, 2 * ni + 2 * nh, 1)[0]
    joint_grad = jnp.concatenate(tiles(early, 0, ni) + tiles(late, 0, 2 * ni), 1)
    output_weight_grad = jnp.concatenate(tiles(early, ni, ni), 1).T
    return_weight_grad = jnp.concatenate(tiles(early, 2 * ni, nh) + [mixed[:, :spare]], 1).T
    hidden_weight_grad = jnp.concatenate(tiles(early, 2 * ni + nh, nh) + [mixed[:, spare : 2 * spare]], 1)
    at = 2 * spare
    columns = mixed[:, at : at + 4 + s.hidden // s.width].T
    last = tiles(late, 2 * ni, 1)[0][:, : 2 + tissue_table.shape[0]].T
    return (
        return_home(outputs),
        return_home(input_grad),
        last[2:],
        last[0],
        last[1],
        joint_grad,
        output_weight_grad,
        columns[0],
        columns[1],
        columns[2],
        hidden_weight_grad,
        columns[4:].reshape(-1),
        return_weight_grad,
        columns[3],
    )
```

```python
import functools

import jax
import jax.numpy as jnp
from jax import lax
from jax.experimental import pallas as pl
from jax.experimental.pallas import tpu as pltpu
from jax.sharding import Mesh
from jax.sharding import PartitionSpec as P

EPSILON = 1e-05
LOWEST = -1e30
bf16 = jnp.bfloat16
f32 = jnp.float32
LANES = 128


def dot(left, right):
    return jnp.dot(left, right, preferred_element_type=f32)


def dot_lanes(left, right):
    return lax.dot_general(left, right, (((1,), (1,)), ((), ())), preferred_element_type=f32)


def norm_rows(values):
    centered = values - jnp.mean(values, 0, keepdims=True)
    inverse = lax.rsqrt(jnp.mean(centered * centered, 0, keepdims=True) + EPSILON)
    return centered * inverse, inverse


def norm_back_rows(upstream, normed, inverse, gain):
    scaled = upstream * gain
    return inverse * (
        scaled
        - jnp.mean(scaled, 0, keepdims=True)
        - normed * jnp.mean(scaled * normed, 0, keepdims=True)
    )


def fold(values):
    total = values[:, :LANES]
    for at in range(LANES, values.shape[1], LANES):
        total = total + values[:, at : at + LANES]
    return total


def split_low(values):
    high = values.astype(bf16)
    return high, (values - high.astype(f32)).astype(bf16)


def lane_index(shape):
    return lax.broadcasted_iota(jnp.int32, shape, len(shape) - 1)


def row_index(shape):
    return lax.broadcasted_iota(jnp.int32, shape, len(shape) - 2)


class Sizes:
    def __init__(self, mesh_sizes, inputs, feature_draws, hidden_weight):
        self.homes, self.rest = mesh_sizes["home"], mesh_sizes["rest"]
        _, self.genes, self.width = inputs.shape
        self.heads, self.feats, self.head = feature_draws.shape
        self.inner = self.heads * self.head
        self.hidden = hidden_weight.shape[1]
        self.rows = -(-self.feats // 16) * 16
        self.ext = self.head + 16
        self.scale = self.head ** (-0.25)


VMEM = pl.BlockSpec(memory_space=pltpu.VMEM)
SMEM = pl.BlockSpec(memory_space=pltpu.SMEM)


def call(name, body, args, out, scratch=(), megabytes=4, smem=0, aliases={}, flops=0):
    return pl.pallas_call(
        body,
        out_shape=out,
        in_specs=[SMEM] * smem + [VMEM] * (len(args) - smem),
        out_specs=jax.tree.map(lambda _: VMEM, out),
        scratch_shapes=list(scratch),
        input_output_aliases=aliases,
        compiler_params=pltpu.CompilerParams(vmem_limit_bytes=megabytes * 1024 * 1024),
        cost_estimate=pl.CostEstimate(flops=int(flops), bytes_accessed=1024, transcendentals=0),
        name=name,
    )(*args)


def array(*shape, dtype=f32):
    return jax.ShapeDtypeStruct(shape, dtype)


def prepare_body(s, tissue, joint, draws, out_t, hid, ret_t, hidden_bias, *refs):
    rows, table = refs[:6], refs[6]
    joint_t, draws_low, draws_t, out_wt, out_w, hid_w, hid_wt, ret_wt, ret_w, joint_w, cols, bias = refs[7:]
    joint_w[...] = joint[...].astype(bf16)
    joint_t[...] = joint[...].T.astype(bf16)
    for h in range(s.heads):
        draw = draws[h]
        filler = jnp.broadcast_to(draw[:, :1], (s.head, s.rows - s.feats))
        draws_low[h] = jnp.concatenate([draw, filler], 1).T.astype(bf16)
        draws_t[h] = jnp.concatenate([draw, jnp.zeros_like(filler)], 1).astype(bf16)
    out_wt[...] = out_t[...].astype(bf16)
    out_w[...] = out_t[...].T.astype(bf16)
    hid_w[...] = hid[...].astype(bf16)
    hid_wt[...] = hid[...].T.astype(bf16)
    ret_wt[...] = ret_t[...].astype(bf16)
    ret_w[...] = ret_t[...].T.astype(bf16)
    stacked = [r[...] for r in rows] + [table[pl.ds(tissue[0], 1), :]]
    stacked += [jnp.zeros((1, s.width), f32)]
    cols[...] = jnp.concatenate(stacked, 0).T
    bias[...] = jnp.broadcast_to(hidden_bias[...], (8, s.hidden)).T


def prepare(s, tissue, joint, draws, out_t, hid, ret_t, hidden_bias, rows, table):
    w, i, f = s.width, s.inner, s.hidden
    out = [
        array(3 * i, w, dtype=bf16),
        array(s.heads, s.rows, s.head, dtype=bf16),
        array(s.heads, s.head, s.rows, dtype=bf16),
        array(w, i, dtype=bf16),
        array(i, w, dtype=bf16),
        array(w, f, dtype=bf16),
        array(f, w, dtype=bf16),
        array(w, f, dtype=bf16),
        array(f, w, dtype=bf16),
        array(w, 3 * i, dtype=bf16),
        array(w, 8),
        array(f, 8),
    ]
    args = [tissue[None], joint, draws, out_t, hid, ret_t, hidden_bias[None], *[r[None] for r in rows], table]
    return call("prepare", functools.partial(prepare_body, s), args, out, smem=1, megabytes=8, flops=4e9)


def keys_body(s, base, count, fresh, *refs):
    refs = list(refs)
    place = refs.pop(0)
    xs = [refs.pop(0) for _ in range(count)]
    cols, joint_t, draws = (refs.pop(0) for _ in range(3))
    if not fresh:
        kv_prev = refs.pop(0)
        refs.pop(0), refs.pop(0)
    kv, shifted, qkv, ext, dashes, tops, cuts = refs
    scale = s.scale
    last_row = s.rows - 1
    tail = (s.heads, LANES - s.head, s.genes)
    ext[:, s.head :, :] = jnp.where(row_index(tail) == 0, 1.0, 0.0).astype(bf16)
    if fresh:
        state = jnp.full((16, 1), LOWEST, f32)
    else:
        state = jnp.concatenate([kv_prev[h, last_row:, 0:1] for h in range(s.heads)] + [jnp.full((16 - s.heads, 1), LOWEST, f32)], 0)
    for n in range(count):
        x = xs[n][...] + cols[:, 6:7]
        shifted[base + n] = x
        normed, _ = norm_rows(x)
        first = (normed * cols[:, 0:1] + cols[:, 1:2]).astype(bf16)
        for part in (1, 2, 0):
            rows = slice(part * s.inner, (part + 1) * s.inner)
            made = dot(joint_t[rows, :], first).astype(bf16)
            qkv[base + n, rows, :] = made
            if part == 2:
                for h in range(s.heads):
                    ext[h, : s.head, :] = made[h * s.head : (h + 1) * s.head]
        for h in range(s.heads):
            key = qkv[base + n, s.inner + h * s.head : s.inner + (h + 1) * s.head, :]
            dash = dot(draws[h], key)
            dashes[h] = dash
            key_f = key.astype(f32)
            cuts[h : h + 1, :] = jnp.sum(key_f * key_f, 0, keepdims=True) * (scale * scale * 0.5)
            tops[h : h + 1, :] = jnp.max(dash, 0, keepdims=True) * scale
        valid = place[base + n] + lane_index((1, s.genes)) < place[s.homes]
        new = jnp.maximum(state, jnp.max(jnp.where(valid, tops[...], LOWEST), 1, keepdims=True))
        decay = jnp.exp(state - new)
        state = new
        lifts = jnp.where(valid, cuts[...] + new, 1e30)
        for h in range(s.heads):
            feats = jnp.exp(scale * dashes[h] - lifts[h : h + 1]).astype(bf16)
            part = dot_lanes(feats, ext[h])
            if n == 0 and fresh:
                kv[h] = part
            else:
                kv[h] = (kv_prev if n == 0 else kv)[h] * decay[h : h + 1] + part
    for h in range(s.heads):
        kv[h, last_row:, :] = jnp.broadcast_to(state[h : h + 1], (1, LANES))


def run_keys(s, base, count, place, xs, cols, joint_t, draws, before=None):
    out = [
        array(s.heads, s.rows, LANES),
        array(s.homes, s.width, s.genes),
        array(s.homes, 3 * s.inner, s.genes, dtype=bf16),
    ]
    args = [place, *xs, cols, joint_t, draws]
    aliases = {}
    if before is not None:
        aliases = {len(args) + 1: 1, len(args) + 2: 2}
        args += list(before)
    scratch = [
        pltpu.VMEM((s.heads, LANES, s.genes), bf16),
        pltpu.VMEM((s.heads, s.rows, s.genes), f32),
        pltpu.VMEM((16, s.genes), f32),
        pltpu.VMEM((16, s.genes), f32),
    ]
    body = functools.partial(keys_body, s, base, count, before is None)
    return call("keys", body, args, out, scratch, 10, 1, aliases, 3e9 * count)


def merged(own, other, kept_rows, kept_lanes):
    last = own.shape[0] - 1
    own_peak, other_peak = own[last:, 0:1], other[last:, 0:1]
    peak = jnp.maximum(own_peak, other_peak)
    total = own * jnp.exp(own_peak - peak) + other * jnp.exp(other_peak - peak)
    inside = (row_index(own.shape) < kept_rows) & (lane_index(own.shape) < kept_lanes)
    return jnp.where(inside, total, 0.0), peak


def eye_like(size):
    return (row_index((size, size)) == lane_index((size, size))).astype(f32).astype(bf16)


def middle_body(s, base, count, first, final, *refs):
    refs = list(refs)

    def take(n):
        taken = refs[:n]
        del refs[:n]
        return taken

    (side,) = take(1)
    before = take(2) if first else take(9)
    shifted, qkv = take(2)
    cots = take(count)
    cols, hidden_bias, draws, draws_t, out_w, out_wt = take(6)
    hid_w, hid_wt, ret_w, ret_wt, joint = take(5)
    outputs = take(count)
    middle_grad, query_part = take(2)
    results = take(3) if final else take(9)
    if first:
        kv3, kv_t = take(2) if final else results[:2]
    else:
        kv3, kv_t = before[:2]
    feats, att, att_low, over, att_grad, query_grad = take(6)
    cot_all, out_all, *sums = refs
    acc_q, acc_o, acc_r, acc_h, acc_cols, acc_hb, values_grad = sums
    scale = s.scale
    ext = s.ext
    if first:
        kv_own, kv_other = before
        eye = eye_like(2 * ext)
        for h in range(s.heads):
            total, _ = merged(kv_own[h], kv_other[h], s.feats, s.head + 1)
            high, low = split_low(total[:, :ext])
            kv3[h] = jnp.concatenate([high, low, high], 1)
            kv_t[h] = dot_lanes(eye, jnp.concatenate([high, low], 1)).astype(bf16)
        for acc in sums:
            acc[...] = jnp.zeros_like(acc)
    else:
        for acc, was in zip(sums, before[2:]):
            acc[...] = was[...]
    for n in range(count):
        cot_all[n] = cots[n][...]

    def block(j, carry):
        def attend(h):
            rows = slice(h * s.head, (h + 1) * s.head)
            query = qkv[base + j, rows, :]
            query_f = query.astype(f32)
            cut = jnp.sum(query_f * query_f, 0, keepdims=True) * (scale * scale * 0.5)
            value = jnp.exp(scale * dot(draws[h], query) - cut)
            feats[h] = value
            both = dot(kv_t[h], value.astype(bf16))
            total = both[:ext] + both[ext:]
            inverse = 1.0 / total[s.head : s.head + 1]
            over[h : h + 1, :] = inverse
            result = total[: s.head] * inverse
            att[rows, :] = result
            att_low[rows, :] = result.astype(bf16)

        for h in range(s.heads):
            attend(h)

        x = shifted[base + j]
        middle = x + dot(out_wt[...], att_low[...]) + cols[:, 2:3]
        normed, inverse = norm_rows(middle)
        gain = cols[:, 3:4]
        second = (normed * gain + cols[:, 4:5]).astype(bf16)
        pre = dot(hid_wt[...], second) + hidden_bias[:, 0:1]
        cumulative = 0.5 * (1.0 + lax.erf(pre * 0.7071067811865476))
        act = (pre * cumulative).astype(bf16)
        slope = cumulative + pre * (jnp.exp(-0.5 * pre * pre) * 0.3989422804014327)
        out_all[j] = middle + dot(ret_wt[...], act) + cols[:, 5:6]
        cot = cot_all[j]
        cot_low = cot.astype(bf16)
        pre_low = (dot(ret_w[...], cot_low) * slope).astype(bf16)
        acc_r[...] += dot_lanes(cot_low, act)
        acc_h[...] += dot_lanes(second, pre_low)
        acc_hb[...] += fold(pre_low.astype(f32))
        second_grad = dot(hid_w[...], pre_low)
        grad = cot + norm_back_rows(second_grad, normed, inverse, gain)
        middle_grad[j] = grad
        branch = grad.astype(bf16)
        acc_cols[0] += fold(branch.astype(f32))
        acc_cols[1] += fold(second_grad * normed)
        acc_cols[2] += fold(second_grad)
        acc_cols[3] += fold(cot)
        acc_o[...] += dot_lanes(branch, att_low[...])
        att_grad[...] = dot(out_w[...], branch)

        def back(h):
            rows = slice(h * s.head, (h + 1) * s.head)
            upstream = att_grad[rows, :]
            inverse = over[h : h + 1, :]
            numer = upstream * inverse
            denom = -jnp.sum(upstream * att[rows, :], 0, keepdims=True) * inverse
            tail_shape = (ext - s.head, s.genes)
            tail = jnp.where(row_index(tail_shape) == 0, denom, 0.0)
            high, low = split_low(jnp.concatenate([numer, tail], 0))
            value = feats[h]
            gap = jnp.zeros((LANES - ext, s.genes), bf16)
            sums = dot_lanes(value.astype(bf16), jnp.concatenate([high, gap, low, gap], 0))
            values_grad[h] += sums[:, :LANES] + sums[:, LANES:]
            back_feats = dot(kv3[h], jnp.concatenate([high, high, low], 0)) * value
            query = qkv[base + j, rows, :].astype(f32)
            total = jnp.sum(back_feats, 0, keepdims=True)
            result = scale * dot(draws_t[h], back_feats.astype(bf16)) - query * (total * (scale * scale))
            query_grad[rows, :] = result.astype(bf16)

        for h in range(s.heads):
            back(h)
        normal = (norm_rows(x)[0] * cols[:, 0:1] + cols[:, 1:2]).astype(bf16)
        acc_q[...] += dot_lanes(normal, query_grad[...])
        query_part[j] = dot(joint[:, : s.inner], query_grad[...])
        return carry

    lax.fori_loop(0, count, block, 0)
    for n in range(count):
        outputs[n][...] = out_all[n]
    if not final:
        if not first:
            results[0][...], results[1][...] = kv3[...], kv_t[...]
        for result, acc in zip(results[2:], sums):
            result[...] = acc[...]
        return
    results[0][...] = values_grad[...]
    keep, send = results[1:]
    spare = s.hidden % LANES
    lane = lane_index((s.width, LANES))
    last = jnp.zeros((s.width, LANES), f32)
    spot = 2 * spare
    for n in range(4):
        last = jnp.where(lane == spot, jnp.sum(acc_cols[n], 1, keepdims=True), last)
        spot += 1
    for n in range(s.hidden // s.width):
        piece = acc_hb[n * s.width : (n + 1) * s.width, :]
        last = jnp.where(lane == spot, jnp.sum(piece, 1, keepdims=True), last)
        spot += 1
    if spare:
        tops = [acc[:, s.hidden - spare :] for acc in (acc_r, acc_h)]
        last = jnp.concatenate(tops + [last[:, 2 * spare :]], 1)
    tiles = []
    for acc in (acc_q, acc_o, acc_r, acc_h):
        tiles += [(acc, n * LANES) for n in range(acc.shape[1] // LANES)]
    deal_tiles(side[0], s.width, keep, send, tiles, last)


def deal_tiles(side, width, keep, send, tiles, last):
    half = keep.shape[0]

    def put(row, value):
        for part in (0, 1):
            begin, end = max(row, part * half), min(row + value.shape[0], (part + 1) * half)
            if begin < end:
                piece = value[begin - row : end - row]
                spots = slice(begin - part * half, end - part * half)
                if send is None:
                    keep[spots, :] = piece
                    continue

                @pl.when(side == part)
                def _():
                    keep[spots, :] = piece

                @pl.when(side != part)
                def _():
                    send[spots, :] = piece

    row = 0
    for acc, at in tiles:
        put(row, acc[:, at : at + LANES])
        row += width
    put(row, last)
    row += width
    total = half if send is None else 2 * half
    if row < total:
        put(row, jnp.zeros((total - row, LANES), f32))


def padded(rows, parts):
    return -(-rows // (8 * parts)) * 8 * parts


def halves(s, tiles, parts):
    rows = padded(tiles * s.width, parts)
    return [array(rows // 2, LANES), array(rows // 2, LANES)]


def run_middle(s, parts, side, groups, kv_own, kv_other, shifted, qkv, cots, weights):
    sums = [
        array(s.width, s.inner),
        array(s.width, s.inner),
        array(s.width, s.hidden),
        array(s.width, s.hidden),
        array(4, s.width, LANES),
        array(s.hidden, LANES),
        array(s.heads, s.rows, LANES),
    ]
    forms = [
        array(s.heads, s.rows, 3 * s.ext, dtype=bf16),
        array(s.heads, 2 * s.ext, s.rows, dtype=bf16),
    ]
    ends = [array(s.heads, s.rows, LANES)]
    ends += halves(s, 2 * (s.inner // LANES) + 2 * (s.hidden // LANES) + 1, parts)
    before, base = [kv_own, kv_other], 0
    outputs, middle_grad, query_part = [], [], []
    for index, count in enumerate(groups):
        first, final = index == 0, index == len(groups) - 1
        tokens = array(count, s.width, s.genes)
        out = [array(s.width, s.genes)] * count + [tokens, tokens]
        out += ends if final else forms + sums
        scratch = list(forms) if first and final else []
        scratch += [
            array(s.heads, s.rows, s.genes),
            array(s.inner, s.genes),
            array(s.inner, s.genes, dtype=bf16),
            array(16, s.genes),
            array(s.inner, s.genes),
            array(s.inner, s.genes, dtype=bf16),
            tokens,
            tokens,
        ] + sums
        scratch = [pltpu.VMEM(a.shape, a.dtype) for a in scratch]
        args = [side[None], *before, shifted, qkv, *cots[base : base + count], *weights]
        body = functools.partial(middle_body, s, base, count, first, final)
        made = call("middle", body, args, out, scratch, 18, 1, flops=7e9 * count)
        outputs += made[:count]
        middle_grad.append(made[count])
        query_part.append(made[count + 1])
        before, base = made[count + 2 :], base + count
    return outputs, middle_grad, query_part, before


def last_body(s, groups, *refs):
    refs = list(refs)
    place, vg_own, vg_other, kv_own, kv_other, shifted, qkv = (refs.pop(0) for _ in range(7))
    middle_grads = [refs.pop(0) for _ in groups]
    query_parts = [refs.pop(0) for _ in groups]
    cols, draws, draws_t, joint = (refs.pop(0) for _ in range(4))
    input_grad = [refs.pop(0) for _ in range(s.homes)]
    keep, send, vg2, vg_t, ext2, grads, result_all, acc, acc_cols = refs
    scale = s.scale
    ext = s.ext
    eye = eye_like(ext)
    peaks = []
    for h in range(s.heads):
        total = vg_own[h] + vg_other[h]
        inside = row_index(total.shape) < s.feats
        high, low = split_low(jnp.where(inside, total, 0.0)[:, :ext])
        vg2[h] = jnp.concatenate([high, low], 1)
        vg_t[h] = dot_lanes(eye, high)[: s.head].astype(bf16)
        peaks.append(jnp.maximum(kv_own[h, s.rows - 1 :, 0:1], kv_other[h, s.rows - 1 :, 0:1]))
    tail = (s.heads, ext - s.head, s.genes)
    ones = jnp.where(row_index(tail) == 0, 1.0, 0.0).astype(bf16)
    ext2[:, s.head : ext, :] = ones
    ext2[:, ext + s.head :, :] = ones
    acc[...] = jnp.zeros_like(acc)
    acc_cols[...] = jnp.zeros_like(acc_cols)

    def block(base, middle_grad, query_part, i, carry):
        j = base + i
        valid = place[j] + lane_index((1, s.genes)) < place[s.homes]

        def head(h):
            rows = slice(h * s.head, (h + 1) * s.head)
            key = qkv[j, s.inner + h * s.head : s.inner + (h + 1) * s.head, :]
            value = qkv[j, 2 * s.inner + h * s.head : 2 * s.inner + (h + 1) * s.head, :]
            ext2[h, : s.head, :] = value
            ext2[h, ext : ext + s.head, :] = value
            key_f = key.astype(f32)
            cut = jnp.sum(key_f * key_f, 0, keepdims=True) * (scale * scale * 0.5)
            cut = jnp.where(valid, cut + peaks[h], 1e30)
            feats = jnp.exp(scale * dot(draws[h], key) - cut)
            back_feats = dot(vg2[h], ext2[h]) * feats
            total = jnp.sum(back_feats, 0, keepdims=True)
            result = scale * dot(draws_t[h], back_feats.astype(bf16)) - key_f * (total * (scale * scale))
            grads[rows, :] = result.astype(bf16)
            result = dot(vg_t[h], feats.astype(bf16))
            grads[s.inner + h * s.head : s.inner + (h + 1) * s.head, :] = result.astype(bf16)

        for h in range(s.heads):
            head(h)
        normed, inverse = norm_rows(shifted[j])
        gain = cols[:, 0:1]
        first = (normed * gain + cols[:, 1:2]).astype(bf16)
        acc[...] += dot_lanes(first, grads[...])
        first_grad = query_part[i] + dot(joint[:, s.inner :], grads[...])
        result = middle_grad[i] + norm_back_rows(first_grad, normed, inverse, gain)
        result_all[j] = result
        acc_cols[0] += fold(first_grad * normed)
        acc_cols[1] += fold(first_grad)
        acc_cols[2] += fold(result)
        return carry

    base = 0
    for count, middle_grad, query_part in zip(groups, middle_grads, query_parts):
        lax.fori_loop(0, count, functools.partial(block, base, middle_grad, query_part), 0)
        base += count
    for n in range(s.homes):
        input_grad[n][...] = result_all[n]
    lane = lane_index((s.width, LANES))
    sums = [jnp.sum(acc_cols[n], 1, keepdims=True) for n in range(3)]
    last = jnp.where(lane == 0, sums[0], jnp.where(lane == 1, sums[1], 0.0))
    last = jnp.where(lane == 2 + place[s.homes + 1], sums[2], last)
    tiles = [(acc, n * LANES) for n in range(acc.shape[1] // LANES)]
    deal_tiles(place[s.homes + 2], s.width, keep, send, tiles, last)


def run_last(s, parts, groups, place, vg_own, vg_other, kv_own, kv_other, shifted, qkv, middle_grad, query_part, weights):
    out = [array(s.width, s.genes)] * s.homes + halves(s, 2 * (s.inner // LANES) + 1, parts)
    scratch = [
        pltpu.VMEM((s.heads, s.rows, 2 * s.ext), bf16),
        pltpu.VMEM((s.heads, s.head, s.rows), bf16),
        pltpu.VMEM((s.heads, 2 * s.ext, s.genes), bf16),
        pltpu.VMEM((2 * s.inner, s.genes), bf16),
        pltpu.VMEM((s.homes, s.width, s.genes), f32),
        pltpu.VMEM((s.width, 2 * s.inner), f32),
        pltpu.VMEM((3, s.width, LANES), f32),
    ]
    args = [place, vg_own, vg_other, kv_own, kv_other, shifted, qkv, *middle_grad, *query_part, *weights]
    return call("last", functools.partial(last_body, s, groups), args, out, scratch, 10, 1, flops=15e9)


def partners(size, step):
    return [(i, i ^ step) for i in range(size)]


def send(values, axis, size):
    return [lax.ppermute(values[k], axis, partners(size, k)) for k in range(1, size)]


def add_split(index, terms, parts):
    rows = terms[0].shape[0] // parts

    def body(place, *refs):
        ins, outs = refs[: len(terms)], refs[len(terms) :]
        for k in range(parts):
            at = pl.multiple_of((place[0] ^ k) * rows, 8) if parts > 1 else 0
            total = ins[0][pl.ds(at, rows), :]
            for other in ins[1:]:
                total = total + other[pl.ds(at, rows), :]
            outs[k][...] = total

    out = [array(rows, LANES)] * parts
    return call("add_split", body, [index[None], *terms], out, smem=1, flops=1e9)


def stack_rows(pieces):
    def body(*refs):
        at = 0
        for ref in refs[:-1]:
            refs[-1][at : at + ref.shape[0], :] = ref[...]
            at += ref.shape[0]

    return call("stack", body, pieces, array(sum(p.shape[0] for p in pieces), LANES), flops=5e8)


def place_blocks(s, home, blocks):
    def body(place, *refs):
        for k in range(s.homes):
            refs[-1][place[0] ^ k] = refs[k][...]

    return call("place_blocks", body, [home[None], *blocks], array(s.homes, s.width, s.genes), smem=1, flops=1e9)


def finish_body(s, sizes, tissues, place, early_own, early_other, late_own, late_other, *refs):
    early, late = refs[-2:]
    outs = refs[:-2]
    if sizes is None:
        early[...] = early_own[...]
        late[...] = late_own[...]
    else:
        cells, homes = sizes
        for whole_ref, sources in ((early, (early_own, early_other)), (late, (late_own, late_other))):
            rows = whole_ref.shape[0] // (2 * cells * homes)
            for a in range(2):
                for b in range(cells):
                    for c in range(homes):
                        spot = ((place[0] ^ a) * cells + (place[1] ^ b)) * homes + (place[2] ^ c)
                        at = (b * homes + c) * rows
                        whole_ref[pl.ds(pl.multiple_of(spot * rows, 8), rows), :] = sources[a][at : at + rows, :]
    ni, nh, spare = s.inner // LANES, s.hidden // LANES, s.hidden % LANES
    w = s.width

    def tile(ref, n):
        return ref[n * w : (n + 1) * w, :]

    joint, out_t, hid, ret_t, ob, sg, sb, rb, hb, tissue, fg, fb = outs
    for n in range(ni):
        joint[:, n * LANES : (n + 1) * LANES] = tile(early, n)
        out_t[:, n * LANES : (n + 1) * LANES] = tile(early, ni + n)
    for n in range(2 * ni):
        joint[:, (ni + n) * LANES : (ni + n + 1) * LANES] = tile(late, n)
    for n in range(nh):
        ret_t[:, n * LANES : (n + 1) * LANES] = tile(early, 2 * ni + n)
        hid[:, n * LANES : (n + 1) * LANES] = tile(early, 2 * ni + nh + n)
    mixed = tile(early, 2 * ni + 2 * nh)
    ret_t[:, nh * LANES :] = mixed[:, :spare]
    hid[:, nh * LANES :] = mixed[:, spare : 2 * spare]
    columns = mixed.T
    at = 2 * spare
    for ref in (ob, sg, sb, rb):
        ref[...] = columns[at : at + 1, :]
        at += 1
    hb[...] = columns[at : at + s.hidden // w, :]
    columns = tile(late, 2 * ni).T
    fg[...] = columns[0:1, :]
    fb[...] = columns[1:2, :]
    tissue[...] = columns[2 : 2 + tissues, :]


def finish(s, sizes, tissues, place, early, late):
    w = s.width
    row = array(1, w)
    out = [array(w, 3 * s.inner), array(w, s.inner), array(w, s.hidden), array(w, s.hidden)]
    out += [row, row, row, row, array(s.hidden // w, w), array(tissues, w), row, row]
    doubled = 1 if sizes is None else 2
    scratch = [pltpu.VMEM((doubled * b[0].shape[0], LANES), f32) for b in (early, late)]
    body = functools.partial(finish_body, s, sizes, tissues)
    return call("finish", body, [place, *early, *late], out, scratch, 8, 1, flops=3e9)


def solution(mesh):
    def run(inputs, lengths, *others):
        cells_axis, genes_axis = mesh.shape["cells"], mesh.shape["genes"]
        homes = inputs.shape[0] // cells_axis
        rest = genes_axis // homes
        sizes = {"cells": cells_axis, "home": homes, "rest": rest}
        fine = Mesh(mesh.devices.reshape(cells_axis, homes, rest), ("cells", "home", "rest"))
        tokens = P("cells", ("home", "rest"), None)
        return jax.shard_map(
            lambda *args: local(sizes, *args),
            mesh=fine,
            in_specs=(tokens, P("cells"), P("cells")) + (P(),) * 13 + (tokens,),
            out_specs=(tokens, tokens) + (P(),) * 12,
            check_vma=False,
        )(inputs, lengths, *others)

    return run


def after(value, *others):
    return lax.optimization_barrier((value, *others))[0]


def local(
    sizes,
    inputs,
    lengths,
    tissue_ids,
    tissue_table,
    first_gain,
    first_bias,
    joint_weight,
    feature_draws,
    output_weight,
    output_bias,
    second_gain,
    second_bias,
    hidden_weight,
    hidden_bias,
    return_weight,
    return_bias,
    cotangent,
):
    s = Sizes(sizes, inputs, feature_draws, hidden_weight)
    homes, rest, cells = s.homes, s.rest, sizes["cells"]
    parts = cells * homes * rest
    home = lax.axis_index("home").astype(jnp.int32)
    side = lax.axis_index("rest").astype(jnp.int32)
    half_side = side % 2
    cell = lax.axis_index("cells").astype(jnp.int32)
    paired = rest == 2

    def pick(array, k):
        return lax.dynamic_index_in_dim(array, home ^ k, 0, False)

    inputs_t = inputs.transpose(0, 2, 1)
    cot_t = cotangent.transpose(0, 2, 1)
    mine = [pick(inputs_t, k) for k in range(homes)]
    arrived = send(mine, "home", homes)
    my_cots = [pick(cot_t, k).astype(f32) for k in range(homes)]
    tissue = pick(tissue_ids, 0)
    starts = [(((home ^ k) * rest + side) * s.genes) for k in range(homes)]
    place = jnp.stack(starts + [pick(lengths, 0), tissue, half_side]).astype(jnp.int32)
    rows = (first_gain, first_bias, output_bias, second_gain, second_bias, return_bias)
    joint_t, draws, draws_t, out_wt, out_w, hid_w, hid_wt, ret_wt, ret_w, joint, cols, bias = prepare(
        s,
        tissue,
        joint_weight,
        feature_draws.transpose(0, 2, 1),
        output_weight.T,
        hidden_weight,
        return_weight.T,
        hidden_bias,
        rows,
        tissue_table,
    )
    state = run_keys(s, 0, 1, place, mine[:1], cols, joint_t, draws)
    late_cots = [my_cots[0]] + [after(c, *arrived) for c in my_cots[1:]]
    arrived_cot = my_cots[:1] + send(late_cots, "home", homes)
    if homes > 1:
        state = run_keys(s, 1, homes - 1, place, arrived, cols, joint_t, draws, state)
    kv, shifted, qkv = state

    def other(value):
        return lax.ppermute(value, "rest", partners(2, 1))

    if paired:
        kv_other = other(after(kv, arrived_cot[1]))
    else:
        last_row = (jnp.arange(s.rows) == s.rows - 1)[None, :, None]
        if rest > 2:
            peak = kv[:, -1:, :]
            top = lax.pmax(peak, "rest")
            kv = lax.psum(kv * jnp.exp(peak - top), "rest")
            kv = jnp.where(last_row, top, kv)
        kv_other = jnp.where(last_row, LOWEST, jnp.zeros_like(kv))
    weights = (cols, bias, draws, draws_t, out_w, out_wt, hid_w, hid_wt, ret_w, ret_wt, joint)
    groups = (homes // 2, homes - homes // 2) if homes > 1 else (homes,)
    out_blocks, middle_grad, query_part, made = run_middle(
        s, parts, half_side, groups, kv, kv_other, shifted, qkv, arrived_cot, weights
    )
    vg, early_keep, early_send = made
    vg_other = other(vg) if paired else jnp.zeros_like(vg)
    if rest > 2:
        vg = lax.psum(vg, "rest")
    made = run_last(
        s,
        parts,
        groups,
        place,
        vg,
        vg_other,
        kv,
        kv_other,
        shifted,
        qkv,
        middle_grad,
        query_part,
        (cols, draws, draws_t, joint),
    )
    grad_blocks, late_keep, late_send = made[:homes], made[homes], made[homes + 1]

    def return_home(own, received):
        return place_blocks(s, home, [own] + received).transpose(0, 2, 1)

    out_received = send(out_blocks, "home", homes)
    grad_received = send(grad_blocks, "home", homes)

    if paired and cells in (2, 4) and homes in (2, 4):

        def spread(pieces, axis, size):
            return [pieces[0]] + send(pieces, axis, size)

        def repeated(piece, axis, size):
            return [piece] + send([piece] * size, axis, size)

        early = spread(add_split(cell, [early_keep, other(early_send)], cells), "cells", cells)
        outputs = return_home(out_blocks[0], out_received)
        late_send = after(late_send, *out_received, *early[1:])
        made = add_split(cell, [late_keep, other(late_send)], cells)
        late = spread(made, "cells", cells)
        early[0] = after(early[0], made[0])
        early = spread(add_split(home, early, homes), "home", homes)
        late[0] = after(late[0], outputs)
        made = add_split(home, late, homes)
        late = spread(made, "home", homes)
        early[0] = after(early[0], made[0])
        early = repeated(add_split(home, early, 1)[0], "home", homes)
        made = add_split(home, late, 1)[0]
        late = repeated(made, "home", homes)
        early[0] = after(early[0], made)
        early = repeated(stack_rows(early), "cells", cells)
        late[0] = after(late[0], *grad_received)
        made = stack_rows(late)
        late = repeated(made, "cells", cells)
        early[0] = after(early[0], made)
        early = stack_rows(early)
        late = stack_rows(late)
        early, late = (early, other(early)), (late, other(late))
        order = (cells, homes)
    else:
        axes = ("rest", "cells", "home")

        def summed(keep, sent):
            swap = half_side == 1
            whole_sum = jnp.where(swap, jnp.concatenate([sent, keep]), jnp.concatenate([keep, sent]))
            total = lax.psum(whole_sum, axes)
            return total, total

        outputs = return_home(out_blocks[0], out_received)
        early, late, order = summed(early_keep, early_send), summed(late_keep, late_send), None
    joint_grad, out_t, hid, ret_t, ob, sg, sb, rb, hb, tissue_grad, fg, fb = finish(
        s, order, tissue_table.shape[0], jnp.stack([side, cell, home]), early, late
    )
    return (
        outputs,
        return_home(grad_blocks[0], grad_received),
        tissue_grad,
        fg[0],
        fb[0],
        joint_grad,
        out_t.T,
        ob[0],
        sg[0],
        sb[0],
        hid,
        hb.reshape(-1),
        ret_t.T,
        rb[0],
    )
```

```python
import functools

import jax
import jax.numpy as jnp
from jax import lax
from jax.experimental import pallas as pl
from jax.experimental.pallas import tpu as pltpu
from jax.sharding import Mesh
from jax.sharding import PartitionSpec as P

EPSILON = 1e-05
LOWEST = -1e30
bf16 = jnp.bfloat16
f32 = jnp.float32
LANES = 128


def dot(left, right):
    return jnp.dot(left, right, preferred_element_type=f32)


def dot_lanes(left, right):
    return lax.dot_general(left, right, (((1,), (1,)), ((), ())), preferred_element_type=f32)


def norm_rows(values):
    centered = values - jnp.mean(values, 0, keepdims=True)
    inverse = lax.rsqrt(jnp.mean(centered * centered, 0, keepdims=True) + EPSILON)
    return centered * inverse, inverse


def norm_back_rows(upstream, normed, inverse, gain):
    scaled = upstream * gain
    return inverse * (
        scaled
        - jnp.mean(scaled, 0, keepdims=True)
        - normed * jnp.mean(scaled * normed, 0, keepdims=True)
    )


def fold(values):
    total = values[:, :LANES]
    for at in range(LANES, values.shape[1], LANES):
        total = total + values[:, at : at + LANES]
    return total


def split_low(values):
    high = values.astype(bf16)
    return high, (values - high.astype(f32)).astype(bf16)


def lane_index(shape):
    return lax.broadcasted_iota(jnp.int32, shape, len(shape) - 1)


def row_index(shape):
    return lax.broadcasted_iota(jnp.int32, shape, len(shape) - 2)


class Sizes:
    def __init__(self, mesh_sizes, inputs, feature_draws, hidden_weight):
        self.homes, self.rest = mesh_sizes["home"], mesh_sizes["rest"]
        _, self.genes, self.width = inputs.shape
        self.heads, self.feats, self.head = feature_draws.shape
        self.inner = self.heads * self.head
        self.hidden = hidden_weight.shape[1]
        self.rows = -(-self.feats // 16) * 16
        self.ext = self.head + 16
        self.scale = self.head ** (-0.25)


FIRST_MB, FINAL_MB, LAST_MB = 13, 15, 12
VMEM = pl.BlockSpec(memory_space=pltpu.VMEM)
SMEM = pl.BlockSpec(memory_space=pltpu.SMEM)


def call(name, body, args, out, scratch=(), megabytes=4, smem=0, aliases={}, flops=0):
    return pl.pallas_call(
        body,
        out_shape=out,
        in_specs=[SMEM] * smem + [VMEM] * (len(args) - smem),
        out_specs=jax.tree.map(lambda _: VMEM, out),
        scratch_shapes=list(scratch),
        input_output_aliases=aliases,
        compiler_params=pltpu.CompilerParams(vmem_limit_bytes=megabytes * 1024 * 1024),
        cost_estimate=pl.CostEstimate(flops=int(flops), bytes_accessed=1024, transcendentals=0),
        name=name,
    )(*args)


def array(*shape, dtype=f32):
    return jax.ShapeDtypeStruct(shape, dtype)


def prepare_body(s, place, joint, draws, out_t, hid, ret_t, hidden_bias, *refs):
    rows, table = refs[:6], refs[6]
    joint_t, draws_low, draws_t, out_wt, out_w, hid_w, hid_wt, ret_wt, ret_w, joint_w, cols, bias = refs[7:]
    joint_w[...] = joint[...].astype(bf16)
    joint_t[...] = joint[...].T.astype(bf16)
    for h in range(s.heads):
        draw = draws[h]
        filler = jnp.broadcast_to(draw[:, :1], (s.head, s.rows - s.feats))
        draws_low[h] = jnp.concatenate([draw, filler], 1).T.astype(bf16)
        draws_t[h] = jnp.concatenate([draw, jnp.zeros_like(filler)], 1).astype(bf16)
    out_wt[...] = out_t[...].astype(bf16)
    out_w[...] = out_t[...].T.astype(bf16)
    hid_w[...] = hid[...].astype(bf16)
    hid_wt[...] = hid[...].T.astype(bf16)
    ret_wt[...] = ret_t[...].astype(bf16)
    ret_w[...] = ret_t[...].T.astype(bf16)
    stacked = [r[...] for r in rows] + [table[pl.ds(place[s.homes + 1], 1), :]]
    stacked += [jnp.zeros((1, s.width), f32)]
    cols[...] = jnp.concatenate(stacked, 0).T
    bias[...] = jnp.broadcast_to(hidden_bias[...], (8, s.hidden)).T


def prepare(s, place, joint, draws, out_t, hid, ret_t, hidden_bias, rows, table):
    w, i, f = s.width, s.inner, s.hidden
    out = [
        array(3 * i, w, dtype=bf16),
        array(s.heads, s.rows, s.head, dtype=bf16),
        array(s.heads, s.head, s.rows, dtype=bf16),
        array(w, i, dtype=bf16),
        array(i, w, dtype=bf16),
        array(w, f, dtype=bf16),
        array(f, w, dtype=bf16),
        array(w, f, dtype=bf16),
        array(f, w, dtype=bf16),
        array(w, 3 * i, dtype=bf16),
        array(w, 8),
        array(f, 8),
    ]
    args = [place, joint, draws, out_t, hid, ret_t, hidden_bias[None], *[r[None] for r in rows], table]
    return call("prepare", functools.partial(prepare_body, s), args, out, smem=1, megabytes=8, flops=4e9)


def keys_body(s, base, count, fresh, *refs):
    refs = list(refs)
    place = refs.pop(0)
    xs = [refs.pop(0) for _ in range(count)]
    cols, joint_t, draws = (refs.pop(0) for _ in range(3))
    if not fresh:
        kv_prev = refs.pop(0)
        refs.pop(0), refs.pop(0)
    kv, shifted, qkv, ext, dashes, tops, cuts = refs
    scale = s.scale
    last_row = s.rows - 1
    tail = (s.heads, LANES - s.head, s.genes)
    ext[:, s.head :, :] = jnp.where(row_index(tail) == 0, 1.0, 0.0).astype(bf16)
    if fresh:
        state = jnp.full((16, 1), LOWEST, f32)
    else:
        state = jnp.concatenate([kv_prev[h, last_row:, 0:1] for h in range(s.heads)] + [jnp.full((16 - s.heads, 1), LOWEST, f32)], 0)
    for n in range(count):
        x = xs[n][...] + cols[:, 6:7]
        shifted[base + n] = x
        normed, _ = norm_rows(x)
        first = (normed * cols[:, 0:1] + cols[:, 1:2]).astype(bf16)
        for part in (1, 2, 0):
            rows = slice(part * s.inner, (part + 1) * s.inner)
            made = dot(joint_t[rows, :], first).astype(bf16)
            qkv[base + n, rows, :] = made
            if part == 2:
                for h in range(s.heads):
                    ext[h, : s.head, :] = made[h * s.head : (h + 1) * s.head]
        for h in range(s.heads):
            key = qkv[base + n, s.inner + h * s.head : s.inner + (h + 1) * s.head, :]
            dash = dot(draws[h], key)
            dashes[h] = dash
            key_f = key.astype(f32)
            cuts[h : h + 1, :] = jnp.sum(key_f * key_f, 0, keepdims=True) * (scale * scale * 0.5)
            tops[h : h + 1, :] = jnp.max(dash, 0, keepdims=True) * scale
        valid = place[base + n] + lane_index((1, s.genes)) < place[s.homes]
        new = jnp.maximum(state, jnp.max(jnp.where(valid, tops[...], LOWEST), 1, keepdims=True))
        decay = jnp.exp(state - new)
        state = new
        lifts = jnp.where(valid, cuts[...] + new, 1e30)
        for h in range(s.heads):
            feats = jnp.exp(scale * dashes[h] - lifts[h : h + 1]).astype(bf16)
            part = dot_lanes(feats, ext[h])
            if n == 0 and fresh:
                kv[h] = part
            else:
                kv[h] = (kv_prev if n == 0 else kv)[h] * decay[h : h + 1] + part
    for h in range(s.heads):
        kv[h, last_row:, :] = jnp.broadcast_to(state[h : h + 1], (1, LANES))


def run_keys(s, base, count, place, xs, cols, joint_t, draws, before=None):
    out = [
        array(s.heads, s.rows, LANES),
        array(s.homes, s.width, s.genes),
        array(s.homes, 3 * s.inner, s.genes, dtype=bf16),
    ]
    args = [place, *xs, cols, joint_t, draws]
    aliases = {}
    if before is not None:
        aliases = {len(args) + 1: 1, len(args) + 2: 2}
        args += list(before)
    scratch = [
        pltpu.VMEM((s.heads, LANES, s.genes), bf16),
        pltpu.VMEM((s.heads, s.rows, s.genes), f32),
        pltpu.VMEM((16, s.genes), f32),
        pltpu.VMEM((16, s.genes), f32),
    ]
    body = functools.partial(keys_body, s, base, count, before is None)
    return call("keys", body, args, out, scratch, 10, 1, aliases, 3e9 * count)


def merged(own, other, kept_rows, kept_lanes):
    last = own.shape[0] - 1
    own_peak, other_peak = own[last:, 0:1], other[last:, 0:1]
    peak = jnp.maximum(own_peak, other_peak)
    total = own * jnp.exp(own_peak - peak) + other * jnp.exp(other_peak - peak)
    inside = (row_index(own.shape) < kept_rows) & (lane_index(own.shape) < kept_lanes)
    return jnp.where(inside, total, 0.0), peak


def eye_like(size):
    return (row_index((size, size)) == lane_index((size, size))).astype(f32).astype(bf16)


def middle_body(s, base, count, first, final, *refs):
    refs = list(refs)

    def take(n):
        taken = refs[:n]
        del refs[:n]
        return taken

    (place,) = take(1)
    before = take(2) if first else take(9)
    shifted, qkv = take(2)
    cots = take(count)
    cols, hidden_bias, draws, draws_t, out_w, out_wt = take(6)
    hid_w, hid_wt, ret_w, ret_wt, joint = take(5)
    outputs, middle_grad, query_part = take(3)
    results = take(3) if final else take(9)
    if first:
        kv3, kv_t = take(2) if final else results[:2]
    else:
        kv3, kv_t = before[:2]
    feats, att, att_low, over, att_grad, query_grad = take(6)
    cot_all, acts, pre_grads = take(3)
    sums = refs if final else results[2:]
    acc_q, acc_o, acc_r, acc_h, acc_cols, acc_hb, values_grad = sums
    scale = s.scale
    ext = s.ext
    if first:
        kv_own, kv_other = before
        eye = eye_like(2 * ext)
        for h in range(s.heads):
            total, _ = merged(kv_own[h], kv_other[h], s.feats, s.head + 1)
            high, low = split_low(total[:, :ext])
            kv3[h] = jnp.concatenate([high, low, high], 1)
            kv_t[h] = dot_lanes(eye, jnp.concatenate([high, low], 1)).astype(bf16)
        for acc in sums:
            acc[...] = jnp.zeros_like(acc)
    else:
        for acc, was in zip(sums, before[2:]):
            acc[...] = was[...]
    for n in range(count):
        cot_all[n] = cots[n][...]

    def block(j, carry):
        def attend(h):
            rows = slice(h * s.head, (h + 1) * s.head)
            query = qkv[base + j, rows, :]
            query_f = query.astype(f32)
            cut = jnp.sum(query_f * query_f, 0, keepdims=True) * (scale * scale * 0.5)
            value = jnp.exp(scale * dot(draws[h], query) - cut)
            feats[h] = value
            both = dot(kv_t[h], value.astype(bf16))
            total = both[:ext] + both[ext:]
            inverse = 1.0 / total[s.head : s.head + 1]
            over[h : h + 1, :] = inverse
            result = total[: s.head] * inverse
            att[rows, :] = result
            att_low[rows, :] = result.astype(bf16)

        for h in range(s.heads):
            attend(h)

        x = shifted[base + j]
        middle = x + dot(out_wt[...], att_low[...]) + cols[:, 2:3]
        normed, inverse = norm_rows(middle)
        gain = cols[:, 3:4]
        second = (normed * gain + cols[:, 4:5]).astype(bf16)
        cot = cot_all[j]
        cot_low = cot.astype(bf16)
        result = middle + cols[:, 5:6]
        step = s.hidden // 2
        for at in range(0, s.hidden, step):
            part = slice(at, at + step)
            pre = dot(hid_wt[part, :], second) + hidden_bias[part, 0:1]
            cumulative = 0.5 * (1.0 + lax.erf(pre * 0.7071067811865476))
            acts[part, :] = (pre * cumulative).astype(bf16)
            slope = cumulative + pre * (jnp.exp(-0.5 * pre * pre) * 0.3989422804014327)
            pre_low = (dot(ret_w[part, :], cot_low) * slope).astype(bf16)
            pre_grads[part, :] = pre_low
            acc_hb[part, :] += fold(pre_low.astype(f32))
        outputs[j] = result + dot(ret_wt[...], acts[...])
        acc_r[...] += dot_lanes(cot_low, acts[...])
        acc_h[...] += dot_lanes(second, pre_grads[...])
        second_grad = dot(hid_w[...], pre_grads[...])
        grad = cot + norm_back_rows(second_grad, normed, inverse, gain)
        middle_grad[j] = grad
        branch = grad.astype(bf16)
        acc_cols[0] += fold(branch.astype(f32))
        acc_cols[1] += fold(second_grad * normed)
        acc_cols[2] += fold(second_grad)
        acc_cols[3] += fold(cot)
        acc_o[...] += dot_lanes(branch, att_low[...])
        att_grad[...] = dot(out_w[...], branch)

        def back(h):
            rows = slice(h * s.head, (h + 1) * s.head)
            upstream = att_grad[rows, :]
            inverse = over[h : h + 1, :]
            numer = upstream * inverse
            denom = -jnp.sum(upstream * att[rows, :], 0, keepdims=True) * inverse
            tail_shape = (ext - s.head, s.genes)
            tail = jnp.where(row_index(tail_shape) == 0, denom, 0.0)
            high, low = split_low(jnp.concatenate([numer, tail], 0))
            value = feats[h]
            gap = jnp.zeros((LANES - ext, s.genes), bf16)
            sums = dot_lanes(value.astype(bf16), jnp.concatenate([high, gap, low, gap], 0))
            values_grad[h] += sums[:, :LANES] + sums[:, LANES:]
            back_feats = dot(kv3[h], jnp.concatenate([high, high, low], 0)) * value
            query = qkv[base + j, rows, :].astype(f32)
            total = jnp.sum(back_feats, 0, keepdims=True)
            result = scale * dot(draws_t[h], back_feats.astype(bf16)) - query * (total * (scale * scale))
            query_grad[rows, :] = result.astype(bf16)

        for h in range(s.heads):
            back(h)
        normal = (norm_rows(x)[0] * cols[:, 0:1] + cols[:, 1:2]).astype(bf16)
        acc_q[...] += dot_lanes(normal, query_grad[...])
        query_part[j] = dot(joint[:, : s.inner], query_grad[...])
        return carry

    lax.fori_loop(0, count, block, 0)
    if not final:
        if not first:
            results[0][...], results[1][...] = kv3[...], kv_t[...]
        return
    results[0][...] = values_grad[...]
    keep, send = results[1:]
    spare = s.hidden % LANES
    lane = lane_index((s.width, LANES))
    last = jnp.zeros((s.width, LANES), f32)
    spot = 2 * spare
    for n in range(4):
        last = jnp.where(lane == spot, jnp.sum(acc_cols[n], 1, keepdims=True), last)
        spot += 1
    for n in range(s.hidden // s.width):
        piece = acc_hb[n * s.width : (n + 1) * s.width, :]
        last = jnp.where(lane == spot, jnp.sum(piece, 1, keepdims=True), last)
        spot += 1
    if spare:
        tops = [acc[:, s.hidden - spare :] for acc in (acc_r, acc_h)]
        last = jnp.concatenate(tops + [last[:, 2 * spare :]], 1)
    tiles = []
    for acc in (acc_q, acc_o, acc_r, acc_h):
        tiles += [(acc, n * LANES) for n in range(acc.shape[1] // LANES)]
    deal_tiles(place[s.homes + 2], s.width, keep, send, tiles, last)


def deal_tiles(side, width, keep, send, tiles, last):
    half = keep.shape[0]

    def put(row, value):
        for part in (0, 1):
            begin, end = max(row, part * half), min(row + value.shape[0], (part + 1) * half)
            if begin < end:
                piece = value[begin - row : end - row]
                spots = slice(begin - part * half, end - part * half)
                if send is None:
                    keep[spots, :] = piece
                    continue

                @pl.when(side == part)
                def _():
                    keep[spots, :] = piece

                @pl.when(side != part)
                def _():
                    send[spots, :] = piece

    row = 0
    for acc, at in tiles:
        put(row, acc[:, at : at + LANES])
        row += width
    put(row, last)
    row += width
    total = half if send is None else 2 * half
    if row < total:
        put(row, jnp.zeros((total - row, LANES), f32))


def padded(rows, parts):
    return -(-rows // (8 * parts)) * 8 * parts


def halves(s, tiles, parts):
    rows = padded(tiles * s.width, parts)
    return [array(rows // 2, LANES), array(rows // 2, LANES)]


def run_middle(s, parts, place, groups, kv_own, kv_other, shifted, qkv, cots, weights):
    sums = [
        array(s.width, s.inner),
        array(s.width, s.inner),
        array(s.width, s.hidden),
        array(s.width, s.hidden),
        array(4, s.width, LANES),
        array(s.hidden, LANES),
        array(s.heads, s.rows, LANES),
    ]
    forms = [
        array(s.heads, s.rows, 3 * s.ext, dtype=bf16),
        array(s.heads, 2 * s.ext, s.rows, dtype=bf16),
    ]
    ends = [array(s.heads, s.rows, LANES)]
    ends += halves(s, 2 * (s.inner // LANES) + 2 * (s.hidden // LANES) + 1, parts)
    before, base = [kv_own, kv_other], 0
    outputs, middle_grad, query_part = [], [], []
    for index, count in enumerate(groups):
        first, final = index == 0, index == len(groups) - 1
        tokens = array(count, s.width, s.genes)
        out = [tokens, tokens, tokens]
        out += ends if final else forms + sums
        scratch = list(forms) if first and final else []
        scratch += [
            array(s.heads, s.rows, s.genes),
            array(s.inner, s.genes),
            array(s.inner, s.genes, dtype=bf16),
            array(16, s.genes),
            array(s.inner, s.genes),
            array(s.inner, s.genes, dtype=bf16),
            tokens,
            array(s.hidden, s.genes, dtype=bf16),
            array(s.hidden, s.genes, dtype=bf16),
        ]
        scratch += sums if final else []
        scratch = [pltpu.VMEM(a.shape, a.dtype) for a in scratch]
        args = [place, *before, shifted, qkv, *cots[base : base + count], *weights]
        body = functools.partial(middle_body, s, base, count, first, final)
        made = call("middle", body, args, out, scratch, FINAL_MB if final else FIRST_MB, 1, flops=7e9 * count)
        outputs.append(made[0])
        middle_grad.append(made[1])
        query_part.append(made[2])
        before, base = made[3:], base + count
    return outputs, middle_grad, query_part, before


def last_body(s, groups, *refs):
    refs = list(refs)
    place, vg_own, vg_other, kv_own, kv_other, shifted, qkv = (refs.pop(0) for _ in range(7))
    middle_grads = [refs.pop(0) for _ in groups]
    query_parts = [refs.pop(0) for _ in groups]
    cols, draws, draws_t, joint = (refs.pop(0) for _ in range(4))
    input_grad = [refs.pop(0) for _ in range(s.homes)]
    keep, send, vg2, vg_t, ext2, grads, result_all, acc, acc_cols = refs
    scale = s.scale
    ext = s.ext
    eye = eye_like(ext)
    peaks = []
    for h in range(s.heads):
        total = vg_own[h] + vg_other[h]
        inside = row_index(total.shape) < s.feats
        high, low = split_low(jnp.where(inside, total, 0.0)[:, :ext])
        vg2[h] = jnp.concatenate([high, low], 1)
        vg_t[h] = dot_lanes(eye, high)[: s.head].astype(bf16)
        peaks.append(jnp.maximum(kv_own[h, s.rows - 1 :, 0:1], kv_other[h, s.rows - 1 :, 0:1]))
    tail = (s.heads, ext - s.head, s.genes)
    ones = jnp.where(row_index(tail) == 0, 1.0, 0.0).astype(bf16)
    ext2[:, s.head : ext, :] = ones
    ext2[:, ext + s.head :, :] = ones
    acc[...] = jnp.zeros_like(acc)
    acc_cols[...] = jnp.zeros_like(acc_cols)

    def block(base, middle_grad, query_part, i, carry):
        j = base + i
        valid = place[j] + lane_index((1, s.genes)) < place[s.homes]

        def head(h):
            rows = slice(h * s.head, (h + 1) * s.head)
            key = qkv[j, s.inner + h * s.head : s.inner + (h + 1) * s.head, :]
            value = qkv[j, 2 * s.inner + h * s.head : 2 * s.inner + (h + 1) * s.head, :]
            ext2[h, : s.head, :] = value
            ext2[h, ext : ext + s.head, :] = value
            key_f = key.astype(f32)
            cut = jnp.sum(key_f * key_f, 0, keepdims=True) * (scale * scale * 0.5)
            cut = jnp.where(valid, cut + peaks[h], 1e30)
            feats = jnp.exp(scale * dot(draws[h], key) - cut)
            back_feats = dot(vg2[h], ext2[h]) * feats
            total = jnp.sum(back_feats, 0, keepdims=True)
            result = scale * dot(draws_t[h], back_feats.astype(bf16)) - key_f * (total * (scale * scale))
            grads[rows, :] = result.astype(bf16)
            result = dot(vg_t[h], feats.astype(bf16))
            grads[s.inner + h * s.head : s.inner + (h + 1) * s.head, :] = result.astype(bf16)

        for h in range(s.heads):
            head(h)
        normed, inverse = norm_rows(shifted[j])
        gain = cols[:, 0:1]
        first = (normed * gain + cols[:, 1:2]).astype(bf16)
        acc[...] += dot_lanes(first, grads[...])
        first_grad = query_part[i] + dot(joint[:, s.inner :], grads[...])
        result = middle_grad[i] + norm_back_rows(first_grad, normed, inverse, gain)
        result_all[j] = result
        acc_cols[0] += fold(first_grad * normed)
        acc_cols[1] += fold(first_grad)
        acc_cols[2] += fold(result)
        return carry

    base = 0
    for n, count in enumerate(groups):
        lax.fori_loop(0, count, functools.partial(block, base, middle_grads[n], query_parts[n]), 0)
        base += count
    for n in range(s.homes):
        input_grad[n][...] = result_all[n]
    lane = lane_index((s.width, LANES))
    sums = [jnp.sum(acc_cols[n], 1, keepdims=True) for n in range(3)]
    last = jnp.where(lane == 0, sums[0], jnp.where(lane == 1, sums[1], 0.0))
    last = jnp.where(lane == 2 + place[s.homes + 1], sums[2], last)
    tiles = [(acc, n * LANES) for n in range(acc.shape[1] // LANES)]
    deal_tiles(place[s.homes + 2], s.width, keep, send, tiles, last)


def run_last(s, parts, groups, place, vg_own, vg_other, kv_own, kv_other, shifted, qkv, middle_grad, query_part, weights):
    out = [array(s.width, s.genes)] * s.homes + halves(s, 2 * (s.inner // LANES) + 1, parts)
    scratch = [
        pltpu.VMEM((s.heads, s.rows, 2 * s.ext), bf16),
        pltpu.VMEM((s.heads, s.head, s.rows), bf16),
        pltpu.VMEM((s.heads, 2 * s.ext, s.genes), bf16),
        pltpu.VMEM((2 * s.inner, s.genes), bf16),
        pltpu.VMEM((s.homes, s.width, s.genes), f32),
        pltpu.VMEM((s.width, 2 * s.inner), f32),
        pltpu.VMEM((3, s.width, LANES), f32),
    ]
    args = [place, vg_own, vg_other, kv_own, kv_other, shifted, qkv, *middle_grad, *query_part, *weights]
    return call("last", functools.partial(last_body, s, groups), args, out, scratch, LAST_MB, 1, flops=15e9)


def partners(size, step):
    return [(i, i ^ step) for i in range(size)]


def send(values, axis, size):
    return [lax.ppermute(values[k], axis, partners(size, k)) for k in range(1, size)]


def add_split(place, spot, terms, parts):
    rows = terms[0].shape[0] // parts

    def body(numbers, *refs):
        ins, outs = refs[: len(terms)], refs[len(terms) :]
        for k in range(parts):
            at = pl.multiple_of((numbers[spot] ^ k) * rows, 8) if parts > 1 else 0
            total = ins[0][pl.ds(at, rows), :]
            for other in ins[1:]:
                total = total + other[pl.ds(at, rows), :]
            outs[k][...] = total

    out = [array(rows, LANES)] * parts
    return call("add_split", body, [place, *terms], out, smem=1, flops=1e9)


def meet(place, spot, early, late, parts):
    first, second = early[0].shape[0] // parts, late[0].shape[0] // parts

    def body(numbers, *refs):
        outs = refs[len(early) + len(late) :]
        for terms, rows, begin in ((refs[: len(early)], first, 0), (refs[len(early) : -parts], second, first)):
            for k in range(parts):
                at = pl.multiple_of((numbers[spot] ^ k) * rows, 8)
                total = terms[0][pl.ds(at, rows), :]
                for other in terms[1:]:
                    total = total + other[pl.ds(at, rows), :]
                outs[k][begin : begin + rows, :] = total

    out = [array(first + second, LANES)] * parts
    return call("meet", body, [place, *early, *late], out, smem=1, flops=1e9)


def stack_rows(pieces):
    def body(*refs):
        at = 0
        for ref in refs[:-1]:
            refs[-1][at : at + ref.shape[0], :] = ref[...]
            at += ref.shape[0]

    return call("stack", body, pieces, array(sum(p.shape[0] for p in pieces), LANES), flops=1e9)


def forward_pair(near, far):
    def body(near_ref, far_ref, out):
        out[0] = near_ref[1]
        out[1] = far_ref[1]

    return call("forward_pair", body, [near, far], array(*near.shape), flops=1e9)


def place_blocks(s, place, near, far, last):
    def body(numbers, near_ref, far_ref, last_ref, out):
        home = numbers[s.homes + 4]
        out[home] = near_ref[0]
        out[home ^ 1] = last_ref[0]
        out[home ^ 2] = far_ref[0]
        out[home ^ 3] = last_ref[1]

    out = array(s.homes, s.width, s.genes)
    made = call("place_blocks", body, [place, near, far, last], out, smem=1, flops=1e9)
    return made.transpose(0, 2, 1)


def place_apart(s, place, blocks):
    def body(numbers, *refs):
        for k in range(s.homes):
            refs[-1][numbers[s.homes + 4] ^ k] = refs[k][...]

    out = array(s.homes, s.width, s.genes)
    made = call("place_apart", body, [place, *blocks], out, smem=1, flops=1e9)
    return made.transpose(0, 2, 1)


def finish_body(s, split, tissues, rows, place, own, other, *refs):
    early, late = refs[-2:]
    joint, out_t, hid, ret_t, ob, sg, sb, rb, hb, tissue, fg, fb = refs[:-2]
    first, second = rows
    if split:
        side, cell, home = (place[s.homes + n] for n in (2, 3, 4))
        for core in range(2):
            source = (own, other)[core]
            for at in range(16):
                spot = ((side ^ core) * 4 + (cell ^ (at // 4))) * 4 + (home ^ (at % 4))
                begin = at * (first + second)
                early[pl.ds(pl.multiple_of(spot * first, 8), first), :] = source[begin : begin + first, :]
                late[pl.ds(pl.multiple_of(spot * second, 8), second), :] = source[begin + first : begin + first + second, :]
    else:
        early[...] = own[...]
        late[...] = other[...]
    ni, nh, spare = s.inner // LANES, s.hidden // LANES, s.hidden % LANES
    w = s.width

    def tile(ref, n):
        return ref[n * w : (n + 1) * w, :]

    for n in range(ni):
        joint[:, n * LANES : (n + 1) * LANES] = tile(early, n)
        out_t[:, n * LANES : (n + 1) * LANES] = tile(early, ni + n)
    for n in range(2 * ni):
        joint[:, (ni + n) * LANES : (ni + n + 1) * LANES] = tile(late, n)
    for n in range(nh):
        ret_t[:, n * LANES : (n + 1) * LANES] = tile(early, 2 * ni + n)
        hid[:, n * LANES : (n + 1) * LANES] = tile(early, 2 * ni + nh + n)
    mixed = tile(early, 2 * ni + 2 * nh)
    if spare:
        ret_t[:, nh * LANES :] = mixed[:, :spare]
        hid[:, nh * LANES :] = mixed[:, spare : 2 * spare]
    columns = mixed.T
    at = 2 * spare
    for ref in (ob, sg, sb, rb):
        ref[...] = columns[at : at + 1, :]
        at += 1
    hb[...] = columns[at : at + s.hidden // w, :]
    columns = tile(late, 2 * ni).T
    fg[...] = columns[0:1, :]
    fb[...] = columns[1:2, :]
    tissue[...] = columns[2 : 2 + tissues, :]


def finish(s, split, tissues, rows, place, own, other):
    w = s.width
    row = array(1, w)
    out = [array(w, 3 * s.inner), array(w, s.inner), array(w, s.hidden), array(w, s.hidden)]
    out += [row, row, row, row, array(s.hidden // w, w), array(tissues, w), row, row]
    scratch = [pltpu.VMEM((32 * n if split else ref.shape[0], LANES), f32) for n, ref in zip(rows, (own, other))]
    body = functools.partial(finish_body, s, split, tissues, rows)
    return call("finish", body, [place, own, other], out, scratch, 8, 1, flops=1e9)


def solution(mesh):
    def run(inputs, lengths, *others):
        cells_axis, genes_axis = mesh.shape["cells"], mesh.shape["genes"]
        homes = inputs.shape[0] // cells_axis
        rest = genes_axis // homes
        sizes = {"cells": cells_axis, "home": homes, "rest": rest}
        fine = Mesh(mesh.devices.reshape(cells_axis, homes, rest), ("cells", "home", "rest"))
        tokens = P("cells", ("home", "rest"), None)
        return jax.shard_map(
            lambda *args: local(sizes, *args),
            mesh=fine,
            in_specs=(tokens, P("cells"), P("cells")) + (P(),) * 13 + (tokens,),
            out_specs=(tokens, tokens) + (P(),) * 12,
            check_vma=False,
        )(inputs, lengths, *others)

    return run


def after(value, *others):
    return lax.optimization_barrier((value, *others))[0]


def local(
    sizes,
    inputs,
    lengths,
    tissue_ids,
    tissue_table,
    first_gain,
    first_bias,
    joint_weight,
    feature_draws,
    output_weight,
    output_bias,
    second_gain,
    second_bias,
    hidden_weight,
    hidden_bias,
    return_weight,
    return_bias,
    cotangent,
):
    s = Sizes(sizes, inputs, feature_draws, hidden_weight)
    homes, rest, cells = s.homes, s.rest, sizes["cells"]
    parts = cells * homes * rest
    home = lax.axis_index("home").astype(jnp.int32)
    side = lax.axis_index("rest").astype(jnp.int32)
    half_side = side % 2
    cell = lax.axis_index("cells").astype(jnp.int32)
    paired = rest == 2

    def pick(array, k):
        return lax.dynamic_index_in_dim(array, home ^ k, 0, False)

    tissue = pick(tissue_ids, 0)
    starts = [(((home ^ k) * rest + side) * s.genes) for k in range(homes)]
    place = jnp.stack(starts + [pick(lengths, 0), tissue, half_side, cell, home]).astype(jnp.int32)
    inputs_t = inputs.transpose(0, 2, 1)
    cot_t = cotangent.transpose(0, 2, 1)
    mine = [pick(inputs_t, k) for k in range(homes)]
    arrived = send(mine, "home", homes)
    my_cots = [pick(cot_t, k).astype(f32) for k in range(homes)]
    rows = (first_gain, first_bias, output_bias, second_gain, second_bias, return_bias)
    joint_t, draws, draws_t, out_wt, out_w, hid_w, hid_wt, ret_wt, ret_w, joint, cols, bias = prepare(
        s,
        place,
        joint_weight,
        feature_draws.transpose(0, 2, 1),
        output_weight.T,
        hidden_weight,
        return_weight.T,
        hidden_bias,
        rows,
        tissue_table,
    )
    state = run_keys(s, 0, 1, place, mine[:1], cols, joint_t, draws)
    late_cots = [my_cots[0]] + [after(c, *arrived) for c in my_cots[1:]]
    arrived_cot = my_cots[:1] + send(late_cots, "home", homes)
    if homes > 1:
        state = run_keys(s, 1, homes - 1, place, arrived, cols, joint_t, draws, state)
    kv, shifted, qkv = state

    def other(value):
        return lax.ppermute(value, "rest", partners(2, 1))

    if paired:
        kv_other = other(after(kv, arrived_cot[1]))
    else:
        last_row = (jnp.arange(s.rows) == s.rows - 1)[None, :, None]
        if rest > 2:
            peak = kv[:, -1:, :]
            top = lax.pmax(peak, "rest")
            kv = lax.psum(kv * jnp.exp(peak - top), "rest")
            kv = jnp.where(last_row, top, kv)
        kv_other = jnp.where(last_row, LOWEST, jnp.zeros_like(kv))
    weights = (cols, bias, draws, draws_t, out_w, out_wt, hid_w, hid_wt, ret_w, ret_wt, joint)
    groups = (2, 2)
    out_blocks, middle_grad, query_part, made = run_middle(
        s, parts, place, groups, kv, kv_other, shifted, qkv, arrived_cot, weights
    )
    vg, early_keep, early_send = made
    vg_other = other(vg) if paired else jnp.zeros_like(vg)
    if rest > 2:
        vg = lax.psum(vg, "rest")
    made = run_last(
        s,
        parts,
        groups,
        place,
        vg,
        vg_other,
        kv,
        kv_other,
        shifted,
        qkv,
        middle_grad,
        query_part,
        (cols, draws, draws_t, joint),
    )
    grad_blocks, late_keep, late_send = made[:homes], made[homes], made[homes + 1]

    out_far = lax.ppermute(out_blocks[1], "home", partners(homes, 2))
    grad_received = send(grad_blocks, "home", homes)

    def finish_outputs(far):
        near = lax.ppermute(forward_pair(out_blocks[0], far), "home", partners(homes, 1))
        return place_blocks(s, place, out_blocks[0], far, near)

    split = paired and cells == 4 and homes == 4
    if split:

        def spread(pieces, axis, size):
            return [pieces[0]] + send(pieces, axis, size)

        def repeated(piece, axis, size):
            return [piece] + send([piece] * size, axis, size)

        outputs = finish_outputs(after(out_far, late_keep))
        early = spread(add_split(place, homes + 3, [early_keep, other(early_send)], cells), "cells", cells)
        late_send = after(late_send, out_far, *early[1:])
        late = spread(add_split(place, homes + 3, [late_keep, other(late_send)], cells), "cells", cells)
        rows = (early[0].shape[0] // homes, late[0].shape[0] // homes)
        both = spread(meet(place, homes + 4, early, late, homes), "home", homes)
        both[0] = after(both[0], outputs)
        both = repeated(add_split(place, homes + 4, both, 1)[0], "home", homes)
        both = repeated(stack_rows(both), "cells", cells)
        both[0] = after(both[0], grad_received[1])
        both = stack_rows(both)
        sums = (both, other(after(both, grad_received[0], grad_received[2])))
    else:
        axes = ("rest", "cells", "home")

        def summed(keep, sent):
            swap = half_side == 1
            whole_sum = jnp.where(swap, jnp.concatenate([sent, keep]), jnp.concatenate([keep, sent]))
            return lax.psum(whole_sum, axes)

        outputs = finish_outputs(out_far)
        sums, rows = (summed(early_keep, early_send), summed(late_keep, late_send)), (0, 0)
    joint_grad, out_t, hid, ret_t, ob, sg, sb, rb, hb, tissue_grad, fg, fb = finish(
        s, split, tissue_table.shape[0], rows, place, *sums
    )
    return (
        outputs,
        place_apart(s, place, [grad_blocks[0]] + grad_received),
        tissue_grad,
        fg[0],
        fb[0],
        joint_grad,
        out_t.T,
        ob[0],
        sg[0],
        sb[0],
        hid,
        hb.reshape(-1),
        ret_t.T,
        rb[0],
    )
```

```python
import functools

import jax
import jax.numpy as jnp
from jax import lax
from jax.experimental import pallas as pl
from jax.experimental.pallas import tpu as pltpu
from jax.sharding import Mesh
from jax.sharding import PartitionSpec as P

EPSILON = 1e-05
LOWEST = -1e30
bf16 = jnp.bfloat16
f32 = jnp.float32
LANES = 128


def dot(left, right):
    return jnp.dot(left, right, preferred_element_type=f32)


def dot_lanes(left, right):
    return lax.dot_general(left, right, (((1,), (1,)), ((), ())), preferred_element_type=f32)


def norm_rows(values):
    centered = values - jnp.mean(values, 0, keepdims=True)
    inverse = lax.rsqrt(jnp.mean(centered * centered, 0, keepdims=True) + EPSILON)
    return centered * inverse, inverse


def norm_back_rows(upstream, normed, inverse, gain):
    scaled = upstream * gain
    return inverse * (
        scaled
        - jnp.mean(scaled, 0, keepdims=True)
        - normed * jnp.mean(scaled * normed, 0, keepdims=True)
    )


def fold(values):
    total = values[:, :LANES]
    for at in range(LANES, values.shape[1], LANES):
        total = total + values[:, at : at + LANES]
    return total


def split_low(values):
    high = values.astype(bf16)
    return high, (values - high.astype(f32)).astype(bf16)


def lane_index(shape):
    return lax.broadcasted_iota(jnp.int32, shape, len(shape) - 1)


def row_index(shape):
    return lax.broadcasted_iota(jnp.int32, shape, len(shape) - 2)


class Sizes:
    def __init__(self, mesh_sizes, inputs, feature_draws, hidden_weight):
        self.homes, self.rest = mesh_sizes["home"], mesh_sizes["rest"]
        _, self.genes, self.width = inputs.shape
        self.heads, self.feats, self.head = feature_draws.shape
        self.inner = self.heads * self.head
        self.hidden = hidden_weight.shape[1]
        self.rows = -(-self.feats // 16) * 16
        self.ext = self.head + 16
        self.scale = self.head ** (-0.25)


FIRST_MB, FINAL_MB, LAST_MB = 13, 15, 12
VMEM = pl.BlockSpec(memory_space=pltpu.VMEM)
SMEM = pl.BlockSpec(memory_space=pltpu.SMEM)


def call(name, body, args, out, scratch=(), megabytes=4, smem=0, aliases={}, flops=0):
    return pl.pallas_call(
        body,
        out_shape=out,
        in_specs=[SMEM] * smem + [VMEM] * (len(args) - smem),
        out_specs=jax.tree.map(lambda _: VMEM, out),
        scratch_shapes=list(scratch),
        input_output_aliases=aliases,
        compiler_params=pltpu.CompilerParams(vmem_limit_bytes=megabytes * 1024 * 1024),
        cost_estimate=pl.CostEstimate(flops=int(flops), bytes_accessed=1024, transcendentals=0),
        name=name,
    )(*args)


def array(*shape, dtype=f32):
    return jax.ShapeDtypeStruct(shape, dtype)


def prepare_body(s, place, joint, draws, out_t, hid, ret_t, hidden_bias, *refs):
    rows, table = refs[:6], refs[6]
    joint_t, draws_low, draws_t, out_wt, out_w, hid_w, hid_wt, ret_wt, ret_w, joint_w, cols, bias = refs[7:]
    joint_w[...] = joint[...].astype(bf16)
    joint_t[...] = joint[...].T.astype(bf16)
    for h in range(s.heads):
        draw = draws[h]
        filler = jnp.broadcast_to(draw[:, :1], (s.head, s.rows - s.feats))
        draws_low[h] = jnp.concatenate([draw, filler], 1).T.astype(bf16)
        draws_t[h] = jnp.concatenate([draw, jnp.zeros_like(filler)], 1).astype(bf16)
    out_wt[...] = out_t[...].astype(bf16)
    out_w[...] = out_t[...].T.astype(bf16)
    hid_w[...] = hid[...].astype(bf16)
    hid_wt[...] = hid[...].T.astype(bf16)
    ret_wt[...] = ret_t[...].astype(bf16)
    ret_w[...] = ret_t[...].T.astype(bf16)
    stacked = [r[...] for r in rows] + [table[pl.ds(place[s.homes + 1], 1), :]]
    stacked += [jnp.zeros((1, s.width), f32)]
    cols[...] = jnp.concatenate(stacked, 0).T
    bias[...] = jnp.broadcast_to(hidden_bias[...], (8, s.hidden)).T


def prepare(s, place, joint, draws, out_t, hid, ret_t, hidden_bias, rows, table):
    w, i, f = s.width, s.inner, s.hidden
    out = [
        array(3 * i, w, dtype=bf16),
        array(s.heads, s.rows, s.head, dtype=bf16),
        array(s.heads, s.head, s.rows, dtype=bf16),
        array(w, i, dtype=bf16),
        array(i, w, dtype=bf16),
        array(w, f, dtype=bf16),
        array(f, w, dtype=bf16),
        array(w, f, dtype=bf16),
        array(f, w, dtype=bf16),
        array(w, 3 * i, dtype=bf16),
        array(w, 8),
        array(f, 8),
    ]
    args = [place, joint, draws, out_t, hid, ret_t, hidden_bias[None], *[r[None] for r in rows], table]
    return call("prepare", functools.partial(prepare_body, s), args, out, smem=1, megabytes=8, flops=4e9)


def keys_body(s, base, count, fresh, *refs):
    refs = list(refs)
    place = refs.pop(0)
    xs = [refs.pop(0) for _ in range(count)]
    cols, joint_t, draws = (refs.pop(0) for _ in range(3))
    if not fresh:
        kv_prev = refs.pop(0)
        refs.pop(0), refs.pop(0)
    kv, shifted, qkv, ext, dashes, tops, cuts = refs
    scale = s.scale
    last_row = s.rows - 1
    tail = (s.heads, LANES - s.head, s.genes)
    ext[:, s.head :, :] = jnp.where(row_index(tail) == 0, 1.0, 0.0).astype(bf16)
    if fresh:
        state = jnp.full((16, 1), LOWEST, f32)
    else:
        state = jnp.concatenate([kv_prev[h, last_row:, 0:1] for h in range(s.heads)] + [jnp.full((16 - s.heads, 1), LOWEST, f32)], 0)
    for n in range(count):
        x = xs[n][...] + cols[:, 6:7]
        shifted[base + n] = x
        normed, _ = norm_rows(x)
        first = (normed * cols[:, 0:1] + cols[:, 1:2]).astype(bf16)
        for part in (1, 2, 0):
            rows = slice(part * s.inner, (part + 1) * s.inner)
            made = dot(joint_t[rows, :], first).astype(bf16)
            qkv[base + n, rows, :] = made
            if part == 2:
                for h in range(s.heads):
                    ext[h, : s.head, :] = made[h * s.head : (h + 1) * s.head]
        for h in range(s.heads):
            key = qkv[base + n, s.inner + h * s.head : s.inner + (h + 1) * s.head, :]
            dash = dot(draws[h], key)
            dashes[h] = dash
            key_f = key.astype(f32)
            cuts[h : h + 1, :] = jnp.sum(key_f * key_f, 0, keepdims=True) * (scale * scale * 0.5)
            tops[h : h + 1, :] = jnp.max(dash, 0, keepdims=True) * scale
        valid = place[base + n] + lane_index((1, s.genes)) < place[s.homes]
        new = jnp.maximum(state, jnp.max(jnp.where(valid, tops[...], LOWEST), 1, keepdims=True))
        decay = jnp.exp(state - new)
        state = new
        lifts = jnp.where(valid, cuts[...] + new, 1e30)
        for h in range(s.heads):
            feats = jnp.exp(scale * dashes[h] - lifts[h : h + 1]).astype(bf16)
            part = dot_lanes(feats, ext[h])
            if n == 0 and fresh:
                kv[h] = part
            else:
                kv[h] = (kv_prev if n == 0 else kv)[h] * decay[h : h + 1] + part
    for h in range(s.heads):
        kv[h, last_row:, :] = jnp.broadcast_to(state[h : h + 1], (1, LANES))


def run_keys(s, base, count, place, xs, cols, joint_t, draws, before=None):
    out = [
        array(s.heads, s.rows, LANES),
        array(s.homes, s.width, s.genes),
        array(s.homes, 3 * s.inner, s.genes, dtype=bf16),
    ]
    args = [place, *xs, cols, joint_t, draws]
    aliases = {}
    if before is not None:
        aliases = {len(args) + 1: 1, len(args) + 2: 2}
        args += list(before)
    scratch = [
        pltpu.VMEM((s.heads, LANES, s.genes), bf16),
        pltpu.VMEM((s.heads, s.rows, s.genes), f32),
        pltpu.VMEM((16, s.genes), f32),
        pltpu.VMEM((16, s.genes), f32),
    ]
    body = functools.partial(keys_body, s, base, count, before is None)
    return call("keys", body, args, out, scratch, 10, 1, aliases, 3e9 * count)


def merged(own, other, kept_rows, kept_lanes):
    last = own.shape[0] - 1
    own_peak, other_peak = own[last:, 0:1], other[last:, 0:1]
    peak = jnp.maximum(own_peak, other_peak)
    total = own * jnp.exp(own_peak - peak) + other * jnp.exp(other_peak - peak)
    inside = (row_index(own.shape) < kept_rows) & (lane_index(own.shape) < kept_lanes)
    return jnp.where(inside, total, 0.0), peak


def eye_like(size):
    return (row_index((size, size)) == lane_index((size, size))).astype(f32).astype(bf16)


def middle_body(s, base, count, first, final, *refs):
    refs = list(refs)

    def take(n):
        taken = refs[:n]
        del refs[:n]
        return taken

    (place,) = take(1)
    before = take(2) if first else take(9)
    shifted, qkv = take(2)
    cots = take(count)
    cols, hidden_bias, draws, draws_t, out_w, out_wt = take(6)
    hid_w, hid_wt, ret_w, ret_wt, joint = take(5)
    outputs, middle_grad, query_part = take(3)
    results = take(3) if final else take(9)
    if first:
        kv3, kv_t = take(2) if final else results[:2]
    else:
        kv3, kv_t = before[:2]
    feats, att, att_low, over, att_grad, query_grad = take(6)
    cot_all, acts, pre_grads = take(3)
    sums = refs if final else results[2:]
    acc_q, acc_o, acc_r, acc_h, acc_cols, acc_hb, values_grad = sums
    scale = s.scale
    ext = s.ext
    if first:
        kv_own, kv_other = before
        eye = eye_like(2 * ext)
        for h in range(s.heads):
            total, _ = merged(kv_own[h], kv_other[h], s.feats, s.head + 1)
            high, low = split_low(total[:, :ext])
            kv3[h] = jnp.concatenate([high, low, high], 1)
            kv_t[h] = dot_lanes(eye, jnp.concatenate([high, low], 1)).astype(bf16)
        for acc in sums:
            acc[...] = jnp.zeros_like(acc)
    else:
        for acc, was in zip(sums, before[2:]):
            acc[...] = was[...]
    for n in range(count):
        cot_all[n] = cots[n][...]

    def block(j, carry):
        def attend(h):
            rows = slice(h * s.head, (h + 1) * s.head)
            query = qkv[base + j, rows, :]
            query_f = query.astype(f32)
            cut = jnp.sum(query_f * query_f, 0, keepdims=True) * (scale * scale * 0.5)
            value = jnp.exp(scale * dot(draws[h], query) - cut)
            feats[h] = value
            both = dot(kv_t[h], value.astype(bf16))
            total = both[:ext] + both[ext:]
            inverse = 1.0 / total[s.head : s.head + 1]
            over[h : h + 1, :] = inverse
            result = total[: s.head] * inverse
            att[rows, :] = result
            att_low[rows, :] = result.astype(bf16)

        for h in range(s.heads):
            attend(h)

        x = shifted[base + j]
        middle = x + dot(out_wt[...], att_low[...]) + cols[:, 2:3]
        normed, inverse = norm_rows(middle)
        gain = cols[:, 3:4]
        second = (normed * gain + cols[:, 4:5]).astype(bf16)
        cot = cot_all[j]
        cot_low = cot.astype(bf16)
        result = middle + cols[:, 5:6]
        step = s.hidden // 2
        for at in range(0, s.hidden, step):
            part = slice(at, at + step)
            pre = dot(hid_wt[part, :], second) + hidden_bias[part, 0:1]
            cumulative = 0.5 * (1.0 + lax.erf(pre * 0.7071067811865476))
            acts[part, :] = (pre * cumulative).astype(bf16)
            slope = cumulative + pre * (jnp.exp(-0.5 * pre * pre) * 0.3989422804014327)
            pre_low = (dot(ret_w[part, :], cot_low) * slope).astype(bf16)
            pre_grads[part, :] = pre_low
            acc_hb[part, :] += fold(pre_low.astype(f32))
        outputs[j] = result + dot(ret_wt[...], acts[...])
        acc_r[...] += dot_lanes(cot_low, acts[...])
        acc_h[...] += dot_lanes(second, pre_grads[...])
        second_grad = dot(hid_w[...], pre_grads[...])
        grad = cot + norm_back_rows(second_grad, normed, inverse, gain)
        middle_grad[j] = grad
        branch = grad.astype(bf16)
        acc_cols[0] += fold(branch.astype(f32))
        acc_cols[1] += fold(second_grad * normed)
        acc_cols[2] += fold(second_grad)
        acc_cols[3] += fold(cot)
        acc_o[...] += dot_lanes(branch, att_low[...])
        att_grad[...] = dot(out_w[...], branch)

        def back(h):
            rows = slice(h * s.head, (h + 1) * s.head)
            upstream = att_grad[rows, :]
            inverse = over[h : h + 1, :]
            numer = upstream * inverse
            denom = -jnp.sum(upstream * att[rows, :], 0, keepdims=True) * inverse
            tail_shape = (ext - s.head, s.genes)
            tail = jnp.where(row_index(tail_shape) == 0, denom, 0.0)
            high, low = split_low(jnp.concatenate([numer, tail], 0))
            value = feats[h]
            gap = jnp.zeros((LANES - ext, s.genes), bf16)
            values_grad[h] += dot_lanes(value.astype(bf16), jnp.concatenate([high, gap], 0))
            back_feats = dot(kv3[h], jnp.concatenate([high, high, low], 0)) * value
            query = qkv[base + j, rows, :].astype(f32)
            total = jnp.sum(back_feats, 0, keepdims=True)
            result = scale * dot(draws_t[h], back_feats.astype(bf16)) - query * (total * (scale * scale))
            query_grad[rows, :] = result.astype(bf16)

        for h in range(s.heads):
            back(h)
        normal = (norm_rows(x)[0] * cols[:, 0:1] + cols[:, 1:2]).astype(bf16)
        acc_q[...] += dot_lanes(normal, query_grad[...])
        query_part[j] = dot(joint[:, : s.inner], query_grad[...])
        return carry

    lax.fori_loop(0, count, block, 0)
    if not final:
        if not first:
            results[0][...], results[1][...] = kv3[...], kv_t[...]
        return
    results[0][...] = values_grad[...]
    keep, send = results[1:]
    spare = s.hidden % LANES
    lane = lane_index((s.width, LANES))
    last = jnp.zeros((s.width, LANES), f32)
    spot = 2 * spare
    for n in range(4):
        last = jnp.where(lane == spot, jnp.sum(acc_cols[n], 1, keepdims=True), last)
        spot += 1
    for n in range(s.hidden // s.width):
        piece = acc_hb[n * s.width : (n + 1) * s.width, :]
        last = jnp.where(lane == spot, jnp.sum(piece, 1, keepdims=True), last)
        spot += 1
    if spare:
        tops = [acc[:, s.hidden - spare :] for acc in (acc_r, acc_h)]
        last = jnp.concatenate(tops + [last[:, 2 * spare :]], 1)
    tiles = []
    for acc in (acc_q, acc_o, acc_r, acc_h):
        tiles += [(acc, n * LANES) for n in range(acc.shape[1] // LANES)]
    deal_tiles(place[s.homes + 2], s.width, keep, send, tiles, last)


def deal_tiles(side, width, keep, send, tiles, last):
    half = keep.shape[0]

    def put(row, value):
        for part in (0, 1):
            begin, end = max(row, part * half), min(row + value.shape[0], (part + 1) * half)
            if begin < end:
                piece = value[begin - row : end - row]
                spots = slice(begin - part * half, end - part * half)
                if send is None:
                    keep[spots, :] = piece
                    continue

                @pl.when(side == part)
                def _():
                    keep[spots, :] = piece

                @pl.when(side != part)
                def _():
                    send[spots, :] = piece

    row = 0
    for acc, at in tiles:
        put(row, acc[:, at : at + LANES])
        row += width
    put(row, last)
    row += width
    total = half if send is None else 2 * half
    if row < total:
        put(row, jnp.zeros((total - row, LANES), f32))


def padded(rows, parts):
    return -(-rows // (8 * parts)) * 8 * parts


def halves(s, tiles, parts):
    rows = padded(tiles * s.width, parts)
    return [array(rows // 2, LANES), array(rows // 2, LANES)]


def run_middle(s, parts, place, groups, kv_own, kv_other, shifted, qkv, cots, weights):
    sums = [
        array(s.width, s.inner),
        array(s.width, s.inner),
        array(s.width, s.hidden),
        array(s.width, s.hidden),
        array(4, s.width, LANES),
        array(s.hidden, LANES),
        array(s.heads, s.rows, LANES),
    ]
    forms = [
        array(s.heads, s.rows, 3 * s.ext, dtype=bf16),
        array(s.heads, 2 * s.ext, s.rows, dtype=bf16),
    ]
    ends = [array(s.heads, s.rows, LANES)]
    ends += halves(s, 2 * (s.inner // LANES) + 2 * (s.hidden // LANES) + 1, parts)
    before, base = [kv_own, kv_other], 0
    outputs, middle_grad, query_part = [], [], []
    for index, count in enumerate(groups):
        first, final = index == 0, index == len(groups) - 1
        tokens = array(count, s.width, s.genes)
        out = [tokens, tokens, tokens]
        out += ends if final else forms + sums
        scratch = list(forms) if first and final else []
        scratch += [
            array(s.heads, s.rows, s.genes),
            array(s.inner, s.genes),
            array(s.inner, s.genes, dtype=bf16),
            array(16, s.genes),
            array(s.inner, s.genes),
            array(s.inner, s.genes, dtype=bf16),
            tokens,
            array(s.hidden, s.genes, dtype=bf16),
            array(s.hidden, s.genes, dtype=bf16),
        ]
        scratch += sums if final else []
        scratch = [pltpu.VMEM(a.shape, a.dtype) for a in scratch]
        args = [place, *before, shifted, qkv, *cots[base : base + count], *weights]
        body = functools.partial(middle_body, s, base, count, first, final)
        made = call("middle", body, args, out, scratch, FINAL_MB if final else FIRST_MB, 1, flops=7e9 * count)
        outputs.append(made[0])
        middle_grad.append(made[1])
        query_part.append(made[2])
        before, base = made[3:], base + count
    return outputs, middle_grad, query_part, before


def last_body(s, groups, *refs):
    refs = list(refs)
    place, vg_own, vg_other, kv_own, kv_other, shifted, qkv = (refs.pop(0) for _ in range(7))
    middle_grads = [refs.pop(0) for _ in groups]
    query_parts = [refs.pop(0) for _ in groups]
    cols, draws, draws_t, joint = (refs.pop(0) for _ in range(4))
    input_grad = [refs.pop(0) for _ in range(s.homes)]
    keep, send, vg2, vg_t, ext2, grads, result_all, acc, acc_cols = refs
    scale = s.scale
    ext = s.ext
    eye = eye_like(ext)
    peaks = []
    for h in range(s.heads):
        total = vg_own[h] + vg_other[h]
        inside = row_index(total.shape) < s.feats
        high, low = split_low(jnp.where(inside, total, 0.0)[:, :ext])
        vg2[h] = jnp.concatenate([high, low], 1)
        vg_t[h] = dot_lanes(eye, high)[: s.head].astype(bf16)
        peaks.append(jnp.maximum(kv_own[h, s.rows - 1 :, 0:1], kv_other[h, s.rows - 1 :, 0:1]))
    tail = (s.heads, ext - s.head, s.genes)
    ones = jnp.where(row_index(tail) == 0, 1.0, 0.0).astype(bf16)
    ext2[:, s.head : ext, :] = ones
    ext2[:, ext + s.head :, :] = ones
    acc[...] = jnp.zeros_like(acc)
    acc_cols[...] = jnp.zeros_like(acc_cols)

    def block(base, middle_grad, query_part, i, carry):
        j = base + i
        valid = place[j] + lane_index((1, s.genes)) < place[s.homes]

        def head(h):
            rows = slice(h * s.head, (h + 1) * s.head)
            key = qkv[j, s.inner + h * s.head : s.inner + (h + 1) * s.head, :]
            value = qkv[j, 2 * s.inner + h * s.head : 2 * s.inner + (h + 1) * s.head, :]
            ext2[h, : s.head, :] = value
            ext2[h, ext : ext + s.head, :] = value
            key_f = key.astype(f32)
            cut = jnp.sum(key_f * key_f, 0, keepdims=True) * (scale * scale * 0.5)
            cut = jnp.where(valid, cut + peaks[h], 1e30)
            feats = jnp.exp(scale * dot(draws[h], key) - cut)
            back_feats = dot(vg2[h], ext2[h]) * feats
            total = jnp.sum(back_feats, 0, keepdims=True)
            result = scale * dot(draws_t[h], back_feats.astype(bf16)) - key_f * (total * (scale * scale))
            grads[rows, :] = result.astype(bf16)
            result = dot(vg_t[h], feats.astype(bf16))
            grads[s.inner + h * s.head : s.inner + (h + 1) * s.head, :] = result.astype(bf16)

        for h in range(s.heads):
            head(h)
        normed, inverse = norm_rows(shifted[j])
        gain = cols[:, 0:1]
        first = (normed * gain + cols[:, 1:2]).astype(bf16)
        acc[...] += dot_lanes(first, grads[...])
        first_grad = query_part[i] + dot(joint[:, s.inner :], grads[...])
        result = middle_grad[i] + norm_back_rows(first_grad, normed, inverse, gain)
        result_all[j] = result
        acc_cols[0] += fold(first_grad * normed)
        acc_cols[1] += fold(first_grad)
        acc_cols[2] += fold(result)
        return carry

    base = 0
    for n, count in enumerate(groups):
        lax.fori_loop(0, count, functools.partial(block, base, middle_grads[n], query_parts[n]), 0)
        base += count
    for n in range(s.homes):
        input_grad[n][...] = result_all[n]
    lane = lane_index((s.width, LANES))
    sums = [jnp.sum(acc_cols[n], 1, keepdims=True) for n in range(3)]
    last = jnp.where(lane == 0, sums[0], jnp.where(lane == 1, sums[1], 0.0))
    last = jnp.where(lane == 2 + place[s.homes + 1], sums[2], last)
    tiles = [(acc, n * LANES) for n in range(acc.shape[1] // LANES)]
    deal_tiles(place[s.homes + 2], s.width, keep, send, tiles, last)


def run_last(s, parts, groups, place, vg_own, vg_other, kv_own, kv_other, shifted, qkv, middle_grad, query_part, weights):
    out = [array(s.width, s.genes)] * s.homes + halves(s, 2 * (s.inner // LANES) + 1, parts)
    scratch = [
        pltpu.VMEM((s.heads, s.rows, 2 * s.ext), bf16),
        pltpu.VMEM((s.heads, s.head, s.rows), bf16),
        pltpu.VMEM((s.heads, 2 * s.ext, s.genes), bf16),
        pltpu.VMEM((2 * s.inner, s.genes), bf16),
        pltpu.VMEM((s.homes, s.width, s.genes), f32),
        pltpu.VMEM((s.width, 2 * s.inner), f32),
        pltpu.VMEM((3, s.width, LANES), f32),
    ]
    args = [place, vg_own, vg_other, kv_own, kv_other, shifted, qkv, *middle_grad, *query_part, *weights]
    return call("last", functools.partial(last_body, s, groups), args, out, scratch, LAST_MB, 1, flops=1e9)


def partners(size, step):
    return [(i, i ^ step) for i in range(size)]


def send(values, axis, size):
    return [lax.ppermute(values[k], axis, partners(size, k)) for k in range(1, size)]


def add_split(place, spot, terms, parts):
    rows = terms[0].shape[0] // parts

    def body(numbers, *refs):
        ins, outs = refs[: len(terms)], refs[len(terms) :]
        for k in range(parts):
            at = pl.multiple_of((numbers[spot] ^ k) * rows, 8) if parts > 1 else 0
            total = ins[0][pl.ds(at, rows), :]
            for other in ins[1:]:
                total = total + other[pl.ds(at, rows), :]
            outs[k][...] = total

    out = [array(rows, LANES)] * parts
    return call("add_split", body, [place, *terms], out, smem=1, flops=1e9)


def meet(place, spot, early, late, parts):
    first, second = early[0].shape[0] // parts, late[0].shape[0] // parts

    def body(numbers, *refs):
        outs = refs[len(early) + len(late) :]
        for terms, rows, begin in ((refs[: len(early)], first, 0), (refs[len(early) : -parts], second, first)):
            for k in range(parts):
                at = pl.multiple_of((numbers[spot] ^ k) * rows, 8)
                total = terms[0][pl.ds(at, rows), :]
                for other in terms[1:]:
                    total = total + other[pl.ds(at, rows), :]
                outs[k][begin : begin + rows, :] = total

    out = [array(first + second, LANES)] * parts
    return call("meet", body, [place, *early, *late], out, smem=1, flops=1e9)


def stack_rows(pieces):
    def body(*refs):
        at = 0
        for ref in refs[:-1]:
            refs[-1][at : at + ref.shape[0], :] = ref[...]
            at += ref.shape[0]

    return call("stack", body, pieces, array(sum(p.shape[0] for p in pieces), LANES), flops=1e9)


def forward_pair(near, far):
    def body(near_ref, far_ref, out):
        out[0] = near_ref[1]
        out[1] = far_ref[1]

    return call("forward_pair", body, [near, far], array(*near.shape), flops=1e9)


def place_blocks(s, place, near, far, last):
    def body(numbers, near_ref, far_ref, last_ref, out):
        home = numbers[s.homes + 4]
        out[home] = near_ref[0]
        out[home ^ 1] = last_ref[0]
        out[home ^ 2] = far_ref[0]
        out[home ^ 3] = last_ref[1]

    out = array(s.homes, s.width, s.genes)
    made = call("place_blocks", body, [place, near, far, last], out, smem=1, flops=1e9)
    return made.transpose(0, 2, 1)


def place_apart(s, place, blocks):
    def body(numbers, *refs):
        for k in range(s.homes):
            refs[-1][numbers[s.homes + 4] ^ k] = refs[k][...]

    out = array(s.homes, s.width, s.genes)
    made = call("place_apart", body, [place, *blocks], out, smem=1, flops=1e9)
    return made.transpose(0, 2, 1)


def finish_body(s, split, tissues, rows, place, own, other, *refs):
    early, late = refs[-2:]
    joint, out_t, hid, ret_t, ob, sg, sb, rb, hb, tissue, fg, fb = refs[:-2]
    first, second = rows
    if split:
        side, cell, home = (place[s.homes + n] for n in (2, 3, 4))
        for core in range(2):
            source = (own, other)[core]
            for at in range(16):
                spot = ((side ^ core) * 4 + (cell ^ (at // 4))) * 4 + (home ^ (at % 4))
                begin = at * (first + second)
                early[pl.ds(pl.multiple_of(spot * first, 8), first), :] = source[begin : begin + first, :]
                late[pl.ds(pl.multiple_of(spot * second, 8), second), :] = source[begin + first : begin + first + second, :]
    else:
        early[...] = own[...]
        late[...] = other[...]
    ni, nh, spare = s.inner // LANES, s.hidden // LANES, s.hidden % LANES
    w = s.width

    def tile(ref, n):
        return ref[n * w : (n + 1) * w, :]

    for n in range(ni):
        joint[:, n * LANES : (n + 1) * LANES] = tile(early, n)
        out_t[:, n * LANES : (n + 1) * LANES] = tile(early, ni + n)
    for n in range(2 * ni):
        joint[:, (ni + n) * LANES : (ni + n + 1) * LANES] = tile(late, n)
    for n in range(nh):
        ret_t[:, n * LANES : (n + 1) * LANES] = tile(early, 2 * ni + n)
        hid[:, n * LANES : (n + 1) * LANES] = tile(early, 2 * ni + nh + n)
    mixed = tile(early, 2 * ni + 2 * nh)
    if spare:
        ret_t[:, nh * LANES :] = mixed[:, :spare]
        hid[:, nh * LANES :] = mixed[:, spare : 2 * spare]
    columns = mixed.T
    at = 2 * spare
    for ref in (ob, sg, sb, rb):
        ref[...] = columns[at : at + 1, :]
        at += 1
    hb[...] = jnp.concatenate([columns[at + n, :] for n in range(s.hidden // w)], 0)
    columns = tile(late, 2 * ni).T
    fg[...] = columns[0:1, :]
    fb[...] = columns[1:2, :]
    tissue[...] = columns[2 : 2 + tissues, :]


def finish(s, split, tissues, rows, place, own, other):
    w = s.width
    row = array(1, w)
    out = [array(w, 3 * s.inner), array(w, s.inner), array(w, s.hidden), array(w, s.hidden)]
    out += [row, row, row, row, array(s.hidden), array(tissues, w), row, row]
    scratch = [pltpu.VMEM((32 * n if split else ref.shape[0], LANES), f32) for n, ref in zip(rows, (own, other))]
    body = functools.partial(finish_body, s, split, tissues, rows)
    return call("finish", body, [place, own, other], out, scratch, 8, 1, flops=1e9)


def solution(mesh):
    def run(inputs, lengths, *others):
        cells_axis, genes_axis = mesh.shape["cells"], mesh.shape["genes"]
        homes = inputs.shape[0] // cells_axis
        rest = genes_axis // homes
        sizes = {"cells": cells_axis, "home": homes, "rest": rest}
        fine = Mesh(mesh.devices.reshape(cells_axis, homes, rest), ("cells", "home", "rest"))
        tokens = P("cells", ("home", "rest"), None)
        return jax.shard_map(
            lambda *args: local(sizes, *args),
            mesh=fine,
            in_specs=(tokens, P("cells"), P("cells")) + (P(),) * 13 + (tokens,),
            out_specs=(tokens, tokens) + (P(),) * 12,
            check_vma=False,
        )(inputs, lengths, *others)

    return run


def after(value, *others):
    return lax.optimization_barrier((value, *others))[0]


def local(
    sizes,
    inputs,
    lengths,
    tissue_ids,
    tissue_table,
    first_gain,
    first_bias,
    joint_weight,
    feature_draws,
    output_weight,
    output_bias,
    second_gain,
    second_bias,
    hidden_weight,
    hidden_bias,
    return_weight,
    return_bias,
    cotangent,
):
    s = Sizes(sizes, inputs, feature_draws, hidden_weight)
    homes, rest, cells = s.homes, s.rest, sizes["cells"]
    parts = cells * homes * rest
    home = lax.axis_index("home").astype(jnp.int32)
    side = lax.axis_index("rest").astype(jnp.int32)
    half_side = side % 2
    cell = lax.axis_index("cells").astype(jnp.int32)
    paired = rest == 2

    def pick(array, k):
        return lax.dynamic_index_in_dim(array, home ^ k, 0, False)

    tissue = pick(tissue_ids, 0)
    starts = [(((home ^ k) * rest + side) * s.genes) for k in range(homes)]
    place = jnp.stack(starts + [pick(lengths, 0), tissue, half_side, cell, home]).astype(jnp.int32)
    inputs_t = inputs.transpose(0, 2, 1)
    cot_t = cotangent.transpose(0, 2, 1)
    mine = [pick(inputs_t, k) for k in range(homes)]
    arrived = send(mine, "home", homes)
    my_cots = [pick(cot_t, k).astype(f32) for k in range(homes)]
    rows = (first_gain, first_bias, output_bias, second_gain, second_bias, return_bias)
    joint_t, draws, draws_t, out_wt, out_w, hid_w, hid_wt, ret_wt, ret_w, joint, cols, bias = prepare(
        s,
        place,
        joint_weight,
        feature_draws.transpose(0, 2, 1),
        output_weight.T,
        hidden_weight,
        return_weight.T,
        hidden_bias,
        rows,
        tissue_table,
    )
    state = run_keys(s, 0, 1, place, mine[:1], cols, joint_t, draws)
    late_cots = [my_cots[0]] + [after(c, *arrived) for c in my_cots[1:]]
    arrived_cot = my_cots[:1] + send(late_cots, "home", homes)
    if homes > 1:
        state = run_keys(s, 1, homes - 1, place, arrived, cols, joint_t, draws, state)
    kv, shifted, qkv = state

    def other(value):
        return lax.ppermute(value, "rest", partners(2, 1))

    if paired:
        kv_other = other(after(kv, arrived_cot[1]))
    else:
        last_row = (jnp.arange(s.rows) == s.rows - 1)[None, :, None]
        if rest > 2:
            peak = kv[:, -1:, :]
            top = lax.pmax(peak, "rest")
            kv = lax.psum(kv * jnp.exp(peak - top), "rest")
            kv = jnp.where(last_row, top, kv)
        kv_other = jnp.where(last_row, LOWEST, jnp.zeros_like(kv))
    weights = (cols, bias, draws, draws_t, out_w, out_wt, hid_w, hid_wt, ret_w, ret_wt, joint)
    groups = (2, 2)
    out_blocks, middle_grad, query_part, made = run_middle(
        s, parts, place, groups, kv, kv_other, shifted, qkv, arrived_cot, weights
    )
    vg, early_keep, early_send = made
    vg_other = other(vg) if paired else jnp.zeros_like(vg)
    if rest > 2:
        vg = lax.psum(vg, "rest")
    made = run_last(
        s,
        parts,
        groups,
        place,
        vg,
        vg_other,
        kv,
        kv_other,
        shifted,
        qkv,
        middle_grad,
        query_part,
        (cols, draws, draws_t, joint),
    )
    grad_blocks, late_keep, late_send = made[:homes], made[homes], made[homes + 1]

    out_far = lax.ppermute(out_blocks[1], "home", partners(homes, 2))
    grad_received = send(grad_blocks, "home", homes)

    def finish_outputs(far):
        near = lax.ppermute(forward_pair(out_blocks[0], far), "home", partners(homes, 1))
        return place_blocks(s, place, out_blocks[0], far, near)

    split = paired and cells == 4 and homes == 4
    if split:

        def spread(pieces, axis, size):
            return [pieces[0]] + send(pieces, axis, size)

        def repeated(piece, axis, size):
            return [piece] + send([piece] * size, axis, size)

        outputs = finish_outputs(after(out_far, late_keep))
        early = spread(add_split(place, homes + 3, [early_keep, other(early_send)], cells), "cells", cells)
        late_send = after(late_send, out_far, *early[1:])
        late = spread(add_split(place, homes + 3, [late_keep, other(late_send)], cells), "cells", cells)
        rows = (early[0].shape[0] // homes, late[0].shape[0] // homes)
        both = spread(meet(place, homes + 4, early, late, homes), "home", homes)
        both[0] = after(both[0], outputs)
        both = repeated(add_split(place, homes + 4, both, 1)[0], "home", homes)
        both = repeated(stack_rows(both), "cells", cells)
        both[0] = after(both[0], grad_received[1])
        both = stack_rows(both)
        sums = (both, other(after(both, grad_received[0], grad_received[2])))
    else:
        axes = ("rest", "cells", "home")

        def summed(keep, sent):
            swap = half_side == 1
            whole_sum = jnp.where(swap, jnp.concatenate([sent, keep]), jnp.concatenate([keep, sent]))
            return lax.psum(whole_sum, axes)

        outputs = finish_outputs(out_far)
        sums, rows = (summed(early_keep, early_send), summed(late_keep, late_send)), (0, 0)
    joint_grad, out_t, hid, ret_t, ob, sg, sb, rb, hb, tissue_grad, fg, fb = finish(
        s, split, tissue_table.shape[0], rows, place, *sums
    )
    return (
        outputs,
        place_apart(s, place, [grad_blocks[0]] + grad_received),
        tissue_grad,
        fg[0],
        fb[0],
        joint_grad,
        out_t.T,
        ob[0],
        sg[0],
        sb[0],
        hid,
        hb,
        ret_t.T,
        rb[0],
    )
```

```python
import functools

import jax
import jax.numpy as jnp
from jax import lax
from jax.experimental import pallas as pl
from jax.experimental.pallas import tpu as pltpu
from jax.sharding import Mesh
from jax.sharding import PartitionSpec as P

EPSILON = 1e-05
LOWEST = -1e30
bf16 = jnp.bfloat16
f32 = jnp.float32
LANES = 128


def dot(left, right):
    return jnp.dot(left, right, preferred_element_type=f32)


def dot_lanes(left, right):
    return lax.dot_general(left, right, (((1,), (1,)), ((), ())), preferred_element_type=f32)


def norm_rows(values):
    centered = values - jnp.mean(values, 0, keepdims=True)
    inverse = lax.rsqrt(jnp.mean(centered * centered, 0, keepdims=True) + EPSILON)
    return centered * inverse, inverse


def norm_back_rows(upstream, normed, inverse, gain):
    scaled = upstream * gain
    return inverse * (
        scaled
        - jnp.mean(scaled, 0, keepdims=True)
        - normed * jnp.mean(scaled * normed, 0, keepdims=True)
    )


def fold(values):
    total = values[:, :LANES]
    for at in range(LANES, values.shape[1], LANES):
        total = total + values[:, at : at + LANES]
    return total


def split_low(values):
    high = values.astype(bf16)
    return high, (values - high.astype(f32)).astype(bf16)


def lane_index(shape):
    return lax.broadcasted_iota(jnp.int32, shape, len(shape) - 1)


def row_index(shape):
    return lax.broadcasted_iota(jnp.int32, shape, len(shape) - 2)


class Sizes:
    def __init__(self, mesh_sizes, inputs, feature_draws, hidden_weight):
        self.homes, self.rest = mesh_sizes["home"], mesh_sizes["rest"]
        _, self.genes, self.width = inputs.shape
        self.heads, self.feats, self.head = feature_draws.shape
        self.inner = self.heads * self.head
        self.hidden = hidden_weight.shape[1]
        self.rows = -(-self.feats // 16) * 16
        self.ext = self.head + 16
        self.scale = self.head ** (-0.25)


FIRST_MB, FINAL_MB, LAST_MB = 13, 15, 12
VMEM = pl.BlockSpec(memory_space=pltpu.VMEM)
SMEM = pl.BlockSpec(memory_space=pltpu.SMEM)


def call(name, body, args, out, scratch=(), megabytes=4, smem=0, aliases={}, flops=0):
    return pl.pallas_call(
        body,
        out_shape=out,
        in_specs=[SMEM] * smem + [VMEM] * (len(args) - smem),
        out_specs=jax.tree.map(lambda _: VMEM, out),
        scratch_shapes=list(scratch),
        input_output_aliases=aliases,
        compiler_params=pltpu.CompilerParams(vmem_limit_bytes=megabytes * 1024 * 1024),
        cost_estimate=pl.CostEstimate(flops=int(flops), bytes_accessed=1024, transcendentals=0),
        name=name,
    )(*args)


def array(*shape, dtype=f32):
    return jax.ShapeDtypeStruct(shape, dtype)


def prepare_body(s, place, joint, draws, out_t, hid, ret_t, hidden_bias, *refs):
    rows, table = refs[:6], refs[6]
    joint_t, draws_low, draws_t, out_wt, out_w, hid_w, hid_wt, ret_wt, ret_w, joint_w, cols, bias = refs[7:]
    joint_w[...] = joint[...].astype(bf16)
    joint_t[...] = joint[...].T.astype(bf16)
    for h in range(s.heads):
        draw = draws[h]
        filler = jnp.broadcast_to(draw[:, :1], (s.head, s.rows - s.feats))
        draws_low[h] = jnp.concatenate([draw, filler], 1).T.astype(bf16)
        draws_t[h] = jnp.concatenate([draw, jnp.zeros_like(filler)], 1).astype(bf16)
    out_wt[...] = out_t[...].astype(bf16)
    out_w[...] = out_t[...].T.astype(bf16)
    hid_w[...] = hid[...].astype(bf16)
    hid_wt[...] = hid[...].T.astype(bf16)
    ret_wt[...] = ret_t[...].astype(bf16)
    ret_w[...] = ret_t[...].T.astype(bf16)
    stacked = [r[...] for r in rows] + [table[pl.ds(place[s.homes + 1], 1), :]]
    stacked += [jnp.zeros((1, s.width), f32)]
    cols[...] = jnp.concatenate(stacked, 0).T
    bias[...] = jnp.broadcast_to(hidden_bias[...], (8, s.hidden)).T


def prepare(s, place, joint, draws, out_t, hid, ret_t, hidden_bias, rows, table):
    w, i, f = s.width, s.inner, s.hidden
    out = [
        array(3 * i, w, dtype=bf16),
        array(s.heads, s.rows, s.head, dtype=bf16),
        array(s.heads, s.head, s.rows, dtype=bf16),
        array(w, i, dtype=bf16),
        array(i, w, dtype=bf16),
        array(w, f, dtype=bf16),
        array(f, w, dtype=bf16),
        array(w, f, dtype=bf16),
        array(f, w, dtype=bf16),
        array(w, 3 * i, dtype=bf16),
        array(w, 8),
        array(f, 8),
    ]
    args = [place, joint, draws, out_t, hid, ret_t, hidden_bias[None], *[r[None] for r in rows], table]
    return call("prepare", functools.partial(prepare_body, s), args, out, smem=1, megabytes=8, flops=4e9)


def keys_body(s, base, count, fresh, *refs):
    refs = list(refs)
    place = refs.pop(0)
    xs = [refs.pop(0) for _ in range(count)]
    cols, joint_t, draws = (refs.pop(0) for _ in range(3))
    if not fresh:
        kv_prev = refs.pop(0)
        refs.pop(0), refs.pop(0)
    kv, shifted, qkv, ext, dashes, tops, cuts = refs
    scale = s.scale
    last_row = s.rows - 1
    tail = (s.heads, LANES - s.head, s.genes)
    ext[:, s.head :, :] = jnp.where(row_index(tail) == 0, 1.0, 0.0).astype(bf16)
    if fresh:
        state = jnp.full((16, 1), LOWEST, f32)
    else:
        state = jnp.concatenate([kv_prev[h, last_row:, 0:1] for h in range(s.heads)] + [jnp.full((16 - s.heads, 1), LOWEST, f32)], 0)
    for n in range(count):
        x = xs[n][...] + cols[:, 6:7]
        shifted[base + n] = x
        normed, _ = norm_rows(x)
        first = (normed * cols[:, 0:1] + cols[:, 1:2]).astype(bf16)
        for part in (1, 2, 0):
            rows = slice(part * s.inner, (part + 1) * s.inner)
            made = dot(joint_t[rows, :], first).astype(bf16)
            qkv[base + n, rows, :] = made
            if part == 2:
                for h in range(s.heads):
                    ext[h, : s.head, :] = made[h * s.head : (h + 1) * s.head]
        for h in range(s.heads):
            key = qkv[base + n, s.inner + h * s.head : s.inner + (h + 1) * s.head, :]
            dash = dot(draws[h], key)
            dashes[h] = dash
            key_f = key.astype(f32)
            cuts[h : h + 1, :] = jnp.sum(key_f * key_f, 0, keepdims=True) * (scale * scale * 0.5)
            tops[h : h + 1, :] = jnp.max(dash, 0, keepdims=True) * scale
        valid = place[base + n] + lane_index((1, s.genes)) < place[s.homes]
        new = jnp.maximum(state, jnp.max(jnp.where(valid, tops[...], LOWEST), 1, keepdims=True))
        decay = jnp.exp(state - new)
        state = new
        lifts = jnp.where(valid, cuts[...] + new, 1e30)
        for h in range(s.heads):
            feats = jnp.exp(scale * dashes[h] - lifts[h : h + 1]).astype(bf16)
            part = dot_lanes(feats, ext[h])
            if n == 0 and fresh:
                kv[h] = part
            else:
                kv[h] = (kv_prev if n == 0 else kv)[h] * decay[h : h + 1] + part
    for h in range(s.heads):
        kv[h, last_row:, :] = jnp.broadcast_to(state[h : h + 1], (1, LANES))


def run_keys(s, base, count, place, xs, cols, joint_t, draws, before=None):
    out = [
        array(s.heads, s.rows, LANES),
        array(s.homes, s.width, s.genes),
        array(s.homes, 3 * s.inner, s.genes, dtype=bf16),
    ]
    args = [place, *xs, cols, joint_t, draws]
    aliases = {}
    if before is not None:
        aliases = {len(args) + 1: 1, len(args) + 2: 2}
        args += list(before)
    scratch = [
        pltpu.VMEM((s.heads, LANES, s.genes), bf16),
        pltpu.VMEM((s.heads, s.rows, s.genes), f32),
        pltpu.VMEM((16, s.genes), f32),
        pltpu.VMEM((16, s.genes), f32),
    ]
    body = functools.partial(keys_body, s, base, count, before is None)
    return call("keys", body, args, out, scratch, 10, 1, aliases, 3e9 * count)


def merged(own, other, kept_rows, kept_lanes):
    last = own.shape[0] - 1
    own_peak, other_peak = own[last:, 0:1], other[last:, 0:1]
    peak = jnp.maximum(own_peak, other_peak)
    total = own * jnp.exp(own_peak - peak) + other * jnp.exp(other_peak - peak)
    inside = (row_index(own.shape) < kept_rows) & (lane_index(own.shape) < kept_lanes)
    return jnp.where(inside, total, 0.0), peak


def eye_like(size):
    return (row_index((size, size)) == lane_index((size, size))).astype(f32).astype(bf16)


def middle_body(s, base, count, later, first, final, *refs):
    refs = list(refs)

    def take(n):
        taken = refs[:n]
        del refs[:n]
        return taken

    (place,) = take(1)
    before = take(2) if first else take(13)
    shifted, qkv = take(2)
    cots = take(count)
    cols, hidden_bias, draws, draws_t, out_w, out_wt = take(6)
    hid_w, hid_wt, ret_w, ret_wt, joint = take(5)
    outputs, middle_grad, query_part = take(3)
    results = take(3) if final else take(13)
    if first:
        kv3, kv_t = take(2) if final else results[:2]
    else:
        kv3, kv_t = before[:2]
    mine = take(4) if first else None
    ahead = before[9:] if not first else results[9:]
    att_grad, query_grad = take(2)
    cot_all, acts, pre_grads = take(3)
    sums = refs if final else results[2:9]
    acc_q, acc_o, acc_r, acc_h, acc_cols, acc_hb, values_grad = sums
    scale = s.scale
    ext = s.ext
    if first:
        kv_own, kv_other = before
        eye = eye_like(2 * ext)
        for h in range(s.heads):
            total, _ = merged(kv_own[h], kv_other[h], s.feats, s.head + 1)
            high, low = split_low(total[:, :ext])
            kv3[h] = jnp.concatenate([high, low, high], 1)
            kv_t[h] = dot_lanes(eye, jnp.concatenate([high, low], 1)).astype(bf16)
        for acc in sums:
            acc[...] = jnp.zeros_like(acc)
    else:
        for acc, was in zip(sums, before[2:]):
            acc[...] = was[...]
    for n in range(count):
        cot_all[n] = cots[n][...]

    def attend(index, feats, att, att_low, over):
        for h in range(s.heads):
            rows = slice(h * s.head, (h + 1) * s.head)
            query = qkv[index, rows, :]
            query_f = query.astype(f32)
            cut = jnp.sum(query_f * query_f, 0, keepdims=True) * (scale * scale * 0.5)
            value = jnp.exp(scale * dot(draws[h], query) - cut)
            feats[h] = value
            both = dot(kv_t[h], value.astype(bf16))
            total = both[:ext] + both[ext:]
            inverse = 1.0 / total[s.head : s.head + 1]
            over[h : h + 1, :] = inverse
            result = total[: s.head] * inverse
            att[rows, :] = result
            att_low[rows, :] = result.astype(bf16)

    def block(j, carry):
        feats, att, att_low, over = mine if first else [ref.at[j] for ref in ahead]
        if first:
            attend(base + j, feats, att, att_low, over)
        x = shifted[base + j]
        middle = x + dot(out_wt[...], att_low[...]) + cols[:, 2:3]
        normed, inverse = norm_rows(middle)
        gain = cols[:, 3:4]
        second = (normed * gain + cols[:, 4:5]).astype(bf16)
        cot = cot_all[j]
        cot_low = cot.astype(bf16)
        result = middle + cols[:, 5:6]
        step = s.hidden // 2
        for at in range(0, s.hidden, step):
            part = slice(at, at + step)
            pre = dot(hid_wt[part, :], second) + hidden_bias[part, 0:1]
            cumulative = 0.5 * (1.0 + lax.erf(pre * 0.7071067811865476))
            acts[part, :] = (pre * cumulative).astype(bf16)
            slope = cumulative + pre * (jnp.exp(-0.5 * pre * pre) * 0.3989422804014327)
            pre_low = (dot(ret_w[part, :], cot_low) * slope).astype(bf16)
            pre_grads[part, :] = pre_low
            acc_hb[part, :] += fold(pre_low.astype(f32))
        outputs[j] = result + dot(ret_wt[...], acts[...])
        acc_r[...] += dot_lanes(cot_low, acts[...])
        acc_h[...] += dot_lanes(second, pre_grads[...])
        second_grad = dot(hid_w[...], pre_grads[...])
        grad = cot + norm_back_rows(second_grad, normed, inverse, gain)
        middle_grad[j] = grad
        branch = grad.astype(bf16)
        acc_cols[0] += fold(branch.astype(f32))
        acc_cols[1] += fold(second_grad * normed)
        acc_cols[2] += fold(second_grad)
        acc_cols[3] += fold(cot)
        acc_o[...] += dot_lanes(branch, att_low[...])
        att_grad[...] = dot(out_w[...], branch)

        def back(h):
            rows = slice(h * s.head, (h + 1) * s.head)
            upstream = att_grad[rows, :]
            inverse = over[h : h + 1, :]
            numer = upstream * inverse
            denom = -jnp.sum(upstream * att[rows, :], 0, keepdims=True) * inverse
            tail_shape = (ext - s.head, s.genes)
            tail = jnp.where(row_index(tail_shape) == 0, denom, 0.0)
            high, low = split_low(jnp.concatenate([numer, tail], 0))
            value = feats[h]
            gap = jnp.zeros((LANES - ext, s.genes), bf16)
            values_grad[h] += dot_lanes(value.astype(bf16), jnp.concatenate([high, gap], 0))
            back_feats = dot(kv3[h], jnp.concatenate([high, high, low], 0)) * value
            query = qkv[base + j, rows, :].astype(f32)
            total = jnp.sum(back_feats, 0, keepdims=True)
            result = scale * dot(draws_t[h], back_feats.astype(bf16)) - query * (total * (scale * scale))
            query_grad[rows, :] = result.astype(bf16)

        for h in range(s.heads):
            back(h)
        normal = (norm_rows(x)[0] * cols[:, 0:1] + cols[:, 1:2]).astype(bf16)
        acc_q[...] += dot_lanes(normal, query_grad[...])
        query_part[j] = dot(joint[:, : s.inner], query_grad[...])
        return carry

    lax.fori_loop(0, count, block, 0)
    if not final:

        def attend_ahead(n, carry):
            attend(base + count + n, *[ref.at[n] for ref in ahead])
            return carry

        lax.fori_loop(0, later, attend_ahead, 0)
        if not first:
            results[0][...], results[1][...] = kv3[...], kv_t[...]
        return
    results[0][...] = values_grad[...]
    keep, send = results[1:]
    spare = s.hidden % LANES
    lane = lane_index((s.width, LANES))
    last = jnp.zeros((s.width, LANES), f32)
    spot = 2 * spare
    for n in range(4):
        last = jnp.where(lane == spot, jnp.sum(acc_cols[n], 1, keepdims=True), last)
        spot += 1
    for n in range(s.hidden // s.width):
        piece = acc_hb[n * s.width : (n + 1) * s.width, :]
        last = jnp.where(lane == spot, jnp.sum(piece, 1, keepdims=True), last)
        spot += 1
    if spare:
        tops = [acc[:, s.hidden - spare :] for acc in (acc_r, acc_h)]
        last = jnp.concatenate(tops + [last[:, 2 * spare :]], 1)
    tiles = []
    for acc in (acc_q, acc_o, acc_r, acc_h):
        tiles += [(acc, n * LANES) for n in range(acc.shape[1] // LANES)]
    deal_tiles(place[s.homes + 2], s.width, keep, send, tiles, last)


def deal_tiles(side, width, keep, send, tiles, last):
    half = keep.shape[0]

    def put(row, value):
        for part in (0, 1):
            begin, end = max(row, part * half), min(row + value.shape[0], (part + 1) * half)
            if begin < end:
                piece = value[begin - row : end - row]
                spots = slice(begin - part * half, end - part * half)
                if send is None:
                    keep[spots, :] = piece
                    continue

                @pl.when(side == part)
                def _():
                    keep[spots, :] = piece

                @pl.when(side != part)
                def _():
                    send[spots, :] = piece

    row = 0
    for acc, at in tiles:
        put(row, acc[:, at : at + LANES])
        row += width
    put(row, last)
    row += width
    total = half if send is None else 2 * half
    if row < total:
        put(row, jnp.zeros((total - row, LANES), f32))


def padded(rows, parts):
    return -(-rows // (8 * parts)) * 8 * parts


def halves(s, tiles, parts):
    rows = padded(tiles * s.width, parts)
    return [array(rows // 2, LANES), array(rows // 2, LANES)]


def run_middle(s, parts, place, groups, kv_own, kv_other, shifted, qkv, cots, weights):
    sums = [
        array(s.width, s.inner),
        array(s.width, s.inner),
        array(s.width, s.hidden),
        array(s.width, s.hidden),
        array(4, s.width, LANES),
        array(s.hidden, LANES),
        array(s.heads, s.rows, LANES),
    ]
    forms = [
        array(s.heads, s.rows, 3 * s.ext, dtype=bf16),
        array(s.heads, 2 * s.ext, s.rows, dtype=bf16),
    ]
    attention = [
        array(s.heads, s.rows, s.genes),
        array(s.inner, s.genes),
        array(s.inner, s.genes, dtype=bf16),
        array(16, s.genes),
    ]
    ends = [array(s.heads, s.rows, LANES)]
    ends += halves(s, 2 * (s.inner // LANES) + 2 * (s.hidden // LANES) + 1, parts)
    before, base = [kv_own, kv_other], 0
    outputs, middle_grad, query_part = [], [], []
    for index, count in enumerate(groups):
        first, final = index == 0, index == len(groups) - 1
        tokens = array(count, s.width, s.genes)
        out = [tokens, tokens, tokens]
        later = sum(groups[index + 1 :])
        ahead = [array(later, *a.shape, dtype=a.dtype) for a in attention]
        out += ends if final else forms + sums + ahead
        scratch = list(forms) if first and final else []
        scratch += attention if first else []
        scratch += [
            array(s.inner, s.genes),
            array(s.inner, s.genes, dtype=bf16),
            tokens,
            array(s.hidden, s.genes, dtype=bf16),
            array(s.hidden, s.genes, dtype=bf16),
        ]
        scratch += sums if final else []
        scratch = [pltpu.VMEM(a.shape, a.dtype) for a in scratch]
        args = [place, *before, shifted, qkv, *cots[base : base + count], *weights]
        body = functools.partial(middle_body, s, base, count, later, first, final)
        made = call("middle", body, args, out, scratch, FINAL_MB if final else FIRST_MB, 1, flops=7e9 * count)
        outputs.append(made[0])
        middle_grad.append(made[1])
        query_part.append(made[2])
        before, base = made[3:], base + count
    return outputs, middle_grad, query_part, before


def last_body(s, groups, *refs):
    refs = list(refs)
    place, vg_own, vg_other, kv_own, kv_other, shifted, qkv = (refs.pop(0) for _ in range(7))
    middle_grads = [refs.pop(0) for _ in groups]
    query_parts = [refs.pop(0) for _ in groups]
    cols, draws, draws_t, joint = (refs.pop(0) for _ in range(4))
    input_grad = [refs.pop(0) for _ in range(s.homes)]
    keep, send, vg2, vg_t, ext2, grads, result_all, acc, acc_cols = refs
    scale = s.scale
    ext = s.ext
    eye = eye_like(ext)
    peaks = []
    for h in range(s.heads):
        total = vg_own[h] + vg_other[h]
        inside = row_index(total.shape) < s.feats
        high, low = split_low(jnp.where(inside, total, 0.0)[:, :ext])
        vg2[h] = jnp.concatenate([high, low], 1)
        vg_t[h] = dot_lanes(eye, high)[: s.head].astype(bf16)
        peaks.append(jnp.maximum(kv_own[h, s.rows - 1 :, 0:1], kv_other[h, s.rows - 1 :, 0:1]))
    tail = (s.heads, ext - s.head, s.genes)
    ones = jnp.where(row_index(tail) == 0, 1.0, 0.0).astype(bf16)
    ext2[:, s.head : ext, :] = ones
    ext2[:, ext + s.head :, :] = ones
    acc[...] = jnp.zeros_like(acc)
    acc_cols[...] = jnp.zeros_like(acc_cols)

    def block(base, middle_grad, query_part, i, carry):
        j = base + i
        valid = place[j] + lane_index((1, s.genes)) < place[s.homes]

        def head(h):
            rows = slice(h * s.head, (h + 1) * s.head)
            key = qkv[j, s.inner + h * s.head : s.inner + (h + 1) * s.head, :]
            value = qkv[j, 2 * s.inner + h * s.head : 2 * s.inner + (h + 1) * s.head, :]
            ext2[h, : s.head, :] = value
            ext2[h, ext : ext + s.head, :] = value
            key_f = key.astype(f32)
            cut = jnp.sum(key_f * key_f, 0, keepdims=True) * (scale * scale * 0.5)
            cut = jnp.where(valid, cut + peaks[h], 1e30)
            feats = jnp.exp(scale * dot(draws[h], key) - cut)
            back_feats = dot(vg2[h], ext2[h]) * feats
            total = jnp.sum(back_feats, 0, keepdims=True)
            result = scale * dot(draws_t[h], back_feats.astype(bf16)) - key_f * (total * (scale * scale))
            grads[rows, :] = result.astype(bf16)
            result = dot(vg_t[h], feats.astype(bf16))
            grads[s.inner + h * s.head : s.inner + (h + 1) * s.head, :] = result.astype(bf16)

        for h in range(s.heads):
            head(h)
        normed, inverse = norm_rows(shifted[j])
        gain = cols[:, 0:1]
        first = (normed * gain + cols[:, 1:2]).astype(bf16)
        acc[...] += dot_lanes(first, grads[...])
        first_grad = query_part[i] + dot(joint[:, s.inner :], grads[...])
        result = middle_grad[i] + norm_back_rows(first_grad, normed, inverse, gain)
        result_all[j] = result
        acc_cols[0] += fold(first_grad * normed)
        acc_cols[1] += fold(first_grad)
        acc_cols[2] += fold(result)
        return carry

    base = 0
    for n, count in enumerate(groups):
        lax.fori_loop(0, count, functools.partial(block, base, middle_grads[n], query_parts[n]), 0)
        base += count
    for n in range(s.homes):
        input_grad[n][...] = result_all[n]
    lane = lane_index((s.width, LANES))
    sums = [jnp.sum(acc_cols[n], 1, keepdims=True) for n in range(3)]
    last = jnp.where(lane == 0, sums[0], jnp.where(lane == 1, sums[1], 0.0))
    last = jnp.where(lane == 2 + place[s.homes + 1], sums[2], last)
    tiles = [(acc, n * LANES) for n in range(acc.shape[1] // LANES)]
    deal_tiles(place[s.homes + 2], s.width, keep, send, tiles, last)


def run_last(s, parts, groups, place, vg_own, vg_other, kv_own, kv_other, shifted, qkv, middle_grad, query_part, weights):
    out = [array(s.width, s.genes)] * s.homes + halves(s, 2 * (s.inner // LANES) + 1, parts)
    scratch = [
        pltpu.VMEM((s.heads, s.rows, 2 * s.ext), bf16),
        pltpu.VMEM((s.heads, s.head, s.rows), bf16),
        pltpu.VMEM((s.heads, 2 * s.ext, s.genes), bf16),
        pltpu.VMEM((2 * s.inner, s.genes), bf16),
        pltpu.VMEM((s.homes, s.width, s.genes), f32),
        pltpu.VMEM((s.width, 2 * s.inner), f32),
        pltpu.VMEM((3, s.width, LANES), f32),
    ]
    args = [place, vg_own, vg_other, kv_own, kv_other, shifted, qkv, *middle_grad, *query_part, *weights]
    return call("last", functools.partial(last_body, s, groups), args, out, scratch, LAST_MB, 1, flops=1e9)


def partners(size, step):
    return [(i, i ^ step) for i in range(size)]


def send(values, axis, size):
    return [lax.ppermute(values[k], axis, partners(size, k)) for k in range(1, size)]


def add_split(place, spot, terms, parts):
    rows = terms[0].shape[0] // parts

    def body(numbers, *refs):
        ins, outs = refs[: len(terms)], refs[len(terms) :]
        for k in range(parts):
            at = pl.multiple_of((numbers[spot] ^ k) * rows, 8) if parts > 1 else 0
            total = ins[0][pl.ds(at, rows), :]
            for other in ins[1:]:
                total = total + other[pl.ds(at, rows), :]
            outs[k][...] = total

    out = [array(rows, LANES)] * parts
    return call("add_split", body, [place, *terms], out, smem=1, flops=1e9)


def meet(place, spot, early, late, parts):
    first, second = early[0].shape[0] // parts, late[0].shape[0] // parts

    def body(numbers, *refs):
        outs = refs[len(early) + len(late) :]
        for terms, rows, begin in ((refs[: len(early)], first, 0), (refs[len(early) : -parts], second, first)):
            for k in range(parts):
                at = pl.multiple_of((numbers[spot] ^ k) * rows, 8)
                total = terms[0][pl.ds(at, rows), :]
                for other in terms[1:]:
                    total = total + other[pl.ds(at, rows), :]
                outs[k][begin : begin + rows, :] = total

    out = [array(first + second, LANES)] * parts
    return call("meet", body, [place, *early, *late], out, smem=1, flops=1e9)


def stack_rows(pieces):
    def body(*refs):
        at = 0
        for ref in refs[:-1]:
            refs[-1][at : at + ref.shape[0], :] = ref[...]
            at += ref.shape[0]

    return call("stack", body, pieces, array(sum(p.shape[0] for p in pieces), LANES), flops=1e9)


def forward_pair(near, far):
    def body(near_ref, far_ref, out):
        out[0] = near_ref[1]
        out[1] = far_ref[1]

    return call("forward_pair", body, [near, far], array(*near.shape), flops=1e9)


def place_blocks(s, place, near, far, last):
    def body(numbers, near_ref, far_ref, last_ref, out):
        home = numbers[s.homes + 4]
        out[home] = near_ref[0]
        out[home ^ 1] = last_ref[0]
        out[home ^ 2] = far_ref[0]
        out[home ^ 3] = last_ref[1]

    out = array(s.homes, s.width, s.genes)
    made = call("place_blocks", body, [place, near, far, last], out, smem=1, flops=1e9)
    return made.transpose(0, 2, 1)


def place_apart(s, place, blocks):
    def body(numbers, *refs):
        for k in range(s.homes):
            refs[-1][numbers[s.homes + 4] ^ k] = refs[k][...]

    out = array(s.homes, s.width, s.genes)
    made = call("place_apart", body, [place, *blocks], out, smem=1, flops=1e9)
    return made.transpose(0, 2, 1)


def finish_body(s, split, tissues, rows, place, own, other, *refs):
    early, late = refs[-2:]
    joint, out_t, hid, ret_t, ob, sg, sb, rb, hb, tissue, fg, fb = refs[:-2]
    first, second = rows
    if split:
        side, cell, home = (place[s.homes + n] for n in (2, 3, 4))
        for core in range(2):
            source = (own, other)[core]
            for at in range(16):
                spot = ((side ^ core) * 4 + (cell ^ (at // 4))) * 4 + (home ^ (at % 4))
                begin = at * (first + second)
                early[pl.ds(pl.multiple_of(spot * first, 8), first), :] = source[begin : begin + first, :]
                late[pl.ds(pl.multiple_of(spot * second, 8), second), :] = source[begin + first : begin + first + second, :]
    else:
        early[...] = own[...]
        late[...] = other[...]
    ni, nh, spare = s.inner // LANES, s.hidden // LANES, s.hidden % LANES
    w = s.width

    def tile(ref, n):
        return ref[n * w : (n + 1) * w, :]

    for n in range(ni):
        joint[:, n * LANES : (n + 1) * LANES] = tile(early, n)
        out_t[:, n * LANES : (n + 1) * LANES] = tile(early, ni + n)
    for n in range(2 * ni):
        joint[:, (ni + n) * LANES : (ni + n + 1) * LANES] = tile(late, n)
    for n in range(nh):
        ret_t[:, n * LANES : (n + 1) * LANES] = tile(early, 2 * ni + n)
        hid[:, n * LANES : (n + 1) * LANES] = tile(early, 2 * ni + nh + n)
    mixed = tile(early, 2 * ni + 2 * nh)
    if spare:
        ret_t[:, nh * LANES :] = mixed[:, :spare]
        hid[:, nh * LANES :] = mixed[:, spare : 2 * spare]
    columns = mixed.T
    at = 2 * spare
    for ref in (ob, sg, sb, rb):
        ref[...] = columns[at : at + 1, :]
        at += 1
    hb[...] = jnp.concatenate([columns[at + n, :] for n in range(s.hidden // w)], 0)
    columns = tile(late, 2 * ni).T
    fg[...] = columns[0:1, :]
    fb[...] = columns[1:2, :]
    tissue[...] = columns[2 : 2 + tissues, :]


def finish(s, split, tissues, rows, place, own, other):
    w = s.width
    row = array(1, w)
    out = [array(w, 3 * s.inner), array(w, s.inner), array(w, s.hidden), array(w, s.hidden)]
    out += [row, row, row, row, array(s.hidden), array(tissues, w), row, row]
    scratch = [pltpu.VMEM((32 * n if split else ref.shape[0], LANES), f32) for n, ref in zip(rows, (own, other))]
    body = functools.partial(finish_body, s, split, tissues, rows)
    return call("finish", body, [place, own, other], out, scratch, 8, 1, flops=1e9)


def solution(mesh):
    def run(inputs, lengths, *others):
        cells_axis, genes_axis = mesh.shape["cells"], mesh.shape["genes"]
        homes = inputs.shape[0] // cells_axis
        rest = genes_axis // homes
        sizes = {"cells": cells_axis, "home": homes, "rest": rest}
        fine = Mesh(mesh.devices.reshape(cells_axis, homes, rest), ("cells", "home", "rest"))
        tokens = P("cells", ("home", "rest"), None)
        return jax.shard_map(
            lambda *args: local(sizes, *args),
            mesh=fine,
            in_specs=(tokens, P("cells"), P("cells")) + (P(),) * 13 + (tokens,),
            out_specs=(tokens, tokens) + (P(),) * 12,
            check_vma=False,
        )(inputs, lengths, *others)

    return run


def after(value, *others):
    return lax.optimization_barrier((value, *others))[0]


def local(
    sizes,
    inputs,
    lengths,
    tissue_ids,
    tissue_table,
    first_gain,
    first_bias,
    joint_weight,
    feature_draws,
    output_weight,
    output_bias,
    second_gain,
    second_bias,
    hidden_weight,
    hidden_bias,
    return_weight,
    return_bias,
    cotangent,
):
    s = Sizes(sizes, inputs, feature_draws, hidden_weight)
    homes, rest, cells = s.homes, s.rest, sizes["cells"]
    parts = cells * homes * rest
    home = lax.axis_index("home").astype(jnp.int32)
    side = lax.axis_index("rest").astype(jnp.int32)
    half_side = side % 2
    cell = lax.axis_index("cells").astype(jnp.int32)
    paired = rest == 2

    def pick(array, k):
        return lax.dynamic_index_in_dim(array, home ^ k, 0, False)

    tissue = pick(tissue_ids, 0)
    starts = [(((home ^ k) * rest + side) * s.genes) for k in range(homes)]
    place = jnp.stack(starts + [pick(lengths, 0), tissue, half_side, cell, home]).astype(jnp.int32)
    inputs_t = inputs.transpose(0, 2, 1)
    cot_t = cotangent.transpose(0, 2, 1)
    mine = [pick(inputs_t, k) for k in range(homes)]
    arrived = send(mine, "home", homes)
    my_cots = [pick(cot_t, k).astype(f32) for k in range(homes)]
    rows = (first_gain, first_bias, output_bias, second_gain, second_bias, return_bias)
    joint_t, draws, draws_t, out_wt, out_w, hid_w, hid_wt, ret_wt, ret_w, joint, cols, bias = prepare(
        s,
        place,
        joint_weight,
        feature_draws.transpose(0, 2, 1),
        output_weight.T,
        hidden_weight,
        return_weight.T,
        hidden_bias,
        rows,
        tissue_table,
    )
    state = run_keys(s, 0, 1, place, mine[:1], cols, joint_t, draws)
    late_cots = [my_cots[0]] + [after(c, *arrived) for c in my_cots[1:]]
    arrived_cot = my_cots[:1] + send(late_cots, "home", homes)
    if homes > 1:
        state = run_keys(s, 1, homes - 1, place, arrived, cols, joint_t, draws, state)
    kv, shifted, qkv = state

    def other(value):
        return lax.ppermute(value, "rest", partners(2, 1))

    if paired:
        kv_other = other(after(kv, arrived_cot[1]))
    else:
        last_row = (jnp.arange(s.rows) == s.rows - 1)[None, :, None]
        if rest > 2:
            peak = kv[:, -1:, :]
            top = lax.pmax(peak, "rest")
            kv = lax.psum(kv * jnp.exp(peak - top), "rest")
            kv = jnp.where(last_row, top, kv)
        kv_other = jnp.where(last_row, LOWEST, jnp.zeros_like(kv))
    weights = (cols, bias, draws, draws_t, out_w, out_wt, hid_w, hid_wt, ret_w, ret_wt, joint)
    groups = (2, 2)
    out_blocks, middle_grad, query_part, made = run_middle(
        s, parts, place, groups, kv, kv_other, shifted, qkv, arrived_cot, weights
    )
    vg, early_keep, early_send = made
    vg_other = other(vg) if paired else jnp.zeros_like(vg)
    if rest > 2:
        vg = lax.psum(vg, "rest")
    made = run_last(
        s,
        parts,
        groups,
        place,
        vg,
        vg_other,
        kv,
        kv_other,
        shifted,
        qkv,
        middle_grad,
        query_part,
        (cols, draws, draws_t, joint),
    )
    grad_blocks, late_keep, late_send = made[:homes], made[homes], made[homes + 1]

    out_far = lax.ppermute(out_blocks[1], "home", partners(homes, 2))
    grad_received = send(grad_blocks, "home", homes)

    def finish_outputs(far):
        near = lax.ppermute(forward_pair(out_blocks[0], far), "home", partners(homes, 1))
        return place_blocks(s, place, out_blocks[0], far, near)

    split = paired and cells == 4 and homes == 4
    if split:

        def spread(pieces, axis, size):
            return [pieces[0]] + send(pieces, axis, size)

        def repeated(piece, axis, size):
            return [piece] + send([piece] * size, axis, size)

        outputs = finish_outputs(after(out_far, late_keep))
        early = spread(add_split(place, homes + 3, [early_keep, other(early_send)], cells), "cells", cells)
        late_send = after(late_send, out_far, *early[1:])
        late = spread(add_split(place, homes + 3, [late_keep, other(late_send)], cells), "cells", cells)
        rows = (early[0].shape[0] // homes, late[0].shape[0] // homes)
        both = spread(meet(place, homes + 4, early, late, homes), "home", homes)
        both[0] = after(both[0], outputs)
        both = repeated(add_split(place, homes + 4, both, 1)[0], "home", homes)
        both = repeated(stack_rows(both), "cells", cells)
        both[0] = after(both[0], grad_received[1])
        both = stack_rows(both)
        sums = (both, other(after(both, grad_received[0], grad_received[2])))
    else:
        axes = ("rest", "cells", "home")

        def summed(keep, sent):
            swap = half_side == 1
            whole_sum = jnp.where(swap, jnp.concatenate([sent, keep]), jnp.concatenate([keep, sent]))
            return lax.psum(whole_sum, axes)

        outputs = finish_outputs(out_far)
        sums, rows = (summed(early_keep, early_send), summed(late_keep, late_send)), (0, 0)
    joint_grad, out_t, hid, ret_t, ob, sg, sb, rb, hb, tissue_grad, fg, fb = finish(
        s, split, tissue_table.shape[0], rows, place, *sums
    )
    return (
        outputs,
        place_apart(s, place, [grad_blocks[0]] + grad_received),
        tissue_grad,
        fg[0],
        fb[0],
        joint_grad,
        out_t.T,
        ob[0],
        sg[0],
        sb[0],
        hid,
        hb,
        ret_t.T,
        rb[0],
    )
```

```python
import functools

import jax
import jax.numpy as jnp
from jax import lax
from jax.experimental import pallas as pl
from jax.experimental.pallas import tpu as pltpu
from jax.sharding import Mesh
from jax.sharding import PartitionSpec as P

EPSILON = 1e-05
LOWEST = -1e30
bf16 = jnp.bfloat16
f32 = jnp.float32
LANES = 128


def dot(left, right):
    return jnp.dot(left, right, preferred_element_type=f32)


def dot_lanes(left, right):
    return lax.dot_general(left, right, (((1,), (1,)), ((), ())), preferred_element_type=f32)


def norm_rows(values):
    centered = values - jnp.mean(values, 0, keepdims=True)
    inverse = lax.rsqrt(jnp.mean(centered * centered, 0, keepdims=True) + EPSILON)
    return centered * inverse, inverse


def norm_back_rows(upstream, normed, inverse, gain):
    scaled = upstream * gain
    return inverse * (
        scaled
        - jnp.mean(scaled, 0, keepdims=True)
        - normed * jnp.mean(scaled * normed, 0, keepdims=True)
    )


def fold(values):
    total = values[:, :LANES]
    for at in range(LANES, values.shape[1], LANES):
        total = total + values[:, at : at + LANES]
    return total


def split_low(values):
    high = values.astype(bf16)
    return high, (values - high.astype(f32)).astype(bf16)


def lane_index(shape):
    return lax.broadcasted_iota(jnp.int32, shape, len(shape) - 1)


def row_index(shape):
    return lax.broadcasted_iota(jnp.int32, shape, len(shape) - 2)


class Sizes:
    def __init__(self, mesh_sizes, inputs, feature_draws, hidden_weight):
        self.homes, self.rest = mesh_sizes["home"], mesh_sizes["rest"]
        _, self.genes, self.width = inputs.shape
        self.heads, self.feats, self.head = feature_draws.shape
        self.inner = self.heads * self.head
        self.hidden = hidden_weight.shape[1]
        self.rows = -(-self.feats // 16) * 16
        self.ext = self.head + 16
        self.scale = self.head ** (-0.25)


FIRST_MB, FINAL_MB, LAST_MB = 15, 14, 12
VMEM = pl.BlockSpec(memory_space=pltpu.VMEM)
SMEM = pl.BlockSpec(memory_space=pltpu.SMEM)


def call(name, body, args, out, scratch=(), megabytes=4, smem=0, aliases={}, flops=0):
    return pl.pallas_call(
        body,
        out_shape=out,
        in_specs=[SMEM] * smem + [VMEM] * (len(args) - smem),
        out_specs=jax.tree.map(lambda _: VMEM, out),
        scratch_shapes=list(scratch),
        input_output_aliases=aliases,
        compiler_params=pltpu.CompilerParams(vmem_limit_bytes=megabytes * 1024 * 1024),
        cost_estimate=pl.CostEstimate(flops=int(flops), bytes_accessed=1024, transcendentals=0),
        name=name,
    )(*args)


def array(*shape, dtype=f32):
    return jax.ShapeDtypeStruct(shape, dtype)


def prepare_body(s, place, joint, draws, out_t, hid, ret_t, hidden_bias, *refs):
    rows, table = refs[:6], refs[6]
    joint_t, draws_low, draws_t, out_wt, out_w, hid_w, hid_wt, ret_wt, ret_w, joint_w, cols, bias = refs[7:]
    joint_w[...] = joint[...].astype(bf16)
    joint_t[...] = joint[...].T.astype(bf16)
    for h in range(s.heads):
        draw = draws[h]
        filler = jnp.broadcast_to(draw[:, :1], (s.head, s.rows - s.feats))
        draws_low[h] = jnp.concatenate([draw, filler], 1).T.astype(bf16)
        draws_t[h] = jnp.concatenate([draw, jnp.zeros_like(filler)], 1).astype(bf16)
    out_wt[...] = out_t[...].astype(bf16)
    out_w[...] = out_t[...].T.astype(bf16)
    hid_w[...] = hid[...].astype(bf16)
    hid_wt[...] = hid[...].T.astype(bf16)
    ret_wt[...] = ret_t[...].astype(bf16)
    ret_w[...] = ret_t[...].T.astype(bf16)
    stacked = [r[...] for r in rows] + [table[pl.ds(place[s.homes + 1], 1), :]]
    stacked += [jnp.zeros((1, s.width), f32)]
    cols[...] = jnp.concatenate(stacked, 0).T
    bias[...] = jnp.broadcast_to(hidden_bias[...], (8, s.hidden)).T


def prepare(s, place, joint, draws, out_t, hid, ret_t, hidden_bias, rows, table):
    w, i, f = s.width, s.inner, s.hidden
    out = [
        array(3 * i, w, dtype=bf16),
        array(s.heads, s.rows, s.head, dtype=bf16),
        array(s.heads, s.head, s.rows, dtype=bf16),
        array(w, i, dtype=bf16),
        array(i, w, dtype=bf16),
        array(w, f, dtype=bf16),
        array(f, w, dtype=bf16),
        array(w, f, dtype=bf16),
        array(f, w, dtype=bf16),
        array(w, 3 * i, dtype=bf16),
        array(w, 8),
        array(f, 8),
    ]
    args = [place, joint, draws, out_t, hid, ret_t, hidden_bias[None], *[r[None] for r in rows], table]
    return call("prepare", functools.partial(prepare_body, s), args, out, smem=1, megabytes=8, flops=4e9)


def keys_body(s, base, count, fresh, *refs):
    refs = list(refs)
    place = refs.pop(0)
    xs = [refs.pop(0) for _ in range(count)]
    cols, joint_t, draws = (refs.pop(0) for _ in range(3))
    if not fresh:
        kv_prev = refs.pop(0)
        refs.pop(0), refs.pop(0)
    kv, shifted, qkv, ext, dashes, tops, cuts = refs
    scale = s.scale
    last_row = s.rows - 1
    tail = (s.heads, LANES - s.head, s.genes)
    ext[:, s.head :, :] = jnp.where(row_index(tail) == 0, 1.0, 0.0).astype(bf16)
    if fresh:
        state = jnp.full((16, 1), LOWEST, f32)
    else:
        state = jnp.concatenate([kv_prev[h, last_row:, 0:1] for h in range(s.heads)] + [jnp.full((16 - s.heads, 1), LOWEST, f32)], 0)
    for n in range(count):
        x = xs[n][...] + cols[:, 6:7]
        shifted[base + n] = x
        normed, _ = norm_rows(x)
        first = (normed * cols[:, 0:1] + cols[:, 1:2]).astype(bf16)
        for part in (1, 2, 0):
            rows = slice(part * s.inner, (part + 1) * s.inner)
            made = dot(joint_t[rows, :], first).astype(bf16)
            qkv[base + n, rows, :] = made
            if part == 2:
                for h in range(s.heads):
                    ext[h, : s.head, :] = made[h * s.head : (h + 1) * s.head]
        for h in range(s.heads):
            key = qkv[base + n, s.inner + h * s.head : s.inner + (h + 1) * s.head, :]
            dash = dot(draws[h], key)
            dashes[h] = dash
            key_f = key.astype(f32)
            cuts[h : h + 1, :] = jnp.sum(key_f * key_f, 0, keepdims=True) * (scale * scale * 0.5)
            tops[h : h + 1, :] = jnp.max(dash, 0, keepdims=True) * scale
        valid = place[base + n] + lane_index((1, s.genes)) < place[s.homes]
        new = jnp.maximum(state, jnp.max(jnp.where(valid, tops[...], LOWEST), 1, keepdims=True))
        decay = jnp.exp(state - new)
        state = new
        lifts = jnp.where(valid, cuts[...] + new, 1e30)
        for h in range(s.heads):
            feats = jnp.exp(scale * dashes[h] - lifts[h : h + 1]).astype(bf16)
            part = dot_lanes(feats, ext[h])
            if n == 0 and fresh:
                kv[h] = part
            else:
                kv[h] = (kv_prev if n == 0 else kv)[h] * decay[h : h + 1] + part
    for h in range(s.heads):
        kv[h, last_row:, :] = jnp.broadcast_to(state[h : h + 1], (1, LANES))


def run_keys(s, base, count, place, xs, cols, joint_t, draws, before=None):
    out = [
        array(s.heads, s.rows, LANES),
        array(s.homes, s.width, s.genes),
        array(s.homes, 3 * s.inner, s.genes, dtype=bf16),
    ]
    args = [place, *xs, cols, joint_t, draws]
    aliases = {}
    if before is not None:
        aliases = {len(args) + 1: 1, len(args) + 2: 2}
        args += list(before)
    scratch = [
        pltpu.VMEM((s.heads, LANES, s.genes), bf16),
        pltpu.VMEM((s.heads, s.rows, s.genes), f32),
        pltpu.VMEM((16, s.genes), f32),
        pltpu.VMEM((16, s.genes), f32),
    ]
    body = functools.partial(keys_body, s, base, count, before is None)
    return call("keys", body, args, out, scratch, 10, 1, aliases, 3e9 * count)


def merged(own, other, kept_rows, kept_lanes):
    last = own.shape[0] - 1
    own_peak, other_peak = own[last:, 0:1], other[last:, 0:1]
    peak = jnp.maximum(own_peak, other_peak)
    total = own * jnp.exp(own_peak - peak) + other * jnp.exp(other_peak - peak)
    inside = (row_index(own.shape) < kept_rows) & (lane_index(own.shape) < kept_lanes)
    return jnp.where(inside, total, 0.0), peak


def eye_like(size):
    return (row_index((size, size)) == lane_index((size, size))).astype(f32).astype(bf16)


def middle_body(s, base, count, later, first, final, *refs):
    refs = list(refs)

    def take(n):
        taken = refs[:n]
        del refs[:n]
        return taken

    (place,) = take(1)
    before = take(2) if first else take(17)
    shifted, qkv = take(2)
    cots = take(count)
    cols, hidden_bias, draws, draws_t, out_w, out_wt = take(6)
    hid_w, hid_wt, ret_w, ret_wt, joint = take(5)
    outputs = take(1 if final else 2) if first else None
    middle_grad, query_part = take(2)
    results = take(3) if final else take(17)
    if first:
        kv3, kv_t = take(2) if final else results[:2]
    else:
        kv3, kv_t = before[:2]
    mine = take(8) if first else None
    ahead = before[9:] if not first else results[9:]
    att_grad, query_grad = take(2)
    cot_all, pre_grads = take(2)
    sums = refs if final else results[2:9]
    acc_q, acc_o, acc_r, acc_h, acc_cols, acc_hb, values_grad = sums
    scale = s.scale
    ext = s.ext
    if first:
        kv_own, kv_other = before
        eye = eye_like(2 * ext)
        for h in range(s.heads):
            total, _ = merged(kv_own[h], kv_other[h], s.feats, s.head + 1)
            high, low = split_low(total[:, :ext])
            kv3[h] = jnp.concatenate([high, low, high], 1)
            kv_t[h] = dot_lanes(eye, jnp.concatenate([high, low], 1)).astype(bf16)
        for acc in sums:
            acc[...] = jnp.zeros_like(acc)
    else:
        for acc, was in zip(sums, before[2:]):
            acc[...] = was[...]
    for n in range(count):
        cot_all[n] = cots[n][...]

    def attend(index, feats, att, att_low, over):
        for h in range(s.heads):
            rows = slice(h * s.head, (h + 1) * s.head)
            query = qkv[index, rows, :]
            query_f = query.astype(f32)
            cut = jnp.sum(query_f * query_f, 0, keepdims=True) * (scale * scale * 0.5)
            value = jnp.exp(scale * dot(draws[h], query) - cut)
            feats[h] = value
            both = dot(kv_t[h], value.astype(bf16))
            total = both[:ext] + both[ext:]
            inverse = 1.0 / total[s.head : s.head + 1]
            over[h : h + 1, :] = inverse
            result = total[: s.head] * inverse
            att[rows, :] = result
            att_low[rows, :] = result.astype(bf16)

    gain = cols[:, 3:4]

    def forward(index, result, att_low, acts, slopes, normal, inverses):
        middle = shifted[index] + dot(out_wt[...], att_low[...]) + cols[:, 2:3]
        normed, inverse = norm_rows(middle)
        normal[...] = normed
        inverses[0:1, :] = inverse
        second = (normed * gain + cols[:, 4:5]).astype(bf16)
        step = s.hidden // 2
        for at in range(0, s.hidden, step):
            part = slice(at, at + step)
            pre = dot(hid_wt[part, :], second) + hidden_bias[part, 0:1]
            cumulative = 0.5 * (1.0 + lax.erf(pre * 0.7071067811865476))
            acts[part, :] = (pre * cumulative).astype(bf16)
            slopes[part, :] = cumulative + pre * (jnp.exp(-0.5 * pre * pre) * 0.3989422804014327)
        result[...] = middle + cols[:, 5:6] + dot(ret_wt[...], acts[...])

    def block(j, carry):
        feats, att, att_low, over, acts, slopes, normal, inverses = mine if first else [ref.at[j] for ref in ahead]
        if first:
            attend(base + j, feats, att, att_low, over)
            forward(base + j, outputs[0].at[j], att_low, acts, slopes, normal, inverses)
        x = shifted[base + j]
        normed, inverse = normal[...], inverses[0:1, :]
        second = (normed * gain + cols[:, 4:5]).astype(bf16)
        cot = cot_all[j]
        cot_low = cot.astype(bf16)
        step = s.hidden // 2
        for at in range(0, s.hidden, step):
            part = slice(at, at + step)
            pre_low = (dot(ret_w[part, :], cot_low) * slopes[part, :]).astype(bf16)
            pre_grads[part, :] = pre_low
            acc_hb[part, :] += fold(pre_low.astype(f32))
        acc_r[...] += dot_lanes(cot_low, acts[...])
        acc_h[...] += dot_lanes(second, pre_grads[...])
        second_grad = dot(hid_w[...], pre_grads[...])
        grad = cot + norm_back_rows(second_grad, normed, inverse, gain)
        middle_grad[j] = grad
        branch = grad.astype(bf16)
        acc_cols[0] += fold(branch.astype(f32))
        acc_cols[1] += fold(second_grad * normed)
        acc_cols[2] += fold(second_grad)
        acc_cols[3] += fold(cot)
        acc_o[...] += dot_lanes(branch, att_low[...])
        att_grad[...] = dot(out_w[...], branch)

        def back(h):
            rows = slice(h * s.head, (h + 1) * s.head)
            upstream = att_grad[rows, :]
            inverse = over[h : h + 1, :]
            numer = upstream * inverse
            denom = -jnp.sum(upstream * att[rows, :], 0, keepdims=True) * inverse
            tail_shape = (ext - s.head, s.genes)
            tail = jnp.where(row_index(tail_shape) == 0, denom, 0.0)
            high, low = split_low(jnp.concatenate([numer, tail], 0))
            value = feats[h]
            gap = jnp.zeros((LANES - ext, s.genes), bf16)
            values_grad[h] += dot_lanes(value.astype(bf16), jnp.concatenate([high, gap], 0))
            back_feats = dot(kv3[h], jnp.concatenate([high, high, low], 0)) * value
            query = qkv[base + j, rows, :].astype(f32)
            total = jnp.sum(back_feats, 0, keepdims=True)
            result = scale * dot(draws_t[h], back_feats.astype(bf16)) - query * (total * (scale * scale))
            query_grad[rows, :] = result.astype(bf16)

        for h in range(s.heads):
            back(h)
        first_low = (norm_rows(x)[0] * cols[:, 0:1] + cols[:, 1:2]).astype(bf16)
        acc_q[...] += dot_lanes(first_low, query_grad[...])
        query_part[j] = dot(joint[:, : s.inner], query_grad[...])
        return carry

    lax.fori_loop(0, count, block, 0)
    if not final:

        def attend_ahead(n, carry):
            views = [ref.at[n] for ref in ahead]
            attend(base + count + n, *views[:4])
            forward(base + count + n, outputs[1].at[n], views[2], *views[4:])
            return carry

        lax.fori_loop(0, later, attend_ahead, 0)
        if not first:
            results[0][...], results[1][...] = kv3[...], kv_t[...]
        return
    results[0][...] = values_grad[...]
    keep, send = results[1:]
    spare = s.hidden % LANES
    lane = lane_index((s.width, LANES))
    last = jnp.zeros((s.width, LANES), f32)
    spot = 2 * spare
    for n in range(4):
        last = jnp.where(lane == spot, jnp.sum(acc_cols[n], 1, keepdims=True), last)
        spot += 1
    for n in range(s.hidden // s.width):
        piece = acc_hb[n * s.width : (n + 1) * s.width, :]
        last = jnp.where(lane == spot, jnp.sum(piece, 1, keepdims=True), last)
        spot += 1
    if spare:
        tops = [acc[:, s.hidden - spare :] for acc in (acc_r, acc_h)]
        last = jnp.concatenate(tops + [last[:, 2 * spare :]], 1)
    tiles = []
    for acc in (acc_q, acc_o, acc_r, acc_h):
        tiles += [(acc, n * LANES) for n in range(acc.shape[1] // LANES)]
    deal_tiles(place[s.homes + 2], s.width, keep, send, tiles, last)


def deal_tiles(side, width, keep, send, tiles, last):
    half = keep.shape[0]

    def put(row, value):
        for part in (0, 1):
            begin, end = max(row, part * half), min(row + value.shape[0], (part + 1) * half)
            if begin < end:
                piece = value[begin - row : end - row]
                spots = slice(begin - part * half, end - part * half)
                if send is None:
                    keep[spots, :] = piece
                    continue

                @pl.when(side == part)
                def _():
                    keep[spots, :] = piece

                @pl.when(side != part)
                def _():
                    send[spots, :] = piece

    row = 0
    for acc, at in tiles:
        put(row, acc[:, at : at + LANES])
        row += width
    put(row, last)
    row += width
    total = half if send is None else 2 * half
    if row < total:
        put(row, jnp.zeros((total - row, LANES), f32))


def padded(rows, parts):
    return -(-rows // (8 * parts)) * 8 * parts


def halves(s, tiles, parts):
    rows = padded(tiles * s.width, parts)
    return [array(rows // 2, LANES), array(rows // 2, LANES)]


def run_middle(s, parts, place, groups, kv_own, kv_other, shifted, qkv, cots, weights):
    sums = [
        array(s.width, s.inner),
        array(s.width, s.inner),
        array(s.width, s.hidden),
        array(s.width, s.hidden),
        array(4, s.width, LANES),
        array(s.hidden, LANES),
        array(s.heads, s.rows, LANES),
    ]
    forms = [
        array(s.heads, s.rows, 3 * s.ext, dtype=bf16),
        array(s.heads, 2 * s.ext, s.rows, dtype=bf16),
    ]
    attention = [
        array(s.heads, s.rows, s.genes),
        array(s.inner, s.genes),
        array(s.inner, s.genes, dtype=bf16),
        array(16, s.genes),
        array(s.hidden, s.genes, dtype=bf16),
        array(s.hidden, s.genes),
        array(s.width, s.genes),
        array(8, s.genes),
    ]
    ends = [array(s.heads, s.rows, LANES)]
    ends += halves(s, 2 * (s.inner // LANES) + 2 * (s.hidden // LANES) + 1, parts)
    before, base = [kv_own, kv_other], 0
    outputs, middle_grad, query_part = [], [], []
    for index, count in enumerate(groups):
        first, final = index == 0, index == len(groups) - 1
        tokens = array(count, s.width, s.genes)
        later = sum(groups[index + 1 :])
        out = [tokens, tokens]
        if first:
            out = [array(n, s.width, s.genes) for n in groups] + out
        ahead = [array(later, *a.shape, dtype=a.dtype) for a in attention]
        out += ends if final else forms + sums + ahead
        scratch = list(forms) if first and final else []
        scratch += attention if first else []
        scratch += [
            array(s.inner, s.genes),
            array(s.inner, s.genes, dtype=bf16),
            tokens,
            array(s.hidden, s.genes, dtype=bf16),
        ]
        scratch += sums if final else []
        scratch = [pltpu.VMEM(a.shape, a.dtype) for a in scratch]
        args = [place, *before, shifted, qkv, *cots[base : base + count], *weights]
        body = functools.partial(middle_body, s, base, count, later, first, final)
        made = call("middle", body, args, out, scratch, FINAL_MB if final else FIRST_MB, 1, flops=7e9 * count)
        if first:
            outputs, made = made[: len(groups)], made[len(groups) :]
        middle_grad.append(made[0])
        query_part.append(made[1])
        before, base = made[2:], base + count
    return outputs, middle_grad, query_part, before


def last_body(s, groups, *refs):
    refs = list(refs)
    place, vg_own, vg_other, kv_own, kv_other, shifted, qkv = (refs.pop(0) for _ in range(7))
    middle_grads = [refs.pop(0) for _ in groups]
    query_parts = [refs.pop(0) for _ in groups]
    cols, draws, draws_t, joint = (refs.pop(0) for _ in range(4))
    input_grad = [refs.pop(0) for _ in range(s.homes)]
    keep, send, vg2, vg_t, ext2, grads, result_all, acc, acc_cols = refs
    scale = s.scale
    ext = s.ext
    eye = eye_like(ext)
    peaks = []
    for h in range(s.heads):
        total = vg_own[h] + vg_other[h]
        inside = row_index(total.shape) < s.feats
        high, low = split_low(jnp.where(inside, total, 0.0)[:, :ext])
        vg2[h] = jnp.concatenate([high, low], 1)
        vg_t[h] = dot_lanes(eye, high)[: s.head].astype(bf16)
        peaks.append(jnp.maximum(kv_own[h, s.rows - 1 :, 0:1], kv_other[h, s.rows - 1 :, 0:1]))
    tail = (s.heads, ext - s.head, s.genes)
    ones = jnp.where(row_index(tail) == 0, 1.0, 0.0).astype(bf16)
    ext2[:, s.head : ext, :] = ones
    ext2[:, ext + s.head :, :] = ones
    acc[...] = jnp.zeros_like(acc)
    acc_cols[...] = jnp.zeros_like(acc_cols)

    def block(base, middle_grad, query_part, i, carry):
        j = base + i
        valid = place[j] + lane_index((1, s.genes)) < place[s.homes]

        def head(h):
            rows = slice(h * s.head, (h + 1) * s.head)
            key = qkv[j, s.inner + h * s.head : s.inner + (h + 1) * s.head, :]
            value = qkv[j, 2 * s.inner + h * s.head : 2 * s.inner + (h + 1) * s.head, :]
            ext2[h, : s.head, :] = value
            ext2[h, ext : ext + s.head, :] = value
            key_f = key.astype(f32)
            cut = jnp.sum(key_f * key_f, 0, keepdims=True) * (scale * scale * 0.5)
            cut = jnp.where(valid, cut + peaks[h], 1e30)
            feats = jnp.exp(scale * dot(draws[h], key) - cut)
            back_feats = dot(vg2[h], ext2[h]) * feats
            total = jnp.sum(back_feats, 0, keepdims=True)
            result = scale * dot(draws_t[h], back_feats.astype(bf16)) - key_f * (total * (scale * scale))
            grads[rows, :] = result.astype(bf16)
            result = dot(vg_t[h], feats.astype(bf16))
            grads[s.inner + h * s.head : s.inner + (h + 1) * s.head, :] = result.astype(bf16)

        for h in range(s.heads):
            head(h)
        normed, inverse = norm_rows(shifted[j])
        gain = cols[:, 0:1]
        first = (normed * gain + cols[:, 1:2]).astype(bf16)
        acc[...] += dot_lanes(first, grads[...])
        first_grad = query_part[i] + dot(joint[:, s.inner :], grads[...])
        result = middle_grad[i] + norm_back_rows(first_grad, normed, inverse, gain)
        result_all[j] = result
        acc_cols[0] += fold(first_grad * normed)
        acc_cols[1] += fold(first_grad)
        acc_cols[2] += fold(result)
        return carry

    base = 0
    for n, count in enumerate(groups):
        lax.fori_loop(0, count, functools.partial(block, base, middle_grads[n], query_parts[n]), 0)
        base += count
    for n in range(s.homes):
        input_grad[n][...] = result_all[n]
    lane = lane_index((s.width, LANES))
    sums = [jnp.sum(acc_cols[n], 1, keepdims=True) for n in range(3)]
    last = jnp.where(lane == 0, sums[0], jnp.where(lane == 1, sums[1], 0.0))
    last = jnp.where(lane == 2 + place[s.homes + 1], sums[2], last)
    tiles = [(acc, n * LANES) for n in range(acc.shape[1] // LANES)]
    deal_tiles(place[s.homes + 2], s.width, keep, send, tiles, last)


def run_last(s, parts, groups, place, vg_own, vg_other, kv_own, kv_other, shifted, qkv, middle_grad, query_part, weights):
    out = [array(s.width, s.genes)] * s.homes + halves(s, 2 * (s.inner // LANES) + 1, parts)
    scratch = [
        pltpu.VMEM((s.heads, s.rows, 2 * s.ext), bf16),
        pltpu.VMEM((s.heads, s.head, s.rows), bf16),
        pltpu.VMEM((s.heads, 2 * s.ext, s.genes), bf16),
        pltpu.VMEM((2 * s.inner, s.genes), bf16),
        pltpu.VMEM((s.homes, s.width, s.genes), f32),
        pltpu.VMEM((s.width, 2 * s.inner), f32),
        pltpu.VMEM((3, s.width, LANES), f32),
    ]
    args = [place, vg_own, vg_other, kv_own, kv_other, shifted, qkv, *middle_grad, *query_part, *weights]
    return call("last", functools.partial(last_body, s, groups), args, out, scratch, LAST_MB, 1, flops=1e9)


def partners(size, step):
    return [(i, i ^ step) for i in range(size)]


def send(values, axis, size):
    return [lax.ppermute(values[k], axis, partners(size, k)) for k in range(1, size)]


def add_split(place, spot, terms, parts):
    rows = terms[0].shape[0] // parts

    def body(numbers, *refs):
        ins, outs = refs[: len(terms)], refs[len(terms) :]
        for k in range(parts):
            at = pl.multiple_of((numbers[spot] ^ k) * rows, 8) if parts > 1 else 0
            total = ins[0][pl.ds(at, rows), :]
            for other in ins[1:]:
                total = total + other[pl.ds(at, rows), :]
            outs[k][...] = total

    out = [array(rows, LANES)] * parts
    return call("add_split", body, [place, *terms], out, smem=1, flops=1e9)


def meet(place, spot, early, late, parts):
    first, second = early[0].shape[0] // parts, late[0].shape[0] // parts

    def body(numbers, *refs):
        outs = refs[len(early) + len(late) :]
        for terms, rows, begin in ((refs[: len(early)], first, 0), (refs[len(early) : -parts], second, first)):
            for k in range(parts):
                at = pl.multiple_of((numbers[spot] ^ k) * rows, 8)
                total = terms[0][pl.ds(at, rows), :]
                for other in terms[1:]:
                    total = total + other[pl.ds(at, rows), :]
                outs[k][begin : begin + rows, :] = total

    out = [array(first + second, LANES)] * parts
    return call("meet", body, [place, *early, *late], out, smem=1, flops=1e9)


def stack_rows(pieces):
    def body(*refs):
        at = 0
        for ref in refs[:-1]:
            refs[-1][at : at + ref.shape[0], :] = ref[...]
            at += ref.shape[0]

    return call("stack", body, pieces, array(sum(p.shape[0] for p in pieces), LANES), flops=1e9)


def forward_pair(near, far):
    def body(near_ref, far_ref, out):
        out[0] = near_ref[1]
        out[1] = far_ref[1]

    return call("forward_pair", body, [near, far], array(*near.shape), flops=1e9)


def place_blocks(s, place, near, far, last):
    def body(numbers, near_ref, far_ref, last_ref, out):
        home = numbers[s.homes + 4]
        out[home] = near_ref[0]
        out[home ^ 1] = last_ref[0]
        out[home ^ 2] = far_ref[0]
        out[home ^ 3] = last_ref[1]

    out = array(s.homes, s.width, s.genes)
    made = call("place_blocks", body, [place, near, far, last], out, smem=1, flops=1e9)
    return made.transpose(0, 2, 1)


def place_apart(s, place, blocks):
    def body(numbers, *refs):
        for k in range(s.homes):
            refs[-1][numbers[s.homes + 4] ^ k] = refs[k][...]

    out = array(s.homes, s.width, s.genes)
    made = call("place_apart", body, [place, *blocks], out, smem=1, flops=1e9)
    return made.transpose(0, 2, 1)


def finish_body(s, split, tissues, rows, place, own, other, *refs):
    early, late = refs[-2:]
    joint, out_t, hid, ret_t, ob, sg, sb, rb, hb, tissue, fg, fb = refs[:-2]
    first, second = rows
    if split:
        side, cell, home = (place[s.homes + n] for n in (2, 3, 4))
        for core in range(2):
            source = (own, other)[core]
            for at in range(16):
                spot = ((side ^ core) * 4 + (cell ^ (at // 4))) * 4 + (home ^ (at % 4))
                begin = at * (first + second)
                early[pl.ds(pl.multiple_of(spot * first, 8), first), :] = source[begin : begin + first, :]
                late[pl.ds(pl.multiple_of(spot * second, 8), second), :] = source[begin + first : begin + first + second, :]
    else:
        early[...] = own[...]
        late[...] = other[...]
    ni, nh, spare = s.inner // LANES, s.hidden // LANES, s.hidden % LANES
    w = s.width

    def tile(ref, n):
        return ref[n * w : (n + 1) * w, :]

    for n in range(ni):
        joint[:, n * LANES : (n + 1) * LANES] = tile(early, n)
        out_t[:, n * LANES : (n + 1) * LANES] = tile(early, ni + n)
    for n in range(2 * ni):
        joint[:, (ni + n) * LANES : (ni + n + 1) * LANES] = tile(late, n)
    for n in range(nh):
        ret_t[:, n * LANES : (n + 1) * LANES] = tile(early, 2 * ni + n)
        hid[:, n * LANES : (n + 1) * LANES] = tile(early, 2 * ni + nh + n)
    mixed = tile(early, 2 * ni + 2 * nh)
    if spare:
        ret_t[:, nh * LANES :] = mixed[:, :spare]
        hid[:, nh * LANES :] = mixed[:, spare : 2 * spare]
    columns = mixed.T
    at = 2 * spare
    for ref in (ob, sg, sb, rb):
        ref[...] = columns[at : at + 1, :]
        at += 1
    hb[...] = jnp.concatenate([columns[at + n, :] for n in range(s.hidden // w)], 0)
    columns = tile(late, 2 * ni).T
    fg[...] = columns[0:1, :]
    fb[...] = columns[1:2, :]
    tissue[...] = columns[2 : 2 + tissues, :]


def finish(s, split, tissues, rows, place, own, other):
    w = s.width
    row = array(1, w)
    out = [array(w, 3 * s.inner), array(w, s.inner), array(w, s.hidden), array(w, s.hidden)]
    out += [row, row, row, row, array(s.hidden), array(tissues, w), row, row]
    scratch = [pltpu.VMEM((32 * n if split else ref.shape[0], LANES), f32) for n, ref in zip(rows, (own, other))]
    body = functools.partial(finish_body, s, split, tissues, rows)
    return call("finish", body, [place, own, other], out, scratch, 8, 1, flops=1e9)


def solution(mesh):
    def run(inputs, lengths, *others):
        cells_axis, genes_axis = mesh.shape["cells"], mesh.shape["genes"]
        homes = inputs.shape[0] // cells_axis
        rest = genes_axis // homes
        sizes = {"cells": cells_axis, "home": homes, "rest": rest}
        fine = Mesh(mesh.devices.reshape(cells_axis, homes, rest), ("cells", "home", "rest"))
        tokens = P("cells", ("home", "rest"), None)
        return jax.shard_map(
            lambda *args: local(sizes, *args),
            mesh=fine,
            in_specs=(tokens, P("cells"), P("cells")) + (P(),) * 13 + (tokens,),
            out_specs=(tokens, tokens) + (P(),) * 12,
            check_vma=False,
        )(inputs, lengths, *others)

    return run


def after(value, *others):
    return lax.optimization_barrier((value, *others))[0]


def local(
    sizes,
    inputs,
    lengths,
    tissue_ids,
    tissue_table,
    first_gain,
    first_bias,
    joint_weight,
    feature_draws,
    output_weight,
    output_bias,
    second_gain,
    second_bias,
    hidden_weight,
    hidden_bias,
    return_weight,
    return_bias,
    cotangent,
):
    s = Sizes(sizes, inputs, feature_draws, hidden_weight)
    homes, rest, cells = s.homes, s.rest, sizes["cells"]
    parts = cells * homes * rest
    home = lax.axis_index("home").astype(jnp.int32)
    side = lax.axis_index("rest").astype(jnp.int32)
    half_side = side % 2
    cell = lax.axis_index("cells").astype(jnp.int32)
    paired = rest == 2

    def pick(array, k):
        return lax.dynamic_index_in_dim(array, home ^ k, 0, False)

    tissue = pick(tissue_ids, 0)
    starts = [(((home ^ k) * rest + side) * s.genes) for k in range(homes)]
    place = jnp.stack(starts + [pick(lengths, 0), tissue, half_side, cell, home]).astype(jnp.int32)
    inputs_t = inputs.transpose(0, 2, 1)
    cot_t = cotangent.transpose(0, 2, 1)
    mine = [pick(inputs_t, k) for k in range(homes)]
    arrived = send(mine, "home", homes)
    my_cots = [pick(cot_t, k).astype(f32) for k in range(homes)]
    rows = (first_gain, first_bias, output_bias, second_gain, second_bias, return_bias)
    joint_t, draws, draws_t, out_wt, out_w, hid_w, hid_wt, ret_wt, ret_w, joint, cols, bias = prepare(
        s,
        place,
        joint_weight,
        feature_draws.transpose(0, 2, 1),
        output_weight.T,
        hidden_weight,
        return_weight.T,
        hidden_bias,
        rows,
        tissue_table,
    )
    state = run_keys(s, 0, 1, place, mine[:1], cols, joint_t, draws)
    late_cots = [my_cots[0]] + [after(c, *arrived) for c in my_cots[1:]]
    arrived_cot = my_cots[:1] + send(late_cots, "home", homes)
    if homes > 1:
        state = run_keys(s, 1, homes - 1, place, arrived, cols, joint_t, draws, state)
    kv, shifted, qkv = state

    def other(value):
        return lax.ppermute(value, "rest", partners(2, 1))

    if paired:
        kv_other = other(after(kv, arrived_cot[1]))
    else:
        last_row = (jnp.arange(s.rows) == s.rows - 1)[None, :, None]
        if rest > 2:
            peak = kv[:, -1:, :]
            top = lax.pmax(peak, "rest")
            kv = lax.psum(kv * jnp.exp(peak - top), "rest")
            kv = jnp.where(last_row, top, kv)
        kv_other = jnp.where(last_row, LOWEST, jnp.zeros_like(kv))
    weights = (cols, bias, draws, draws_t, out_w, out_wt, hid_w, hid_wt, ret_w, ret_wt, joint)
    groups = (2, 2)
    out_blocks, middle_grad, query_part, made = run_middle(
        s, parts, place, groups, kv, kv_other, shifted, qkv, arrived_cot, weights
    )
    vg, early_keep, early_send = made
    vg_other = other(vg) if paired else jnp.zeros_like(vg)
    if rest > 2:
        vg = lax.psum(vg, "rest")
    made = run_last(
        s,
        parts,
        groups,
        place,
        vg,
        vg_other,
        kv,
        kv_other,
        shifted,
        qkv,
        middle_grad,
        query_part,
        (cols, draws, draws_t, joint),
    )
    grad_blocks, late_keep, late_send = made[:homes], made[homes], made[homes + 1]

    out_far = lax.ppermute(out_blocks[1], "home", partners(homes, 2))
    grad_received = send(grad_blocks, "home", homes)

    def finish_outputs(far):
        near = lax.ppermute(forward_pair(out_blocks[0], far), "home", partners(homes, 1))
        return place_blocks(s, place, out_blocks[0], far, near)

    split = paired and cells == 4 and homes == 4
    if split:

        def spread(pieces, axis, size):
            return [pieces[0]] + send(pieces, axis, size)

        def repeated(piece, axis, size):
            return [piece] + send([piece] * size, axis, size)

        outputs = finish_outputs(after(out_far, late_keep))
        early = spread(add_split(place, homes + 3, [early_keep, other(early_send)], cells), "cells", cells)
        late_send = after(late_send, out_far, *early[1:])
        late = spread(add_split(place, homes + 3, [late_keep, other(late_send)], cells), "cells", cells)
        rows = (early[0].shape[0] // homes, late[0].shape[0] // homes)
        both = spread(meet(place, homes + 4, early, late, homes), "home", homes)
        both[0] = after(both[0], outputs)
        both = repeated(add_split(place, homes + 4, both, 1)[0], "home", homes)
        both = repeated(stack_rows(both), "cells", cells)
        both[0] = after(both[0], grad_received[2])
        both = stack_rows(both)
        sums = (both, other(after(both, grad_received[0], grad_received[1])))
    else:
        axes = ("rest", "cells", "home")

        def summed(keep, sent):
            swap = half_side == 1
            whole_sum = jnp.where(swap, jnp.concatenate([sent, keep]), jnp.concatenate([keep, sent]))
            return lax.psum(whole_sum, axes)

        outputs = finish_outputs(out_far)
        sums, rows = (summed(early_keep, early_send), summed(late_keep, late_send)), (0, 0)
    joint_grad, out_t, hid, ret_t, ob, sg, sb, rb, hb, tissue_grad, fg, fb = finish(
        s, split, tissue_table.shape[0], rows, place, *sums
    )
    return (
        outputs,
        place_apart(s, place, [grad_blocks[0]] + grad_received),
        tissue_grad,
        fg[0],
        fb[0],
        joint_grad,
        out_t.T,
        ob[0],
        sg[0],
        sb[0],
        hid,
        hb,
        ret_t.T,
        rb[0],
    )
```
